32 devices in a mesh: dp: 8 (over y, x, core), tensor: 4 (over z).
Axes of the slice: x: 2, y: 2, z: 4, core: 2. Of those that a mesh axis runs over, the one named last changes fastest.
Arguments:
- tokens: bfloat16 [8192, 2048], P(('dp', 'tensor')), may hold values from -6 to 6
- lengths: int32 [8], P('dp'), may hold values from 256 to 1024, as said below
- cotangent: bfloat16 [8192, 2048], P(('dp', 'tensor')), may hold values from -6 to 6
- gain_one: float32 [2048], replicated, may hold values from 0.5 to 1.5
- gain_two: float32 [2048], replicated, may hold values from 0.5 to 1.5
- w_query: float32 [2048, 2048], P('dp', 'tensor'), may hold values from -0.125 to 0.125
- w_key: float32 [2048, 2048], P('dp', 'tensor'), may hold values from -0.125 to 0.125
- w_value: float32 [2048, 3456], P('dp', 'tensor'), may hold values from -0.125 to 0.125
- w_gate: float32 [2048, 3456], P('dp', 'tensor'), may hold values from -0.125 to 0.125
- w_out: float32 [2048, 3456], P('dp', 'tensor'), may hold values from -0.109375 to 0.109375
- w_mgate: float32 [2048, 3456], P('dp', 'tensor'), may hold values from -0.125 to 0.125
- w_mup: float32 [2048, 3456], P('dp', 'tensor'), may hold values from -0.125 to 0.125
- w_down: float32 [2048, 3456], P('dp', 'tensor'), may hold values from -0.109375 to 0.109375
Outputs:
- output: bfloat16 [8192, 2048], P(('dp', 'tensor'))
- grad_tokens: bfloat16 [8192, 2048], P(('dp', 'tensor'))
- grad_gain_one: float32 [2048], replicated
- grad_gain_two: float32 [2048], replicated
- grad_w_query: float32 [2048, 2048], P('dp', 'tensor')
- grad_w_key: float32 [2048, 2048], P('dp', 'tensor')
- grad_w_value: float32 [2048, 3456], P('dp', 'tensor')
- grad_w_gate: float32 [2048, 3456], P('dp', 'tensor')
- grad_w_out: float32 [2048, 3456], P('dp', 'tensor')
- grad_w_mgate: float32 [2048, 3456], P('dp', 'tensor')
- grad_w_mup: float32 [2048, 3456], P('dp', 'tensor')
- grad_w_down: float32 [2048, 3456], P('dp', 'tensor')
The draws below stay inside these ranges and needn't reach their ends.
Inputs may be any that keep to these rules, and one draw needn't show every extreme that they name: Valid slots of sequence s are 0 to lengths[s] - 1; some sequence has all 1024 slots valid and some other has 256.
All inputs are finite; a program needn't handle non-finite values.
Results may differ from the reference program's by a relative error of at most 0.019.
Values may be sent and summed in bfloat16 or wider, within the bound.
No kernel may reach another device: no remote copies, remote signals or barrier semaphores. Data moves between devices by JAX's collectives and lax.ppermute only.
A program may use at most 256 MiB of HBM per device.

```python
import jax
import jax.numpy as jnp
from jax import lax

D = 2048
HEADS = 8
KEY = 256
VAL = 432
FF = 3456
SLOTS = 1024
SEQS = 8
TOKENS = 8192
KD = 2048
VD = 3456


def draw_lengths(key, part):
    key = jax.random.fold_in(key, 5)
    keys = jax.random.split(key, 3)
    drawn = jax.random.randint(keys[0], (SEQS,), SLOTS // 4, SLOTS + 1)
    longest = jax.random.randint(keys[1], (), 0, SEQS)
    shortest = (longest + 1 + jax.random.randint(keys[2], (), 0, SEQS - 1)) % SEQS
    places = jnp.arange(SEQS)
    drawn = jnp.where(places == longest, SLOTS, drawn)
    drawn = jnp.where(places == shortest, SLOTS // 4, drawn)
    return drawn.astype(jnp.int32)


def steps_of(own_key, extent, cuts, low, largest):
    factor_of, own = 1.0, jax.random.fold_in(own_key, 6)
    for position, shards_of in cuts:
        heights = jnp.exp(jax.random.uniform(jax.random.fold_in(own, position), (shards_of,), jnp.float32, low / len(cuts), largest / len(cuts)))
        factor_of = factor_of * jnp.repeat(heights, extent[position] // shards_of).reshape([-1 if axis == position else 1 for axis in range(len(extent))])
    return factor_of


def bell_draw(own_key, extent, spread, bound, pieces=(), held_as=jnp.bfloat16):
    array = jax.random.normal(own_key, extent, jnp.float32) * spread
    if len(pieces) > 0:
        array = steps_of(own_key, extent, pieces, -0.22, 0.18) * array
    return jnp.clip(array, min=-bound, max=bound).astype(held_as)


def setup_inputs(seed: int = 0) -> dict:
    key_of = jax.random.split(jax.random.key(seed), 14)
    return {
        "tokens": bell_draw(key_of[0], (TOKENS, D), 1.0, 6.0, ((0, 32),)),
        "lengths": draw_lengths(jax.random.fold_in(key_of[13], 71), 0),
        "cotangent": bell_draw(key_of[2], (TOKENS, D), 1.0, 6.0, ((0, 32),)),
        "gain_one": jnp.clip(1.0 + 0.1 * jax.random.normal(key_of[3], (D,), jnp.float32), 0.5, 1.5),
        "gain_two": jnp.clip(1.0 + 0.1 * jax.random.normal(key_of[4], (D,), jnp.float32), 0.5, 1.5),
        "w_query": bell_draw(key_of[5], (D, KD), D ** -0.5, 0.125, ((0, 8), (1, 4)), jnp.float32),
        "w_key": bell_draw(key_of[6], (D, KD), D ** -0.5, 0.125, ((0, 8), (1, 4)), jnp.float32),
        "w_value": bell_draw(key_of[7], (D, VD), D ** -0.5, 0.125, ((0, 8), (1, 4)), jnp.float32),
        "w_gate": bell_draw(key_of[8], (D, VD), D ** -0.5, 0.125, ((0, 8), (1, 4)), jnp.float32),
        "w_out": bell_draw(key_of[9], (D, VD), VD ** -0.5, 0.109375, ((0, 8), (1, 4)), jnp.float32),
        "w_mgate": bell_draw(key_of[10], (D, FF), D ** -0.5, 0.125, ((0, 8), (1, 4)), jnp.float32),
        "w_mup": bell_draw(key_of[11], (D, FF), D ** -0.5, 0.125, ((0, 8), (1, 4)), jnp.float32),
        "w_down": bell_draw(key_of[12], (D, FF), FF ** -0.5, 0.109375, ((0, 8), (1, 4)), jnp.float32),
    }


@jax.custom_vjp
def low(v):
    return lax.optimization_barrier(v.astype(jnp.bfloat16)).astype(jnp.float32)

@jax.custom_vjp
def low_back(v):
    return v

def low_keep(v):
    return (low(v), None)

def low_pass(kept, grad):
    return (grad,)

def back_keep(v):
    return (v, None)

def back_low(kept, grad):
    return (low(grad),)
low.defvjp(low_keep, low_pass)
low_back.defvjp(back_keep, back_low)
EPS = 1e-05
HEAD_EPS = 1.0
HIGH = lax.Precision.HIGHEST

def multiply(left, right):
    return jnp.dot(left, right, precision=HIGH, preferred_element_type=jnp.float32)

def layer_norm(features, gain_vec):
    centred = features - lax.optimization_barrier(jnp.mean(features, -1, keepdims=True))
    variance = lax.optimization_barrier(jnp.mean(centred * centred, -1, keepdims=True))
    return centred * lax.rsqrt(variance + EPS) * gain_vec

def rotation_tables(seq_slots, width):
    half_width = width // 2
    freqs = 10000.0 ** (-jnp.arange(half_width, dtype=jnp.float32) / half_width)
    angles = jnp.arange(seq_slots, dtype=jnp.float32)[:, None] * freqs[None, :]
    angles = jnp.concatenate([angles, angles], -1)[:, None, :]
    return (jnp.cos(angles), jnp.sin(angles))

def rotate(features, cosines, sines):
    half_width = features.shape[-1] // 2
    turned = jnp.concatenate([-features[..., half_width:], features[..., :half_width]], -1)
    return features * cosines + turned * sines

def rotate_scaled(features, cosines, sines):
    return rotate(features, cosines, sines) * KEY ** (-0.5)

def decay_block(offset, block_rows, seq_slots, log_decay):
    query_pos = jnp.arange(block_rows, dtype=jnp.int32) + offset.astype(jnp.int32)
    key_pos = jnp.arange(seq_slots, dtype=jnp.int32)
    spacing = query_pos[:, None] - key_pos[None, :]
    behind = spacing >= 0
    factor = jnp.exp(log_decay[:, None, None] * jnp.where(behind, spacing, 0).astype(jnp.float32)[None])
    return jnp.where(behind[None], factor, 0.0)

def head_norm(retained):
    centred = retained - lax.optimization_barrier(jnp.mean(retained, -1, keepdims=True))
    variance = lax.optimization_barrier(jnp.mean(centred * centred, -1, keepdims=True))
    return centred * lax.rsqrt(variance + HEAD_EPS)

def gated_heads(gate_pre, retained):
    return jax.nn.silu(gate_pre) * head_norm(retained)

def gelu_gated(mgate_pre, mup_pre):
    return jax.nn.gelu(mgate_pre, approximate=False) * mup_pre

def sequence_forward(features, params, valid):
    gain_one, gain_two, w_query, w_key, w_value, w_gate, w_out, w_mgate, w_mup, w_down = params
    seq_slots = features.shape[0]
    block_rows = min(512, seq_slots)
    first_norm = low(layer_norm(features, gain_one))
    queries = low_back(multiply(first_norm, low(w_query))).reshape(seq_slots, HEADS, KEY)
    key_rows = low_back(multiply(first_norm, low(w_key))).reshape(seq_slots, HEADS, KEY)
    value_rows = low_back(low(multiply(first_norm, low(w_value)))).reshape(seq_slots, HEADS, VAL)
    gate_pre = low_back(multiply(first_norm, low(w_gate))).reshape(seq_slots, HEADS, VAL)
    cosines, sines = rotation_tables(seq_slots, KEY)
    query_turned = low(rotate(queries, cosines, sines))
    key_turned = low(rotate_scaled(key_rows, cosines, sines))
    log_decay = jnp.log(1.0 - jnp.exp2(-5.0 - jnp.arange(HEADS, dtype=jnp.float32)))

    def retain(offset):
        query_block = lax.dynamic_slice_in_dim(query_turned, offset, block_rows, 0)
        scores = low_back(jnp.einsum('qhk,shk->hqs', query_block, key_turned, precision=HIGH))
        weights = low(scores * decay_block(offset, block_rows, seq_slots, log_decay))
        return jnp.einsum('hqs,shv->qhv', weights, value_rows, precision=HIGH)
    offsets = jnp.arange(seq_slots // block_rows, dtype=jnp.int32) * block_rows
    retained = low_back(lax.map(jax.checkpoint(retain), offsets).reshape(seq_slots, HEADS, VAL))
    mixed = low(gated_heads(gate_pre, retained)).reshape(seq_slots, HEADS * VAL)
    middle = features + low_back(multiply(mixed, low(w_out).T))
    second_norm = low(layer_norm(middle, gain_two))
    mgate_pre = low_back(multiply(second_norm, low(w_mgate)))
    mup_pre = low_back(multiply(second_norm, low(w_mup)))
    hidden = low(gelu_gated(mgate_pre, mup_pre))
    final = middle + low_back(multiply(hidden, low(w_down).T))
    return jnp.where(valid[:, None], final, 0.0)

def reference(tokens, lengths, cotangent, gain_one, gain_two, w_query, w_key, w_value, w_gate, w_out, w_mgate, w_mup, w_down):
    params = (gain_one, gain_two, w_query, w_key, w_value, w_gate, w_out, w_mgate, w_mup, w_down)
    inputs = tokens.astype(jnp.float32).reshape(-1, SLOTS, D)
    cotangents = cotangent.astype(jnp.float32).reshape(-1, SLOTS, D)

    def one_sequence(totals, item):
        features, incoming, length = item
        valid = jnp.arange(SLOTS, dtype=jnp.int32) < length

        def forward(values_in, params_in):
            return sequence_forward(values_in, params_in, valid)
        result, pull = jax.vjp(forward, features, params)
        grad_features, grad_params = pull(incoming)
        totals = jax.tree.map(jnp.add, totals, grad_params)
        return (totals, (result.astype(jnp.bfloat16), grad_features.astype(jnp.bfloat16)))
    zeros = jax.tree.map(jnp.zeros_like, params)
    totals, (results, grad_inputs) = lax.scan(one_sequence, zeros, (inputs, cotangents, lengths))
    return (results.reshape(-1, D), grad_inputs.reshape(-1, D), totals[0], totals[1], totals[2], totals[3], totals[4], totals[5], totals[6], totals[7], totals[8], totals[9])
```

```python
from functools import partial

import jax
import jax.numpy as jnp
from jax import lax
from jax.experimental import pallas as pl
from jax.experimental.pallas import tpu as pltpu
from jax.sharding import PartitionSpec as P

KEY = 256
VAL = 432
VPAD = 512
EPS = 1e-05
HEAD_EPS = 1.0
F32 = jnp.float32
BF16 = jnp.bfloat16
VMEM_LIMIT = 48 * 1024 * 1024


def times_plain(left, right):
    return jnp.dot(left, right, preferred_element_type=F32)


def times_left(left, right):
    return lax.dot_general(left, right, (((0,), (0,)), ((), ())), preferred_element_type=F32)


def times_right(left, right):
    return lax.dot_general(left, right, (((1,), (1,)), ((), ())), preferred_element_type=F32)


def after(array, *earlier):
    return lax.optimization_barrier((array, *earlier))[0]


def norm_parts(features):
    centred = features - jnp.mean(features, -1, keepdims=True)
    inverse = lax.rsqrt(jnp.mean(centred * centred, -1, keepdims=True) + EPS)
    return centred * inverse, inverse


def norm_back(normed, inverse, grad, gain):
    scaled = grad * gain
    return inverse * (
        scaled
        - jnp.mean(scaled, -1, keepdims=True)
        - normed * jnp.mean(scaled * normed, -1, keepdims=True)
    )


def decay_rows(log_decay, rows, width):
    query = lax.broadcasted_iota(jnp.int32, (rows, width), 0) + (width - rows)
    key = lax.broadcasted_iota(jnp.int32, (rows, width), 1)
    spacing = query - key
    factor = jnp.exp(log_decay * jnp.maximum(spacing, 0).astype(F32))
    return jnp.where(spacing >= 0, factor, 0.0)


def retain_kernel(slots, rows, place_ref, decay_ref, *refs):
    ins, (cos_ref, sin_ref), outs = refs[: 4 * slots], refs[4 * slots : 4 * slots + 2], refs[4 * slots + 2 :]
    query_ref, key_ref, value_ref, normed_ref, scale_ref, mixed_ref, factor_ref, kept_ref = outs
    head = pl.program_id(0)
    place = place_ref[0]
    seq = slots * rows
    half = KEY // 2
    for slot in range(slots):
        start = pl.multiple_of((slot ^ place) * rows, rows)
        cosines, sines = cos_ref[pl.ds(start, rows), :], sin_ref[pl.ds(start, rows), :]
        for source, target, scale in ((ins[slot], query_ref, 1.0), (ins[slots + slot], key_ref, KEY**-0.5)):
            low = source[:, :half].astype(F32)
            high = source[:, half:].astype(F32)
            target[pl.ds(start, rows), :half] = ((low * cosines - high * sines) * scale).astype(BF16)
            target[pl.ds(start, rows), half:] = ((high * cosines + low * sines) * scale).astype(BF16)
        value_ref[pl.ds(start, rows), :] = ins[2 * slots + slot][...]
    factor_ref[...] = decay_rows(decay_ref[head], rows, seq)
    for block in range(slots):
        width = (block + 1) * rows
        scores = times_right(query_ref[block * rows : width, :], key_ref[:width, :])
        weights = (scores * factor_ref[:, seq - width :]).astype(BF16)
        kept_ref[block * rows : width, :] = times_plain(weights, value_ref[:width, :])
    inside = lax.broadcasted_iota(jnp.int32, (rows, VPAD), 1) < VAL
    for slot in range(slots):
        start = pl.multiple_of((slot ^ place) * rows, rows)
        kept = kept_ref[pl.ds(start, rows), :]
        mean = jnp.sum(kept, -1, keepdims=True) / VAL
        centred = jnp.where(inside, kept - mean, 0.0)
        inverse = lax.rsqrt(jnp.sum(centred * centred, -1, keepdims=True) / VAL + HEAD_EPS)
        normed = centred * inverse
        gate = ins[3 * slots + slot][...].astype(F32)
        mixed = gate * jax.nn.sigmoid(gate) * normed
        mixed_ref[slot * rows : (slot + 1) * rows, :] = mixed.astype(BF16)
        normed_ref[slot * rows : (slot + 1) * rows, :] = normed.astype(BF16)
        scale_ref[slot * rows : (slot + 1) * rows, :] = jnp.broadcast_to(inverse, (rows, 128))


def slot_specs(rows, heads):
    first_value = 2 * heads * KEY // VPAD
    return (
        pl.BlockSpec((rows, KEY), lambda h, *_: (0, h)),
        pl.BlockSpec((rows, KEY), lambda h, *_: (0, heads + h)),
        pl.BlockSpec((rows, VPAD), lambda h, *_: (0, first_value + h)),
        pl.BlockSpec((rows, VPAD), lambda h, *_: (0, first_value + heads + h)),
    )


def retain(projected, place, log_decay, cosines, sines, heads):
    slots, rows = len(projected), projected[0].shape[0]
    seq = slots * rows
    specs = slot_specs(rows, heads)
    table = pl.BlockSpec((seq, KEY // 2), lambda h, *_: (0, 0))

    def column(width):
        return pl.BlockSpec((seq, width), lambda h, *_: (0, h))

    return pl.pallas_call(
        partial(retain_kernel, slots, rows),
        out_shape=(
            jax.ShapeDtypeStruct((seq, heads * KEY), BF16),
            jax.ShapeDtypeStruct((seq, heads * KEY), BF16),
            jax.ShapeDtypeStruct((seq, heads * VPAD), BF16),
            jax.ShapeDtypeStruct((seq, heads * VPAD), BF16),
            jax.ShapeDtypeStruct((seq, heads * 128), F32),
            jax.ShapeDtypeStruct((seq, heads * VPAD), BF16),
        ),
        grid_spec=pltpu.PrefetchScalarGridSpec(
            num_scalar_prefetch=2,
            grid=(heads,),
            in_specs=[spec for spec in specs for _ in range(slots)] + [table, table],
            out_specs=[column(KEY), column(KEY), column(VPAD), column(VPAD), column(128), column(VPAD)],
            scratch_shapes=[pltpu.VMEM((rows, seq), F32), pltpu.VMEM((seq, VPAD), F32)],
        ),
        compiler_params=pltpu.CompilerParams(vmem_limit_bytes=VMEM_LIMIT),
        cost_estimate=pl.CostEstimate(
            flops=heads * seq * seq * (KEY + VPAD), bytes_accessed=heads * seq * 9000, transcendentals=heads * seq * 800
        ),
    )(place, log_decay, *(projected * 4), cosines, sines)


def retain_back_kernel(slots, rows, heads, place_ref, decay_ref, *refs):
    grads, gates, rest = refs[:slots], refs[slots : 2 * slots], refs[2 * slots :]
    (normed_ref, scale_ref, query_ref, key_ref, value_ref, cos_ref, sin_ref, out_ref, factor_ref, ret_ref, key_sum, value_sum) = rest
    head = pl.program_id(0)
    place = place_ref[0]
    seq = slots * rows
    half = KEY // 2
    query_col = pl.multiple_of(head * KEY, KEY)
    key_col = pl.multiple_of((heads + head) * KEY, KEY)
    value_col = pl.multiple_of(2 * heads * KEY + head * VPAD, VPAD)
    gate_col = pl.multiple_of(2 * heads * KEY + (heads + head) * VPAD, VPAD)
    inside = lax.broadcasted_iota(jnp.int32, (rows, VPAD), 1) < VAL
    for slot in range(slots):
        start = pl.multiple_of((slot ^ place) * rows, rows)
        span = slice(slot * rows, (slot + 1) * rows)
        grad, gate = grads[slot][...].astype(F32), gates[slot][...].astype(F32)
        normed, inverse = normed_ref[span, :].astype(F32), scale_ref[span, :1]
        sig = jax.nn.sigmoid(gate)
        out_ref[span, pl.ds(gate_col, VPAD)] = (grad * normed * sig * (1.0 + gate * (1.0 - sig))).astype(BF16)
        grad_normed = grad * gate * sig
        mean = jnp.sum(grad_normed, -1, keepdims=True) / VAL
        along = jnp.sum(grad_normed * normed, -1, keepdims=True) / VAL
        grad_ret = inverse * (grad_normed - mean - normed * along)
        ret_ref[pl.ds(start, rows), :] = jnp.where(inside, grad_ret, 0.0).astype(BF16)
    factor_ref[...] = decay_rows(decay_ref[head], rows, seq)
    key_sum[...] = jnp.zeros_like(key_sum)
    value_sum[...] = jnp.zeros_like(value_sum)
    for block in range(slots):
        width = (block + 1) * rows
        span = slice(block * rows, width)
        query, ret, keys = query_ref[span, :], ret_ref[span, :], key_ref[:width, :]
        factor = factor_ref[:, seq - width :]
        weights = (times_right(query, keys) * factor).astype(BF16)
        grad_scores = (times_right(ret, value_ref[:width, :]) * factor).astype(BF16)
        value_sum[:width, :] += times_left(weights, ret)
        key_sum[:width, :] += times_left(grad_scores, query)
        grad_query = times_plain(grad_scores, keys)
        row = pl.multiple_of((block ^ place) * rows, rows)
        cosines, sines = cos_ref[span, :], sin_ref[span, :]
        low, high = grad_query[:, :half], grad_query[:, half:]
        out_ref[pl.ds(row, rows), pl.ds(query_col, half)] = (low * cosines + high * sines).astype(BF16)
        out_ref[pl.ds(row, rows), pl.ds(pl.multiple_of(query_col + half, half), half)] = (
            high * cosines - low * sines
        ).astype(BF16)
    for block in range(slots):
        span = slice(block * rows, (block + 1) * rows)
        row = pl.multiple_of((block ^ place) * rows, rows)
        cosines, sines = cos_ref[span, :], sin_ref[span, :]
        low, high = key_sum[span, :half] * KEY**-0.5, key_sum[span, half:] * KEY**-0.5
        out_ref[pl.ds(row, rows), pl.ds(key_col, half)] = (low * cosines + high * sines).astype(BF16)
        out_ref[pl.ds(row, rows), pl.ds(pl.multiple_of(key_col + half, half), half)] = (
            high * cosines - low * sines
        ).astype(BF16)
        out_ref[pl.ds(row, rows), pl.ds(value_col, VPAD)] = value_sum[span, :].astype(BF16)


def retain_back(grads, projected, normed, scale, query, key, value, place, log_decay, cosines, sines, heads):
    slots, rows = len(projected), projected[0].shape[0]
    seq = slots * rows
    columns = 2 * heads * (KEY + VPAD)
    table = pl.BlockSpec((seq, KEY // 2), lambda h, *_: (0, 0))

    def column(width):
        return pl.BlockSpec((seq, width), lambda h, *_: (0, h))

    return pl.pallas_call(
        partial(retain_back_kernel, slots, rows, heads),
        out_shape=jax.ShapeDtypeStruct((seq, columns), BF16),
        grid_spec=pltpu.PrefetchScalarGridSpec(
            num_scalar_prefetch=2,
            grid=(heads,),
            in_specs=[pl.BlockSpec((rows, VPAD), lambda h, *_: (0, h))] * slots
            + [slot_specs(rows, heads)[3]] * slots
            + [column(VPAD), column(128), column(KEY), column(KEY), column(VPAD), table, table],
            out_specs=pl.BlockSpec((seq, columns), lambda h, *_: (0, 0)),
            scratch_shapes=[
                pltpu.VMEM((rows, seq), F32),
                pltpu.VMEM((seq, VPAD), BF16),
                pltpu.VMEM((seq, KEY), F32),
                pltpu.VMEM((seq, VPAD), F32),
            ],
        ),
        compiler_params=pltpu.CompilerParams(vmem_limit_bytes=VMEM_LIMIT),
        cost_estimate=pl.CostEstimate(
            flops=heads * seq * seq * (3 * KEY + 2 * VPAD), bytes_accessed=heads * seq * 10000, transcendentals=heads * seq * 800
        ),
    )(place, log_decay, *grads, *projected, normed, scale, query, key, value, cosines, sines)


def per_device(
    dp_size,
    tensor_size,
    tokens,
    lengths,
    cotangent,
    gain_one,
    gain_two,
    w_query,
    w_key,
    w_value,
    w_gate,
    w_out,
    w_mgate,
    w_mup,
    w_down,
):
    rows, width = tokens.shape
    seq = rows * tensor_size
    heads = w_query.shape[1] // KEY
    units = w_mgate.shape[1]
    shard_rows = w_query.shape[0]
    half_rows = shard_rows // 2
    bits = dp_size.bit_length() - 1
    mine, place = lax.axis_index("dp"), lax.axis_index("tensor")
    inner = (place == 1) | (place == 2)
    odd = (mine & 1) == 1
    up_bits = list(range(1, bits))
    down_bits = up_bits[::-1]

    def swap_dp(array, mask):
        return lax.ppermute(array, "dp", [(i, i ^ mask) for i in range(dp_size)])

    def move_tensor(array, pairs):
        return lax.ppermute(array, "tensor", pairs)

    def swap_tensor(array, mask):
        return move_tensor(array, [(i, i ^ mask) for i in range(tensor_size)])

    across = [(1, 2), (2, 1)]
    outward = [(1, 0), (2, 3)]
    inward = [(0, 1), (3, 2)]

    def line_gather(own):
        beside = swap_tensor(own, 1)
        middle = move_tensor(own, across)
        far_ends = move_tensor(middle, outward)
        far_inner = move_tensor(beside, across)
        last = move_tensor(far_inner, outward)
        return own, beside, jnp.where(inner, far_inner, far_ends), jnp.where(inner, middle, last)

    def line_scatter(part):
        third, second = part(3), part(2)
        from_ends = move_tensor(third.astype(BF16), inward)
        from_ends_two = move_tensor(second.astype(BF16), inward)
        second_sum = (second + from_ends.astype(F32)).astype(BF16)
        third_sum = (third + from_ends_two.astype(F32)).astype(BF16)
        first = part(1) + move_tensor(second_sum, across).astype(F32)
        beside = swap_tensor(first.astype(BF16), 1)
        middle = move_tensor(third_sum, across)
        return part(0) + middle.astype(F32) + beside.astype(F32)

    def gather_half(piece, order):
        pieces = [piece]
        for bit in order:
            pieces = pieces + [swap_dp(p, 1 << bit) for p in pieces]
        return pieces

    def scatter_half(low, high, order):
        for bit in order[::-1]:
            total = low + swap_dp(high.astype(BF16), 1 << bit).astype(F32)
            middle = total.shape[-2] // 2
            low, high = total[..., :middle, :], total[..., middle:, :]
        return total

    blocks = [
        (chip << 1 | core, part)
        for core in range(2)
        for part, order in ((0, up_bits), (1, down_bits))
        for chip in [sum((i >> j & 1) << (b - 1) for j, b in enumerate(order)) for i in range(dp_size // 2)]
    ]

    def to_relative(array):
        return jnp.concatenate(
            [
                lax.dynamic_slice_in_dim(array, (mine ^ mask) * shard_rows + part * half_rows, half_rows, -1)
                for mask, part in blocks
            ],
            -1,
        )

    def to_global(array):
        found = []
        for shard in range(dp_size):
            mask = mine ^ shard
            for part, order in ((0, up_bits), (1, down_bits)):
                chip = sum((mask >> b & 1) << j for j, b in enumerate(order))
                index = (mask & 1) * dp_size + part * (dp_size // 2) + chip
                found.append(lax.dynamic_slice_in_dim(array, index * half_rows, half_rows, -1))
        return jnp.concatenate(found, -1)

    def pad_heads(array):
        split = array.reshape(shard_rows, heads, VAL)
        return jnp.pad(split, ((0, 0), (0, 0), (0, VPAD - VAL))).reshape(shard_rows, heads * VPAD)

    def cut_heads(array):
        return array.reshape(shard_rows, heads, VPAD)[:, :, :VAL].reshape(shard_rows, heads * VAL)

    first_row = place * rows
    valid = (first_row + jnp.arange(rows, dtype=jnp.int32) < lengths[0])[:, None]
    head_ids = (place * heads + jnp.arange(heads, dtype=jnp.int32)).astype(F32)
    log_decay = jnp.log(1.0 - jnp.exp2(-5.0 - head_ids))
    place_arg = place.astype(jnp.int32).reshape(1)
    freqs = 10000.0 ** (-jnp.arange(KEY // 2, dtype=F32) / (KEY // 2))
    angles = jnp.arange(seq, dtype=F32)[:, None] * freqs[None, :]
    cosines, sines = jnp.cos(angles), jnp.sin(angles)

    gain_first, gain_second = to_relative(gain_one), to_relative(gain_two)
    features = to_relative(tokens).astype(F32)
    normed_one, inverse_one = norm_parts(features)
    first_slots = line_gather((normed_one * gain_first).astype(BF16))

    local_one = jnp.concatenate(
        [w_query.astype(BF16), w_key.astype(BF16), pad_heads(w_value.astype(BF16)), pad_heads(w_gate.astype(BF16))], -1
    )

    def gather_weight(local):
        own = gather_half(local[:half_rows], up_bits) + gather_half(local[half_rows:], down_bits)
        other = [swap_dp(p, 1) for p in own]
        return jnp.concatenate(own + other, 0)

    proj_low = gather_weight(local_one)
    out_low = gather_weight(pad_heads(w_out.astype(BF16)))

    local_two = jnp.concatenate([w_mgate.astype(BF16), w_mup.astype(BF16), w_down.astype(BF16)], -1)

    def pair(dp_index, tensor_index):
        return dp_index * tensor_size + tensor_index

    top = tensor_size - 1
    to_even = [(pair(m | 1, t), pair(m, t)) for m in range(0, dp_size, 2) for t in range(tensor_size)]
    to_odd = [(pair(m, t), pair(m | 1, t ^ top)) for m in range(0, dp_size, 2) for t in range(tensor_size)]
    odd_turn = [(pair(m | 1, t), pair(m | 1, t ^ top)) for m in range(0, dp_size, 2) for t in range(tensor_size)]
    both = ("dp", "tensor")
    from_core = lax.ppermute(local_two, both, to_even + to_odd)
    turned = lax.ppermute(local_two, both, odd_turn)
    pair_local = jnp.stack([jnp.where(odd, turned, local_two), from_core])
    mlp_pieces = gather_half(pair_local[:, :half_rows], up_bits) + gather_half(pair_local[:, half_rows:], down_bits)
    mgate_low, mup_low, down_low = (
        jnp.concatenate([p[:, :, i * units : (i + 1) * units] for p in mlp_pieces], 1).reshape(width, units)
        for i in range(3)
    )

    def turn_cores(array):
        return jnp.concatenate([array[:, width // 2 :], array[:, : width // 2]], 1)

    def pair_gather(own):
        chips = jnp.concatenate([own, swap_tensor(own, 1)], 0)
        return jnp.concatenate([chips, turn_cores(swap_dp(chips, 1))], 0)

    def pair_scatter(part):
        core = turn_cores(swap_dp(part(1).astype(BF16), 1))
        total = part(0) + core.astype(F32)
        beside = swap_tensor(total[rows:].astype(BF16), 1)
        return total[:rows] + beside.astype(F32)

    grad_final = jnp.where(valid, to_relative(cotangent).astype(F32), 0.0)
    grad_mlp_rows = pair_gather(grad_final.astype(BF16))

    projected = [times_plain(slot, proj_low).astype(BF16) for slot in first_slots]
    query, key, value, normed_head, scale_head, mixed = retain(
        projected, place_arg, log_decay, cosines, sines, heads
    )
    middle = features + line_scatter(lambda s: times_right(mixed[s * rows : (s + 1) * rows], out_low))

    normed_two, inverse_two = norm_parts(middle)
    rows_two = pair_gather((normed_two * gain_second).astype(BF16))
    grad_hidden = times_plain(grad_mlp_rows, down_low)
    mgate_pre = times_plain(rows_two, mgate_low)
    mup_pre = times_plain(rows_two, mup_low)
    below = 0.5 * lax.erfc(-mgate_pre * (0.5**0.5))
    density = jnp.exp(-0.5 * mgate_pre * mgate_pre) * 0.3989422804014327
    hidden = (mgate_pre * below * mup_pre).astype(BF16)
    grad_mgate_low = (grad_hidden * mup_pre * (below + mgate_pre * density)).astype(BF16)
    grad_mup_low = (grad_hidden * mgate_pre * below).astype(BF16)

    grad_second = pair_scatter(
        lambda c: times_right(grad_mgate_low[2 * c * rows : 2 * (c + 1) * rows], mgate_low)
        + times_right(grad_mup_low[2 * c * rows : 2 * (c + 1) * rows], mup_low)
    )
    grad_middle = grad_final + norm_back(normed_two, inverse_two, grad_second, gain_second)
    grad_gain_two = jnp.sum(grad_second * normed_two, 0)

    attn_slots = line_gather(grad_middle.astype(BF16))

    final = middle + pair_scatter(lambda c: times_right(hidden[2 * c * rows : 2 * (c + 1) * rows], down_low))
    output = to_global(jnp.where(valid, final, 0.0).astype(BF16))

    def mlp_grad(left, right):
        left = left.reshape(left.shape[0], 2, 2, 2, width // 8)

        def group(part, end):
            return jnp.stack([times_left(left[:, core, part, end], right) for core in range(2)])

        total = jnp.concatenate(
            [
                scatter_half(group(0, 0), group(0, 1), up_bits),
                scatter_half(group(1, 0), group(1, 1), down_bits),
            ],
            1,
        )
        low = total.astype(BF16)
        core = lax.ppermute(low[1], both, [(b, a) for a, b in to_even + to_odd])
        turn = lax.ppermute(low[0], both, [(b, a) for a, b in odd_turn])
        return jnp.where(odd, turn.astype(F32), total[0]) + core.astype(F32)

    sum_down = mlp_grad(grad_mlp_rows, hidden)
    sum_mgate = mlp_grad(rows_two, grad_mgate_low)
    sum_mup = mlp_grad(rows_two, grad_mup_low)

    grad_mixed = [times_plain(slot, out_low).astype(BF16) for slot in attn_slots]
    grad_proj = retain_back(
        grad_mixed, projected, normed_head, scale_head, query, key, value, place_arg, log_decay, cosines, sines, heads
    )

    def attn_grad(left, right):
        other = swap_dp(times_left(left[:, width // 2 :], right).astype(BF16), 1)
        total = times_left(left[:, : width // 2], right) + other.astype(F32)
        quarter = width // 8
        return jnp.concatenate(
            [
                scatter_half(total[:quarter], total[quarter : 2 * quarter], up_bits),
                scatter_half(total[2 * quarter : 3 * quarter], total[3 * quarter :], down_bits),
            ],
            0,
        )

    sum_out = cut_heads(attn_grad(jnp.concatenate(attn_slots, 0), mixed))
    totals = [times_right(grad_proj[s * rows : (s + 1) * rows], proj_low) for s in range(tensor_size)]
    gain_one_parts = sum(jnp.sum(t * a.astype(F32), 0) for t, a in zip(totals, first_slots)) / gain_first
    grad_first = line_scatter(lambda s: totals[s])
    grad_tokens = grad_middle + norm_back(normed_one, inverse_one, grad_first, gain_first)
    grad_tokens = to_global(grad_tokens.astype(BF16))

    sum_proj = attn_grad(jnp.concatenate(first_slots, 0), grad_proj)
    cuts = [heads * KEY, 2 * heads * KEY, 2 * heads * KEY + heads * VPAD]
    sum_query, sum_key, sum_value, sum_gate = jnp.split(sum_proj, cuts, -1)

    gains = to_global(jnp.stack([gain_one_parts, grad_gain_two]))
    gains = gains + swap_tensor(gains, 1)
    gains = gains + swap_tensor(gains, 2)
    for bit in range(bits):
        gains = gains + swap_dp(gains, 1 << bit)
    return (
        output,
        grad_tokens,
        gains[0],
        gains[1],
        sum_query,
        sum_key,
        cut_heads(sum_value),
        cut_heads(sum_gate),
        sum_out,
        sum_mgate,
        sum_mup,
        sum_down,
    )


def solution(mesh):
    rows = P(("dp", "tensor"), None)
    block = P("dp", "tensor")
    return jax.shard_map(
        partial(per_device, mesh.shape["dp"], mesh.shape["tensor"]),
        mesh=mesh,
        in_specs=(rows, P("dp"), rows, P(), P()) + (block,) * 8,
        out_specs=(rows, rows, P(), P()) + (block,) * 8,
        check_vma=False,
    )
```

```python
from functools import partial

import jax
import jax.numpy as jnp
import numpy as np
from jax import lax
from jax.experimental import pallas as pl
from jax.experimental.pallas import tpu as pltpu
from jax.sharding import PartitionSpec as P

KEY = 256
VAL = 432
VPAD = 512
LANES = 128
EPS = 1e-05
HEAD_EPS = 1.0
F32 = jnp.float32
BF16 = jnp.bfloat16
VMEM_LIMIT = 48 * 1024 * 1024


def times_plain(left, right):
    return jnp.dot(left, right, preferred_element_type=F32)


def times_left(left, right):
    return lax.dot_general(left, right, (((0,), (0,)), ((), ())), preferred_element_type=F32)


def times_right(left, right):
    return lax.dot_general(left, right, (((1,), (1,)), ((), ())), preferred_element_type=F32)


def after(array, *earlier):
    return lax.optimization_barrier((array, *earlier))[0]


def params(**more):
    return pltpu.CompilerParams(vmem_limit_bytes=VMEM_LIMIT, **more)


def cost(flops, moved):
    return pl.CostEstimate(flops=flops // 4, bytes_accessed=moved // 4, transcendentals=0)


def norm_parts(features):
    centred = features - jnp.mean(features, -1, keepdims=True)
    inverse = lax.rsqrt(jnp.mean(centred * centred, -1, keepdims=True) + EPS)
    return centred * inverse, inverse


def norm_back(normed, inverse, grad, gain):
    scaled = grad * gain
    return inverse * (
        scaled
        - jnp.mean(scaled, -1, keepdims=True)
        - normed * jnp.mean(scaled * normed, -1, keepdims=True)
    )


def decay_rows(log_decay, rows, width):
    query = lax.broadcasted_iota(jnp.int32, (rows, width), 0) + (width - rows)
    key = lax.broadcasted_iota(jnp.int32, (rows, width), 1)
    spacing = query - key
    factor = jnp.exp(log_decay * jnp.maximum(spacing, 0).astype(F32))
    return jnp.where(spacing >= 0, factor, 0.0)


def retain_kernel(slots, rows, place_ref, decay_ref, *refs):
    ins, (cos_ref, sin_ref), outs = refs[: 4 * slots], refs[4 * slots : 4 * slots + 2], refs[4 * slots + 2 :]
    query_ref, key_ref, value_ref, normed_ref, scale_ref, mixed_ref, factor_ref, kept_ref = outs
    head = pl.program_id(0)
    place = place_ref[0]
    seq = slots * rows
    half = KEY // 2
    for slot in range(slots):
        start = pl.multiple_of((slot ^ place) * rows, rows)
        cosines, sines = cos_ref[pl.ds(start, rows), :], sin_ref[pl.ds(start, rows), :]
        for source, target, scale in ((ins[slot], query_ref, 1.0), (ins[slots + slot], key_ref, KEY**-0.5)):
            low = source[:, :half].astype(F32)
            high = source[:, half:].astype(F32)
            target[pl.ds(start, rows), :half] = ((low * cosines - high * sines) * scale).astype(BF16)
            target[pl.ds(start, rows), half:] = ((high * cosines + low * sines) * scale).astype(BF16)
        value_ref[pl.ds(start, rows), :] = ins[2 * slots + slot][...]
    factor_ref[...] = decay_rows(decay_ref[head], rows, seq)
    for block in range(slots):
        width = (block + 1) * rows
        scores = times_right(query_ref[block * rows : width, :], key_ref[:width, :])
        weights = (scores * factor_ref[:, seq - width :]).astype(BF16)
        kept_ref[block * rows : width, :] = times_plain(weights, value_ref[:width, :])
    inside = lax.broadcasted_iota(jnp.int32, (rows, VPAD), 1) < VAL
    for slot in range(slots):
        start = pl.multiple_of((slot ^ place) * rows, rows)
        kept = kept_ref[pl.ds(start, rows), :]
        mean = jnp.sum(kept, -1, keepdims=True) / VAL
        centred = jnp.where(inside, kept - mean, 0.0)
        inverse = lax.rsqrt(jnp.sum(centred * centred, -1, keepdims=True) / VAL + HEAD_EPS)
        normed = centred * inverse
        gate = ins[3 * slots + slot][...].astype(F32)
        mixed = gate * jax.nn.sigmoid(gate) * normed
        mixed_ref[slot * rows : (slot + 1) * rows, :] = mixed.astype(BF16)
        normed_ref[slot * rows : (slot + 1) * rows, :] = normed.astype(BF16)
        scale_ref[slot * rows : (slot + 1) * rows, :] = jnp.broadcast_to(inverse, (rows, 128))


def slot_specs(rows, heads):
    first_value = 2 * heads * KEY // VPAD
    return (
        pl.BlockSpec((rows, KEY), lambda h, *_: (0, h)),
        pl.BlockSpec((rows, KEY), lambda h, *_: (0, heads + h)),
        pl.BlockSpec((rows, VPAD), lambda h, *_: (0, first_value + h)),
        pl.BlockSpec((rows, VPAD), lambda h, *_: (0, first_value + heads + h)),
    )


def retain(projected, place, log_decay, cosines, sines, heads):
    slots, rows = len(projected), projected[0].shape[0]
    seq = slots * rows
    specs = slot_specs(rows, heads)
    table = pl.BlockSpec((seq, KEY // 2), lambda h, *_: (0, 0))

    def column(width):
        return pl.BlockSpec((seq, width), lambda h, *_: (0, h))

    return pl.pallas_call(
        partial(retain_kernel, slots, rows),
        out_shape=(
            jax.ShapeDtypeStruct((seq, heads * KEY), BF16),
            jax.ShapeDtypeStruct((seq, heads * KEY), BF16),
            jax.ShapeDtypeStruct((seq, heads * VPAD), BF16),
            jax.ShapeDtypeStruct((seq, heads * VPAD), BF16),
            jax.ShapeDtypeStruct((seq, heads * 128), F32),
            jax.ShapeDtypeStruct((seq, heads * VPAD), BF16),
        ),
        grid_spec=pltpu.PrefetchScalarGridSpec(
            num_scalar_prefetch=2,
            grid=(heads,),
            in_specs=[spec for spec in specs for _ in range(slots)] + [table, table],
            out_specs=[column(KEY), column(KEY), column(VPAD), column(VPAD), column(128), column(VPAD)],
            scratch_shapes=[pltpu.VMEM((rows, seq), F32), pltpu.VMEM((seq, VPAD), F32)],
        ),
        compiler_params=pltpu.CompilerParams(vmem_limit_bytes=VMEM_LIMIT),
        cost_estimate=cost(heads * seq * seq * (KEY + VPAD), heads * seq * 9000),
    )(place, log_decay, *(projected * 4), cosines, sines)


def retain_back_kernel(slots, rows, heads, place_ref, decay_ref, *refs):
    grads, gates, rest = refs[:slots], refs[slots : 2 * slots], refs[2 * slots :]
    (normed_ref, scale_ref, query_ref, key_ref, value_ref, cos_ref, sin_ref, out_ref, factor_ref, ret_ref, key_sum, value_sum) = rest
    head = pl.program_id(0)
    place = place_ref[0]
    seq = slots * rows
    half = KEY // 2
    query_col = pl.multiple_of(head * KEY, KEY)
    key_col = pl.multiple_of((heads + head) * KEY, KEY)
    value_col = pl.multiple_of(2 * heads * KEY + head * VPAD, VPAD)
    gate_col = pl.multiple_of(2 * heads * KEY + (heads + head) * VPAD, VPAD)
    inside = lax.broadcasted_iota(jnp.int32, (rows, VPAD), 1) < VAL
    for slot in range(slots):
        start = pl.multiple_of((slot ^ place) * rows, rows)
        span = slice(slot * rows, (slot + 1) * rows)
        grad, gate = grads[slot][...].astype(F32), gates[slot][...].astype(F32)
        normed, inverse = normed_ref[span, :].astype(F32), scale_ref[span, :1]
        sig = jax.nn.sigmoid(gate)
        out_ref[span, pl.ds(gate_col, VPAD)] = (grad * normed * sig * (1.0 + gate * (1.0 - sig))).astype(BF16)
        grad_normed = grad * gate * sig
        mean = jnp.sum(grad_normed, -1, keepdims=True) / VAL
        along = jnp.sum(grad_normed * normed, -1, keepdims=True) / VAL
        grad_ret = inverse * (grad_normed - mean - normed * along)
        ret_ref[pl.ds(start, rows), :] = jnp.where(inside, grad_ret, 0.0).astype(BF16)
    factor_ref[...] = decay_rows(decay_ref[head], rows, seq)
    key_sum[...] = jnp.zeros_like(key_sum)
    value_sum[...] = jnp.zeros_like(value_sum)
    for block in range(slots):
        width = (block + 1) * rows
        span = slice(block * rows, width)
        query, ret, keys = query_ref[span, :], ret_ref[span, :], key_ref[:width, :]
        factor = factor_ref[:, seq - width :]
        weights = (times_right(query, keys) * factor).astype(BF16)
        grad_scores = (times_right(ret, value_ref[:width, :]) * factor).astype(BF16)
        value_sum[:width, :] += times_left(weights, ret)
        key_sum[:width, :] += times_left(grad_scores, query)
        grad_query = times_plain(grad_scores, keys)
        row = pl.multiple_of((block ^ place) * rows, rows)
        cosines, sines = cos_ref[span, :], sin_ref[span, :]
        low, high = grad_query[:, :half], grad_query[:, half:]
        out_ref[pl.ds(row, rows), pl.ds(query_col, half)] = (low * cosines + high * sines).astype(BF16)
        out_ref[pl.ds(row, rows), pl.ds(pl.multiple_of(query_col + half, half), half)] = (
            high * cosines - low * sines
        ).astype(BF16)
    for block in range(slots):
        span = slice(block * rows, (block + 1) * rows)
        row = pl.multiple_of((block ^ place) * rows, rows)
        cosines, sines = cos_ref[span, :], sin_ref[span, :]
        low, high = key_sum[span, :half] * KEY**-0.5, key_sum[span, half:] * KEY**-0.5
        out_ref[pl.ds(row, rows), pl.ds(key_col, half)] = (low * cosines + high * sines).astype(BF16)
        out_ref[pl.ds(row, rows), pl.ds(pl.multiple_of(key_col + half, half), half)] = (
            high * cosines - low * sines
        ).astype(BF16)
        out_ref[pl.ds(row, rows), pl.ds(value_col, VPAD)] = value_sum[span, :].astype(BF16)


def retain_back(grads, projected, normed, scale, query, key, value, place, log_decay, cosines, sines, heads):
    slots, rows = len(projected), projected[0].shape[0]
    seq = slots * rows
    columns = 2 * heads * (KEY + VPAD)
    table = pl.BlockSpec((seq, KEY // 2), lambda h, *_: (0, 0))

    def column(width):
        return pl.BlockSpec((seq, width), lambda h, *_: (0, h))

    return pl.pallas_call(
        partial(retain_back_kernel, slots, rows, heads),
        out_shape=jax.ShapeDtypeStruct((seq, columns), BF16),
        grid_spec=pltpu.PrefetchScalarGridSpec(
            num_scalar_prefetch=2,
            grid=(heads,),
            in_specs=[pl.BlockSpec((rows, VPAD), lambda h, *_: (0, h))] * slots
            + [slot_specs(rows, heads)[3]] * slots
            + [column(VPAD), column(128), column(KEY), column(KEY), column(VPAD), table, table],
            out_specs=pl.BlockSpec((seq, columns), lambda h, *_: (0, 0)),
            scratch_shapes=[
                pltpu.VMEM((rows, seq), F32),
                pltpu.VMEM((seq, VPAD), BF16),
                pltpu.VMEM((seq, KEY), F32),
                pltpu.VMEM((seq, VPAD), F32),
            ],
        ),
        compiler_params=pltpu.CompilerParams(vmem_limit_bytes=VMEM_LIMIT),
        cost_estimate=cost(heads * seq * seq * (3 * KEY + 2 * VPAD), heads * seq * 10000),
    )(place, log_decay, *grads, *projected, normed, scale, query, key, value, cosines, sines)


def rows_kernel(slots, pieces, *refs):
    lefts, weights, outs = refs[:slots], refs[slots : slots + pieces], refs[slots + pieces :]
    left = jnp.concatenate([ref[...] for ref in lefts], 0)
    result = times_plain(left, jnp.concatenate([ref[...] for ref in weights], 0)).astype(BF16)
    rows = lefts[0].shape[0]
    for slot in range(slots):
        outs[slot][...] = result[slot * rows : (slot + 1) * rows]


def rows_times(lefts, pieces, first, columns, tile=512):
    rows, width = lefts[0].shape
    return pl.pallas_call(
        partial(rows_kernel, len(lefts), len(pieces)),
        out_shape=[jax.ShapeDtypeStruct((rows, columns), BF16)] * len(lefts),
        grid=(columns // tile,),
        in_specs=[pl.BlockSpec((rows, width), lambda n: (0, 0))] * len(lefts)
        + [pl.BlockSpec((p.shape[0], tile), lambda n: (0, n + first // tile)) for p in pieces],
        out_specs=[pl.BlockSpec((rows, tile), lambda n: (0, n))] * len(lefts),
        compiler_params=params(),
        cost_estimate=cost(2 * len(lefts) * rows * width * columns, 2 * width * columns),
    )(*lefts, *pieces)


def rows_back_kernel(slots, pieces, weigh, *refs):
    lefts, weights, rest = refs[:slots], refs[slots : slots + pieces], refs[slots + pieces :]
    total = rest[-1]
    step = pl.program_id(0)
    left = jnp.concatenate([ref[...] for ref in lefts], 0)
    part = times_right(left, jnp.concatenate([ref[...] for ref in weights], 0))

    @pl.when(step == 0)
    def _():
        total[...] = part

    @pl.when(step > 0)
    def _():
        total[...] += part

    @pl.when(step == pl.num_programs(0) - 1)
    def _():
        rows = lefts[0].shape[0]
        for slot in range(slots):
            rest[weigh * slots + slot][...] = total[slot * rows : (slot + 1) * rows, :].astype(BF16)
        if weigh:
            other = jnp.concatenate([ref[...] for ref in rest[:slots]], 0).astype(F32)
            along = jnp.sum(total[...] * other, 0, keepdims=True)
            rest[2 * slots][...] = jnp.broadcast_to(along, (8, along.shape[1]))


def rows_back(left, slots, pieces, first=0, weigh=(), tile=512):
    rows = left.shape[0] // 4
    columns = left.shape[1]
    width = sum(p.shape[0] for p in pieces)
    whole = pl.BlockSpec((rows, width), lambda k: (0, 0))
    return pl.pallas_call(
        partial(rows_back_kernel, len(slots), len(pieces), 1 if weigh else 0),
        out_shape=[jax.ShapeDtypeStruct((rows, width), BF16)] * len(slots)
        + ([jax.ShapeDtypeStruct((8, width), F32)] if weigh else []),
        grid=(columns // tile,),
        in_specs=[pl.BlockSpec((rows, tile), partial(lambda s, k: (s, k), s)) for s in slots]
        + [pl.BlockSpec((p.shape[0], tile), lambda k: (0, k + first // tile)) for p in pieces]
        + [whole] * len(weigh),
        out_specs=[whole] * len(slots) + ([pl.BlockSpec((8, width), lambda k: (0, 0))] if weigh else []),
        scratch_shapes=[pltpu.VMEM((len(slots) * rows, width), F32)],
        compiler_params=params(),
        cost_estimate=cost(2 * len(slots) * rows * width * columns, 2 * width * columns),
    )(*([left] * len(slots)), *pieces, *weigh)


def turn(array):
    middle = array.shape[1] // 2
    return jnp.concatenate([array[:, middle:], array[:, :middle]], 1)


def mlp_kernel(pieces, units, own_ref, other_ref, own_grad_ref, other_grad_ref, *refs):
    sources, outs = refs[:pieces], refs[pieces : pieces + 8]
    gate_ref, up_ref, down_ref, semaphores = refs[pieces + 8 :]
    rows = own_ref.shape[0]
    height = sources[0].shape[1]
    copies = []
    for part, target in enumerate((gate_ref, up_ref, down_ref)):
        for core in range(2):
            for index, source in enumerate(sources):
                place = core * pieces + index
                copy = pltpu.make_async_copy(
                    source.at[core, :, pl.ds(part * units, units)],
                    target.at[pl.ds(place * height, height), :],
                    semaphores.at[part, place],
                )
                copy.start()
                copies.append(copy)
    third = 2 * pieces
    left = jnp.concatenate([own_ref[...], turn(other_ref[...])], 0)
    grad = jnp.concatenate([own_grad_ref[...], turn(other_grad_ref[...])], 0)
    for copy in copies[:third]:
        copy.wait()
    gate = times_plain(left, gate_ref[...])
    for copy in copies[third : 2 * third]:
        copy.wait()
    up = times_plain(left, up_ref[...])
    for copy in copies[2 * third :]:
        copy.wait()
    grad_hidden = times_plain(grad, down_ref[...])
    below = 0.5 + 0.5 * lax.erf(gate * (0.5**0.5))
    density = jnp.exp(-0.5 * gate * gate) * 0.3989422804014327
    smooth = gate * below
    hidden = (smooth * up).astype(BF16)
    grad_gate = (grad_hidden * up * (below + gate * density)).astype(BF16)
    grad_up = (grad_hidden * smooth).astype(BF16)
    for slot in range(2):
        span = slice(slot * rows, (slot + 1) * rows)
        outs[slot][...] = hidden[span]
        outs[2 + slot][...] = grad_gate[span]
        outs[4 + slot][...] = grad_up[span]
    back = times_right(grad_gate, gate_ref[...]) + times_right(grad_up, up_ref[...])
    outs[6][...] = back[:rows].astype(BF16)
    outs[7][...] = turn(back[rows:]).astype(BF16)


def mlp(own, other, own_grad, other_grad, pieces):
    rows, width = own.shape
    units = pieces[0].shape[2] // 3
    whole = pl.BlockSpec(memory_space=pltpu.VMEM)
    small, large = jax.ShapeDtypeStruct((rows, units), BF16), jax.ShapeDtypeStruct((rows, width), BF16)
    return pl.pallas_call(
        partial(mlp_kernel, len(pieces), units),
        out_shape=[small] * 6 + [large] * 2,
        in_specs=[whole] * 4 + [pl.BlockSpec(memory_space=pl.ANY)] * len(pieces),
        out_specs=[whole] * 8,
        scratch_shapes=[pltpu.VMEM((width, units), BF16)] * 3 + [pltpu.SemaphoreType.DMA((3, 2 * len(pieces)))],
        compiler_params=params(),
        cost_estimate=cost(2 * 2 * rows * width * units * 5, 6 * width * units),
    )(own, other, own_grad, other_grad, *pieces)


def down_kernel(pieces, *refs):
    lefts, weights, outs = refs[:4], refs[4 : 4 + pieces], refs[4 + pieces :]
    rows = lefts[0].shape[0]
    weight = jnp.concatenate([ref[core] for core in range(2) for ref in weights], 0)
    for core in range(2):
        left = jnp.concatenate([lefts[2 * core][...], lefts[2 * core + 1][...]], 0)
        result = times_right(left, weight)
        outs[core][...] = (turn(result) if core else result).astype(BF16)


def mlp_down(hidden, pieces):
    rows, units = hidden[0].shape
    width = 2 * sum(p.shape[1] for p in pieces)
    whole = pl.BlockSpec((rows, units), lambda n: (0, 0))
    out = pl.BlockSpec((2 * rows, width), lambda n: (0, 0))
    return pl.pallas_call(
        partial(down_kernel, len(pieces)),
        out_shape=[jax.ShapeDtypeStruct((2 * rows, width), BF16)] * 2,
        grid=(1,),
        in_specs=[whole] * 4 + [pl.BlockSpec((2, p.shape[1], units), lambda n: (0, 0, 2)) for p in pieces],
        out_specs=[out] * 2,
        compiler_params=params(),
        cost_estimate=cost(8 * rows * width * units, 2 * width * units),
    )(*hidden, *pieces)


def mlp_grad_kernel(*refs):
    lefts, grads, rights, outs = refs[:4], refs[4:8], refs[8:20], refs[20:]
    left = jnp.concatenate([ref[...] for ref in lefts], 0)
    grad = jnp.concatenate([ref[...] for ref in grads], 0)
    parts = []
    for index, rows in enumerate((left, left, grad)):
        right = jnp.concatenate([ref[...] for ref in rights[4 * index : 4 * index + 4]], 0)
        parts.append(times_left(rows, right).astype(BF16))
    result = jnp.concatenate(parts, 1)
    for part in range(2):

        @pl.when(pl.program_id(0) == part)
        def _():
            outs[part][...] = result


def mlp_grads(end, core, lefts, grads, grad_gate, grad_up, hidden):
    rows, width = lefts[0].shape
    units = hidden[0].shape[1]
    tile = width // 8

    def column(other, step):
        return (0, (core ^ other) * 4 + step * 2 + end)

    narrow = [pl.BlockSpec((rows, tile), partial(column, other)) for other in (0, 0, 1, 1)]
    whole = pl.BlockSpec((rows, units), lambda i: (0, 0))
    return pl.pallas_call(
        mlp_grad_kernel,
        out_shape=[jax.ShapeDtypeStruct((tile, 3 * units), BF16)] * 2,
        grid=(2,),
        in_specs=narrow * 2 + [whole] * 12,
        out_specs=[pl.BlockSpec((tile, 3 * units), lambda i: (0, 0))] * 2,
        compiler_params=params(),
        cost_estimate=cost(2 * rows * width * units * 3, 2 * width * units),
    )(*lefts, *grads, *grad_gate, *grad_up, *hidden)


def attn_grad_kernel(*refs):
    left = jnp.concatenate([ref[...] for ref in refs[:4]], 0)
    refs[5][...] = times_left(left, refs[4][...]).astype(BF16)


def attn_grad_add_kernel(*refs):
    left = jnp.concatenate([ref[...] for ref in refs[:4]], 0)
    result = (times_left(left, refs[4][...]) + refs[5][...].astype(F32)).astype(BF16)
    for part in range(2):

        @pl.when(pl.program_id(0) == part)
        def _():
            refs[6 + part][...] = result


def attn_grads(end, lefts, right, other=None):
    rows, width = lefts[0].shape
    columns = right.shape[1]
    tile = width // 8
    core = 1 if other is None else 0
    narrow = pl.BlockSpec((rows, tile), lambda i: (0, core * 4 + 2 * i + end))
    block = pl.BlockSpec((tile, columns), lambda i: (i, 0))
    whole = pl.BlockSpec((tile, columns), lambda i: (0, 0))
    return pl.pallas_call(
        attn_grad_kernel if core else attn_grad_add_kernel,
        out_shape=jax.ShapeDtypeStruct((2 * tile, columns), BF16)
        if core
        else [jax.ShapeDtypeStruct((tile, columns), BF16)] * 2,
        grid=(2,),
        in_specs=[narrow] * 4 + [pl.BlockSpec(right.shape, lambda i: (0, 0))] + ([] if core else [block]),
        out_specs=block if core else [whole] * 2,
        compiler_params=params(),
        cost_estimate=cost(2 * rows * width * columns, width * columns),
    )(*lefts, right, *([] if core else [other]))


def own_order_kernel(blocks, sizes, mine_ref, *refs):
    (shard_rows, half_rows), count = sizes, len(refs) // 2
    for index, (mask, part) in enumerate(blocks):
        start = pl.multiple_of((mine_ref[0] ^ mask) * shard_rows + part * half_rows, half_rows)
        for source, target in zip(refs[:count], refs[count:]):
            target[:, index * half_rows : (index + 1) * half_rows] = source[:, pl.ds(start, half_rows)]


def global_order_kernel(blocks, sizes, mine_ref, source, target):
    shard_rows, half_rows = sizes
    for index, (mask, part) in enumerate(blocks):
        start = pl.multiple_of((mine_ref[0] ^ mask) * shard_rows + part * half_rows, half_rows)
        target[:, pl.ds(start, half_rows)] = source[:, index * half_rows : (index + 1) * half_rows]


def reorder(kernel, blocks, sizes, mine, arrays):
    specs = [pl.BlockSpec(a.shape, lambda i, *_: (0, 0)) for a in arrays]
    return pl.pallas_call(
        partial(kernel, blocks, sizes),
        out_shape=[jax.ShapeDtypeStruct(a.shape, a.dtype) for a in arrays],
        grid_spec=pltpu.PrefetchScalarGridSpec(num_scalar_prefetch=1, grid=(1,), in_specs=specs, out_specs=specs),
        compiler_params=params(),
    )(mine, *arrays)


def widen(array, height):
    return jnp.concatenate([array, jnp.zeros((height - array.shape[0], array.shape[1]), array.dtype)], 0)


def send_attn_kernel(heads, *refs):
    sources, targets = refs[:5], refs[5:]
    half = targets[0].shape[0]
    spans = [slice(part * half, (part + 1) * half) for part in range(2)]
    for index, source in enumerate(sources):
        if index < 2:
            for span, target in zip(spans, targets):
                target[:, index * heads * KEY : (index + 1) * heads * KEY] = source[span, :].astype(BF16)
        else:
            for head in range(heads):
                column = 2 * heads * KEY + ((index - 2) * heads + head) * VPAD
                block = widen(source[head * VAL : (head + 1) * VAL, :], VPAD).T.astype(BF16)
                for span, target in zip(spans, targets):
                    target[:, column : column + VPAD] = block[span, :]


def send_attn(weights, heads):
    half = weights[0].shape[0] // 2
    columns = heads * (2 * KEY + 3 * VPAD)
    arrays = [*weights[:2], *(w.T for w in weights[2:])]
    return pl.pallas_call(
        partial(send_attn_kernel, heads),
        out_shape=[jax.ShapeDtypeStruct((half, columns), BF16)] * 2,
        grid=(1,),
        in_specs=[pl.BlockSpec(w.shape, lambda i: (0, 0)) for w in arrays],
        out_specs=[pl.BlockSpec((half, columns), lambda i: (0, 0))] * 2,
        compiler_params=params(),
        cost_estimate=cost(0, half * columns * 12),
    )(*arrays)


def send_mlp_kernel(padded, *refs):
    target = refs[-1]
    for index, source in enumerate(refs[:-1]):
        target[:, index * padded : (index + 1) * padded] = widen(source[...], padded).T.astype(BF16)


def send_mlp(weights, padded):
    rows, units = weights[0].shape
    return pl.pallas_call(
        partial(send_mlp_kernel, padded),
        out_shape=jax.ShapeDtypeStruct((rows, len(weights) * padded), BF16),
        grid=(1,),
        in_specs=[pl.BlockSpec((units, rows), lambda i: (0, 0))] * len(weights),
        out_specs=pl.BlockSpec((rows, len(weights) * padded), lambda i: (0, 0)),
        compiler_params=params(),
        cost_estimate=cost(0, rows * padded * 18),
    )(*(w.T for w in weights))


def receive_kernel(narrow, heads, *refs):
    targets = refs[4:]
    total = jnp.concatenate(
        [refs[2 * part][...].astype(F32) + refs[2 * part + 1][...].astype(F32) for part in range(2)], 0
    )
    column = 0
    for index, target in enumerate(targets):
        if index < narrow:
            target[...] = total[:, column : column + heads * KEY]
            column += heads * KEY
        else:
            for head in range(heads):
                target[head * VAL : (head + 1) * VAL, :] = total[:, column : column + VPAD].T[:VAL]
                column += VPAD


def receive_attn(parts, narrow, wide, heads):
    rows = 2 * parts[0].shape[0]
    shapes = [(rows, heads * KEY)] * narrow + [(heads * VAL, rows)] * wide
    found = pl.pallas_call(
        partial(receive_kernel, narrow, heads),
        out_shape=[jax.ShapeDtypeStruct(s, F32) for s in shapes],
        grid=(1,),
        in_specs=[pl.BlockSpec(p.shape, lambda i: (0, 0)) for p in parts],
        out_specs=[pl.BlockSpec(s, lambda i: (0, 0)) for s in shapes],
        compiler_params=params(),
        cost_estimate=cost(0, rows * sum(s[0] for s in shapes) * 4),
    )(*parts)
    return [*found[:narrow], *(f.T for f in found[narrow:])]


def receive_mlp_kernel(padded, odd_ref, kept, turned, core, *targets):
    first = jnp.where(odd_ref[0] == 1, turned[...], kept[...]).astype(F32)
    total = first + core[...].astype(F32)
    for index, target in enumerate(targets):
        target[...] = total[:, index * padded : (index + 1) * padded].T[: target.shape[0]]


def receive_mlp(odd, kept, turned, core, units):
    rows, columns = kept.shape
    whole = pl.BlockSpec((rows, columns), lambda i, *_: (0, 0))
    found = pl.pallas_call(
        partial(receive_mlp_kernel, columns // 3),
        out_shape=[jax.ShapeDtypeStruct((units, rows), F32)] * 3,
        grid_spec=pltpu.PrefetchScalarGridSpec(
            num_scalar_prefetch=1,
            grid=(1,),
            in_specs=[whole] * 3,
            out_specs=[pl.BlockSpec((units, rows), lambda i, *_: (0, 0))] * 3,
        ),
        compiler_params=params(),
        cost_estimate=cost(0, rows * columns * 10),
    )(odd, kept, turned, core)
    return [f.T for f in found]


def per_device(
    dp_size,
    tensor_size,
    tokens,
    lengths,
    cotangent,
    gain_one,
    gain_two,
    w_query,
    w_key,
    w_value,
    w_gate,
    w_out,
    w_mgate,
    w_mup,
    w_down,
):
    rows, width = tokens.shape
    seq = rows * tensor_size
    heads = w_query.shape[1] // KEY
    units = w_mgate.shape[1]
    shard_rows = w_query.shape[0]
    half_rows = shard_rows // 2
    bits = dp_size.bit_length() - 1
    mine, place = lax.axis_index("dp"), lax.axis_index("tensor")
    inner = (place == 1) | (place == 2)
    odd = (mine & 1) == 1
    up_bits = list(range(1, bits))
    down_bits = up_bits[::-1]

    def add(*arrays):
        return sum(array.astype(F32) for array in arrays)

    def swap_dp(array, mask):
        return lax.ppermute(array, "dp", [(i, i ^ mask) for i in range(dp_size)])

    def move_tensor(array, pairs):
        return lax.ppermute(array, "tensor", pairs)

    def swap_tensor(array, mask):
        return move_tensor(array, [(i, i ^ mask) for i in range(tensor_size)])

    across = [(1, 2), (2, 1)]
    outward = [(1, 0), (2, 3)]
    inward = [(0, 1), (3, 2)]

    def pair(dp_index, tensor_index):
        return dp_index * tensor_size + tensor_index

    top = tensor_size - 1
    to_even = [(pair(m | 1, t), pair(m, t)) for m in range(0, dp_size, 2) for t in range(tensor_size)]
    to_odd = [(pair(m, t), pair(m | 1, t ^ top)) for m in range(0, dp_size, 2) for t in range(tensor_size)]
    odd_turn = [(pair(m | 1, t), pair(m | 1, t ^ top)) for m in range(0, dp_size, 2) for t in range(tensor_size)]
    both = ("dp", "tensor")

    def hold(array):
        return after(array, token[0])

    def close(*results):
        token[0] = after(token[0], *results)

    def line_out(slots, beside, middle):
        return move_tensor(hold(beside), across), move_tensor(hold(middle), outward)

    def line_all(own, beside, middle, far_inner, far_ends, last):
        return own, beside, jnp.where(inner, far_inner, far_ends), jnp.where(inner, middle, last)

    def first_level(piece, order):
        return swap_dp(piece, 1 << order[0])

    def second_level(piece, order):
        return swap_dp(hold(piece), 1 << order[1])

    def further(pieces, order):
        for bit in order[2:]:
            pieces = pieces + [swap_dp(p, 1 << bit) for p in pieces]
        return pieces

    def to_core(piece):
        return swap_dp(hold(piece), 1)

    def sum_start(high, order):
        return swap_dp(hold(high), 1 << order[-1])

    def sum_split(low, come):
        middle = low.shape[0] // 2
        return [add(low[span], come[span]).astype(BF16) for span in (slice(0, middle), slice(middle, 2 * middle))]

    def sum_end(low, high, order):
        for bit in order[-2:0:-1]:
            low, high = sum_split(low, swap_dp(hold(high), 1 << bit))
        return low, swap_dp(hold(high), 1 << order[0])

    blocks = [
        (chip << 1 | core, part)
        for core in range(2)
        for part, order in ((0, up_bits), (1, down_bits))
        for chip in [sum((i >> j & 1) << (b - 1) for j, b in enumerate(order)) for i in range(dp_size // 2)]
    ]

    sizes = (shard_rows, half_rows)
    aligned = half_rows % LANES == 0
    mine_arg = mine.astype(jnp.int32).reshape(1)

    def to_relative(*arrays):
        if aligned:
            return reorder(own_order_kernel, blocks, sizes, mine_arg, arrays)
        return [
            jnp.concatenate(
                [
                    lax.dynamic_slice_in_dim(a, (mine ^ mask) * shard_rows + part * half_rows, half_rows, -1)
                    for mask, part in blocks
                ],
                -1,
            )
            for a in arrays
        ]

    def to_global(array):
        if aligned:
            return reorder(global_order_kernel, blocks, sizes, mine_arg, [array])[0]
        found = []
        for shard in range(dp_size):
            mask = mine ^ shard
            for part, order in ((0, up_bits), (1, down_bits)):
                chip = sum((mask >> b & 1) << j for j, b in enumerate(order))
                index = (mask & 1) * dp_size + part * (dp_size // 2) + chip
                found.append(lax.dynamic_slice_in_dim(array, index * half_rows, half_rows, -1))
        return jnp.concatenate(found, -1)

    first_row = place * rows
    valid = (first_row + jnp.arange(rows, dtype=jnp.int32) < lengths[0])[:, None]
    head_ids = (place * heads + jnp.arange(heads, dtype=jnp.int32)).astype(F32)
    log_decay = jnp.log(1.0 - jnp.exp2(-5.0 - head_ids))
    place_arg = place.astype(jnp.int32).reshape(1)
    freqs = np.float32(10000.0) ** (-np.arange(KEY // 2, dtype=np.float32) / np.float32(KEY // 2))
    angles = np.arange(seq, dtype=np.float32)[:, None] * freqs[None, :]
    cosines, sines = jnp.asarray(np.cos(angles)), jnp.asarray(np.sin(angles))

    token = [mine_arg]
    proj_columns, out_columns = 2 * heads * (KEY + VPAD), heads * VPAD
    padded = -(-units // LANES) * LANES

    sent_up, sent_down = send_attn((w_query, w_key, w_value, w_gate, w_out), heads)
    features_low, gain_first = to_relative(tokens, gain_one[None])
    features = features_low.astype(F32)
    normed_one, inverse_one = norm_parts(features)
    first_own = (normed_one * gain_first).astype(BF16)
    close(sent_up, sent_down, first_own)

    up_one = first_level(hold(sent_up), up_bits)
    down_one = first_level(hold(sent_down), down_bits)
    first_beside = swap_tensor(hold(first_own), 1)
    first_middle = move_tensor(hold(first_own), across)
    local_two = send_mlp((w_mgate, w_mup, hold(w_down)), padded)
    cotangent_low, gain_second = to_relative(hold(cotangent), gain_two[None])
    grad_own = jnp.where(valid, cotangent_low, 0.0)
    grad_final = grad_own.astype(F32)
    close(up_one, down_one, first_beside, first_middle, local_two, grad_own)

    up_two, down_two = second_level(sent_up, up_bits), second_level(sent_down, down_bits)
    first_far = line_out(None, first_beside, first_middle)
    core_one = [to_core(p) for p in (sent_up, sent_down)]
    close(up_two, down_two, *first_far, *core_one)

    up_three, down_three = second_level(up_one, up_bits), second_level(down_one, down_bits)
    first_last = move_tensor(hold(first_far[0]), outward)
    core_two = [to_core(p) for p in (up_one, down_one)]
    close(up_three, down_three, first_last, *core_two)

    up_all = further([sent_up, up_one, up_two, up_three], up_bits)
    down_all = further([sent_down, down_one, down_two, down_three], down_bits)
    up_core = [core_one[0], core_two[0]] + [to_core(p) for p in up_all[2:]]
    down_core = [core_one[1], core_two[1]] + [to_core(p) for p in down_all[2:]]
    close(*up_core, *down_core)
    attn_low = up_all + down_all + up_core + down_core
    first_slots = line_all(first_own, first_beside, first_middle, *first_far, first_last)

    turned = lax.ppermute(hold(local_two), both, odd_turn)
    grad_beside = swap_tensor(hold(grad_own), 1)
    grad_core = to_core(grad_own)
    projected = rows_times([hold(first_slots[0]), *first_slots[1:]], attn_low, 0, proj_columns)
    query, key, value, normed_head, scale_head, mixed = retain(
        projected, place_arg, log_decay, cosines, sines, heads
    )
    close(turned, grad_beside, grad_core, mixed)

    from_core = lax.ppermute(hold(local_two), both, to_even + to_odd)
    grad_rows = [grad_own, grad_beside, grad_core, to_core(grad_beside)]
    mixed_second, mixed_third = rows_back(hold(mixed), (2, 3), attn_low, proj_columns)
    from_ends = move_tensor(mixed_third, inward)
    mixed_own, mixed_first = rows_back(after(mixed, mixed_third), (0, 1), attn_low, proj_columns)
    mixed_partial = add(mixed_second, from_ends).astype(BF16)
    close(from_core, grad_rows[3], mixed_partial, mixed_own)

    def pair_half(span):
        return jnp.stack([jnp.where(odd, turned[span], local_two[span]), hold(from_core)[span]])

    mlp_up, mlp_across = pair_half(slice(0, half_rows)), pair_half(slice(half_rows, shard_rows))
    mlp_up_one, mlp_across_one = first_level(mlp_up, up_bits), first_level(mlp_across, down_bits)
    from_inner = move_tensor(hold(mixed_partial), across)
    from_ends = move_tensor(hold(mixed_second), inward)
    close(mlp_up_one, mlp_across_one, from_inner, from_ends)

    mlp_up_two, mlp_across_two = second_level(mlp_up, up_bits), second_level(mlp_across, down_bits)
    from_beside = swap_tensor(add(mixed_first, hold(from_inner)).astype(BF16), 1)
    from_middle = move_tensor(add(mixed_third, hold(from_ends)).astype(BF16), across)
    middle = features + add(mixed_own, from_beside, from_middle)
    normed_two, inverse_two = norm_parts(middle)
    second_own = (normed_two * gain_second).astype(BF16)
    close(mlp_up_two, mlp_across_two, second_own)

    mlp_up_three, mlp_across_three = second_level(mlp_up_one, up_bits), second_level(mlp_across_one, down_bits)
    second_beside = swap_tensor(hold(second_own), 1)
    second_core = to_core(second_own)
    close(mlp_up_three, mlp_across_three, second_beside, second_core)
    mlp_pieces = further([mlp_up, mlp_up_one, mlp_up_two, mlp_up_three], up_bits) + further(
        [mlp_across, mlp_across_one, mlp_across_two, mlp_across_three], down_bits
    )

    first_part = mlp(hold(second_own), second_core, grad_rows[0], grad_rows[2], mlp_pieces)
    second_far = to_core(second_beside)
    second_rows = [second_own, second_beside, second_core, second_far]
    close(first_part[7], second_far)

    second_part = mlp(hold(second_beside), second_far, grad_rows[1], grad_rows[3], mlp_pieces)
    near_core = to_core(first_part[7])
    close(second_part[7], near_core)
    hidden, grad_gate, grad_up = (
        [first_part[2 * i], second_part[2 * i], first_part[2 * i + 1], second_part[2 * i + 1]] for i in range(3)
    )

    far = add(second_part[6], to_core(second_part[7])).astype(BF16)
    near = add(first_part[6], near_core)
    close(far)

    def mlp_grad(end, core):
        return mlp_grads(end, core, [hold(second_rows[0]), *second_rows[1:]], grad_rows, grad_gate, grad_up, hidden)

    second_back = swap_tensor(hold(far), 1)
    high = [mlp_grad(1, 0), mlp_grad(1, 1)]
    down_own, down_other = mlp_down([hold(hidden[0]), *hidden[1:]], mlp_pieces)
    close(second_back, *high[0], *high[1], down_own)

    grad_second = near + hold(second_back).astype(F32)
    grad_middle = grad_final + norm_back(normed_two, inverse_two, grad_second, gain_second)
    grad_gain_two = jnp.sum(grad_second * normed_two, 0)
    attn_own = grad_middle.astype(BF16)
    attn_beside = swap_tensor(attn_own, 1)
    attn_middle = move_tensor(attn_own, across)
    come = [[sum_start(high[0][0], up_bits), sum_start(high[0][1], down_bits)]]
    low = [mlp_grad(0, 0), mlp_grad(0, 1)]
    close(attn_beside, attn_middle, *come[0], *low[0], *low[1])

    attn_far = line_out(None, attn_beside, attn_middle)
    come.append([sum_start(high[1][0], up_bits), sum_start(high[1][1], down_bits)])
    down_core = to_core(down_other)
    close(*attn_far, *come[1], down_core)

    attn_last = move_tensor(hold(attn_far[0]), outward)
    mlp_total = []
    for core in range(2):
        ends = []
        for part, order in enumerate((up_bits, down_bits)):
            ends.append(add(*sum_end(*sum_split(low[core][part], hold(come[core][part])), order)).astype(BF16))
        mlp_total.append(jnp.concatenate(ends, 0))
    down_sum = add(down_own, hold(down_core))
    down_sent = down_sum[rows:].astype(BF16)
    close(attn_last, *mlp_total, down_sent)
    attn_slots = line_all(attn_own, attn_beside, attn_middle, *attn_far, attn_last)

    grad_turn = lax.ppermute(hold(mlp_total[0]), both, [(b, a) for a, b in odd_turn])
    down_beside = swap_tensor(hold(down_sent), 1)
    grad_mixed = rows_times([hold(attn_slots[0]), *attn_slots[1:]], attn_low, proj_columns, out_columns)
    grad_proj = retain_back(
        grad_mixed, projected, normed_head, scale_head, query, key, value, place_arg, log_decay, cosines, sines, heads
    )
    back_second, back_third, gain_far = rows_back(grad_proj, (2, 3), attn_low, 0, first_slots[2:])
    close(grad_turn, down_beside, back_third)

    grad_core = lax.ppermute(hold(mlp_total[1]), both, [(b, a) for a, b in to_even + to_odd])
    from_ends = move_tensor(hold(back_third), inward)
    other_high = attn_grads(1, first_slots, hold(grad_proj))
    other_low = attn_grads(0, first_slots, after(grad_proj, other_high))
    core_high = swap_dp(other_high, 1)
    close(grad_core, from_ends, core_high, other_low)

    from_inner = move_tensor(add(back_second, hold(from_ends)).astype(BF16), across)
    from_ends = move_tensor(hold(back_second), inward)
    core_low = to_core(other_low)
    up_high, down_high = attn_grads(1, first_slots, hold(grad_proj), core_high)
    back_own, back_first, gain_near = rows_back(after(grad_proj, up_high), (0, 1), attn_low, 0, first_slots[:2])
    close(from_inner, from_ends, core_low, back_own)

    from_beside = swap_tensor(add(back_first, hold(from_inner)).astype(BF16), 1)
    from_middle = move_tensor(add(back_third, hold(from_ends)).astype(BF16), across)
    proj_come = sum_start(up_high, up_bits), sum_start(down_high, down_bits)
    up_low, down_low = attn_grads(0, first_slots, hold(grad_proj), core_low)
    out_other_high = attn_grads(1, attn_slots, after(mixed, up_low))
    out_other_low = attn_grads(0, attn_slots, after(mixed, out_other_high))
    out_up_high, out_down_high = attn_grads(1, attn_slots, after(mixed, out_other_low), swap_dp(out_other_high, 1))
    out_up_low, out_down_low = attn_grads(0, attn_slots, after(mixed, out_up_high), swap_dp(out_other_low, 1))
    close(from_beside, from_middle, *proj_come, out_up_low)

    gains = to_global(jnp.stack([hold(gain_far[0] + gain_near[0]) / gain_first[0], grad_gain_two]))
    gains = gains + swap_tensor(gains, 1)
    gains = gains + swap_tensor(gains, 2)
    gains = gains + swap_dp(gains, 1)
    proj_up = sum_end(*sum_split(up_low, hold(proj_come[0])), up_bits)
    proj_down = sum_end(*sum_split(down_low, hold(proj_come[1])), down_bits)
    out_come = sum_start(out_up_high, up_bits), sum_start(out_down_high, down_bits)
    grad_first = add(back_own, hold(from_beside), from_middle)
    grad_tokens = grad_middle + norm_back(normed_one, inverse_one, grad_first, gain_first)
    grad_tokens = to_global(grad_tokens.astype(BF16))
    final = middle + down_sum[:rows] + hold(down_beside).astype(F32)
    output = to_global(jnp.where(valid, final, 0.0).astype(BF16))
    sum_mgate, sum_mup, sum_down = receive_mlp(
        (mine & 1).astype(jnp.int32).reshape(1), hold(mlp_total[0]), grad_turn, grad_core, units
    )
    close(gains, *proj_up, *proj_down, *out_come, grad_tokens, output, sum_mgate)

    out_up = sum_end(*sum_split(out_up_low, hold(out_come[0])), up_bits)
    out_down = sum_end(*sum_split(out_down_low, hold(out_come[1])), down_bits)
    gains = hold(gains)
    for bit in range(1, bits):
        gains = gains + swap_dp(gains, 1 << bit)
    sum_query, sum_key, sum_value, sum_gate = receive_attn(
        (hold(proj_up[0]), proj_up[1], *proj_down), 2, 2, heads
    )
    (sum_out,) = receive_attn((*out_up, *out_down), 0, 1, heads)
    return (
        output,
        grad_tokens,
        gains[0],
        gains[1],
        sum_query,
        sum_key,
        sum_value,
        sum_gate,
        sum_out,
        sum_mgate,
        sum_mup,
        sum_down,
    )


def solution(mesh):
    rows = P(("dp", "tensor"), None)
    block = P("dp", "tensor")
    return jax.shard_map(
        partial(per_device, mesh.shape["dp"], mesh.shape["tensor"]),
        mesh=mesh,
        in_specs=(rows, P("dp"), rows, P(), P()) + (block,) * 8,
        out_specs=(rows, rows, P(), P()) + (block,) * 8,
        check_vma=False,
    )
```

```python
from functools import partial

import jax
import jax.numpy as jnp
import numpy as np
from jax import lax
from jax.experimental import pallas as pl
from jax.experimental.pallas import tpu as pltpu
from jax.sharding import PartitionSpec as P

KEY = 256
VAL = 432
VPAD = 512
LANES = 128
EPS = 1e-05
HEAD_EPS = 1.0
F32 = jnp.float32
BF16 = jnp.bfloat16
VMEM_LIMIT = 48 * 1024 * 1024


def times_plain(left, right):
    return jnp.dot(left, right, preferred_element_type=F32)


def times_left(left, right):
    return lax.dot_general(left, right, (((0,), (0,)), ((), ())), preferred_element_type=F32)


def times_right(left, right):
    return lax.dot_general(left, right, (((1,), (1,)), ((), ())), preferred_element_type=F32)


def after(array, *earlier):
    return lax.optimization_barrier((array, *earlier))[0]


def params(**more):
    return pltpu.CompilerParams(vmem_limit_bytes=VMEM_LIMIT, **more)


def cost(flops, moved):
    return pl.CostEstimate(flops=flops // 64, bytes_accessed=moved // 64, transcendentals=0)


def norm_parts(features):
    centred = features - jnp.mean(features, -1, keepdims=True)
    inverse = lax.rsqrt(jnp.mean(centred * centred, -1, keepdims=True) + EPS)
    return centred * inverse, inverse


def norm_back(normed, inverse, grad, gain):
    scaled = grad * gain
    return inverse * (
        scaled
        - jnp.mean(scaled, -1, keepdims=True)
        - normed * jnp.mean(scaled * normed, -1, keepdims=True)
    )


def decay_rows(log_decay, rows, width):
    query = lax.broadcasted_iota(jnp.int32, (rows, width), 0) + (width - rows)
    key = lax.broadcasted_iota(jnp.int32, (rows, width), 1)
    spacing = query - key
    factor = jnp.exp(log_decay * jnp.maximum(spacing, 0).astype(F32))
    return jnp.where(spacing >= 0, factor, 0.0)


def retain_kernel(slots, rows, place_ref, decay_ref, *refs):
    ins, (cos_ref, sin_ref), outs = refs[: 4 * slots], refs[4 * slots : 4 * slots + 2], refs[4 * slots + 2 :]
    query_ref, key_ref, value_ref, normed_ref, scale_ref, mixed_ref, factor_ref, kept_ref = outs
    head = pl.program_id(0)
    place = place_ref[0]
    seq = slots * rows
    half = KEY // 2
    for slot in range(slots):
        start = pl.multiple_of((slot ^ place) * rows, rows)
        cosines, sines = cos_ref[pl.ds(start, rows), :], sin_ref[pl.ds(start, rows), :]
        for source, target, scale in ((ins[slot], query_ref, 1.0), (ins[slots + slot], key_ref, KEY**-0.5)):
            low = source[:, :half].astype(F32)
            high = source[:, half:].astype(F32)
            target[pl.ds(start, rows), :half] = ((low * cosines - high * sines) * scale).astype(BF16)
            target[pl.ds(start, rows), half:] = ((high * cosines + low * sines) * scale).astype(BF16)
        value_ref[pl.ds(start, rows), :] = ins[2 * slots + slot][...]
    factor_ref[...] = decay_rows(decay_ref[head], rows, seq)
    for block in range(slots):
        width = (block + 1) * rows
        scores = times_right(query_ref[block * rows : width, :], key_ref[:width, :])
        weights = (scores * factor_ref[:, seq - width :]).astype(BF16)
        kept_ref[block * rows : width, :] = times_plain(weights, value_ref[:width, :])
    inside = lax.broadcasted_iota(jnp.int32, (rows, VPAD), 1) < VAL
    for slot in range(slots):
        start = pl.multiple_of((slot ^ place) * rows, rows)
        kept = kept_ref[pl.ds(start, rows), :]
        mean = jnp.sum(kept, -1, keepdims=True) / VAL
        centred = jnp.where(inside, kept - mean, 0.0)
        inverse = lax.rsqrt(jnp.sum(centred * centred, -1, keepdims=True) / VAL + HEAD_EPS)
        normed = centred * inverse
        gate = ins[3 * slots + slot][...].astype(F32)
        mixed = gate * jax.nn.sigmoid(gate) * normed
        mixed_ref[slot * rows : (slot + 1) * rows, :] = mixed.astype(BF16)
        normed_ref[slot * rows : (slot + 1) * rows, :] = normed.astype(BF16)
        scale_ref[slot * rows : (slot + 1) * rows, :] = jnp.broadcast_to(inverse, (rows, 128))


def slot_specs(rows, heads):
    first_value = 2 * heads * KEY // VPAD
    return (
        pl.BlockSpec((rows, KEY), lambda h, *_: (0, h)),
        pl.BlockSpec((rows, KEY), lambda h, *_: (0, heads + h)),
        pl.BlockSpec((rows, VPAD), lambda h, *_: (0, first_value + h)),
        pl.BlockSpec((rows, VPAD), lambda h, *_: (0, first_value + heads + h)),
    )


def retain(projected, place, log_decay, cosines, sines, heads):
    slots, rows = len(projected), projected[0].shape[0]
    seq = slots * rows
    specs = slot_specs(rows, heads)
    table = pl.BlockSpec((seq, KEY // 2), lambda h, *_: (0, 0))

    def column(width):
        return pl.BlockSpec((seq, width), lambda h, *_: (0, h))

    return pl.pallas_call(
        partial(retain_kernel, slots, rows),
        out_shape=(
            jax.ShapeDtypeStruct((seq, heads * KEY), BF16),
            jax.ShapeDtypeStruct((seq, heads * KEY), BF16),
            jax.ShapeDtypeStruct((seq, heads * VPAD), BF16),
            jax.ShapeDtypeStruct((seq, heads * VPAD), BF16),
            jax.ShapeDtypeStruct((seq, heads * 128), F32),
            jax.ShapeDtypeStruct((seq, heads * VPAD), BF16),
        ),
        grid_spec=pltpu.PrefetchScalarGridSpec(
            num_scalar_prefetch=2,
            grid=(heads,),
            in_specs=[spec for spec in specs for _ in range(slots)] + [table, table],
            out_specs=[column(KEY), column(KEY), column(VPAD), column(VPAD), column(128), column(VPAD)],
            scratch_shapes=[pltpu.VMEM((rows, seq), F32), pltpu.VMEM((seq, VPAD), F32)],
        ),
        compiler_params=pltpu.CompilerParams(vmem_limit_bytes=VMEM_LIMIT),
        cost_estimate=cost(heads * seq * seq * (KEY + VPAD), heads * seq * 9000),
    )(place, log_decay, *(projected * 4), cosines, sines)


def retain_back_kernel(slots, rows, heads, place_ref, decay_ref, *refs):
    grads, gates, rest = refs[:slots], refs[slots : 2 * slots], refs[2 * slots :]
    (normed_ref, scale_ref, query_ref, key_ref, value_ref, cos_ref, sin_ref, out_ref, factor_ref, ret_ref, key_sum, value_sum) = rest
    head = pl.program_id(0)
    place = place_ref[0]
    seq = slots * rows
    half = KEY // 2
    query_col = pl.multiple_of(head * KEY, KEY)
    key_col = pl.multiple_of((heads + head) * KEY, KEY)
    value_col = pl.multiple_of(2 * heads * KEY + head * VPAD, VPAD)
    gate_col = pl.multiple_of(2 * heads * KEY + (heads + head) * VPAD, VPAD)
    inside = lax.broadcasted_iota(jnp.int32, (rows, VPAD), 1) < VAL
    for slot in range(slots):
        start = pl.multiple_of((slot ^ place) * rows, rows)
        span = slice(slot * rows, (slot + 1) * rows)
        grad, gate = grads[slot][...].astype(F32), gates[slot][...].astype(F32)
        normed, inverse = normed_ref[span, :].astype(F32), scale_ref[span, :1]
        sig = jax.nn.sigmoid(gate)
        out_ref[span, pl.ds(gate_col, VPAD)] = (grad * normed * sig * (1.0 + gate * (1.0 - sig))).astype(BF16)
        grad_normed = grad * gate * sig
        mean = jnp.sum(grad_normed, -1, keepdims=True) / VAL
        along = jnp.sum(grad_normed * normed, -1, keepdims=True) / VAL
        grad_ret = inverse * (grad_normed - mean - normed * along)
        ret_ref[pl.ds(start, rows), :] = jnp.where(inside, grad_ret, 0.0).astype(BF16)
    factor_ref[...] = decay_rows(decay_ref[head], rows, seq)
    key_sum[...] = jnp.zeros_like(key_sum)
    value_sum[...] = jnp.zeros_like(value_sum)
    for block in range(slots):
        width = (block + 1) * rows
        span = slice(block * rows, width)
        query, ret, keys = query_ref[span, :], ret_ref[span, :], key_ref[:width, :]
        factor = factor_ref[:, seq - width :]
        weights = (times_right(query, keys) * factor).astype(BF16)
        grad_scores = (times_right(ret, value_ref[:width, :]) * factor).astype(BF16)
        value_sum[:width, :] += times_left(weights, ret)
        key_sum[:width, :] += times_left(grad_scores, query)
        grad_query = times_plain(grad_scores, keys)
        row = pl.multiple_of((block ^ place) * rows, rows)
        cosines, sines = cos_ref[span, :], sin_ref[span, :]
        low, high = grad_query[:, :half], grad_query[:, half:]
        out_ref[pl.ds(row, rows), pl.ds(query_col, half)] = (low * cosines + high * sines).astype(BF16)
        out_ref[pl.ds(row, rows), pl.ds(pl.multiple_of(query_col + half, half), half)] = (
            high * cosines - low * sines
        ).astype(BF16)
    for block in range(slots):
        span = slice(block * rows, (block + 1) * rows)
        row = pl.multiple_of((block ^ place) * rows, rows)
        cosines, sines = cos_ref[span, :], sin_ref[span, :]
        low, high = key_sum[span, :half] * KEY**-0.5, key_sum[span, half:] * KEY**-0.5
        out_ref[pl.ds(row, rows), pl.ds(key_col, half)] = (low * cosines + high * sines).astype(BF16)
        out_ref[pl.ds(row, rows), pl.ds(pl.multiple_of(key_col + half, half), half)] = (
            high * cosines - low * sines
        ).astype(BF16)
        out_ref[pl.ds(row, rows), pl.ds(value_col, VPAD)] = value_sum[span, :].astype(BF16)


def retain_back(grads, projected, normed, scale, query, key, value, place, log_decay, cosines, sines, heads):
    slots, rows = len(projected), projected[0].shape[0]
    seq = slots * rows
    columns = 2 * heads * (KEY + VPAD)
    table = pl.BlockSpec((seq, KEY // 2), lambda h, *_: (0, 0))

    def column(width):
        return pl.BlockSpec((seq, width), lambda h, *_: (0, h))

    return pl.pallas_call(
        partial(retain_back_kernel, slots, rows, heads),
        out_shape=jax.ShapeDtypeStruct((seq, columns), BF16),
        grid_spec=pltpu.PrefetchScalarGridSpec(
            num_scalar_prefetch=2,
            grid=(heads,),
            in_specs=[pl.BlockSpec((rows, VPAD), lambda h, *_: (0, h))] * slots
            + [slot_specs(rows, heads)[3]] * slots
            + [column(VPAD), column(128), column(KEY), column(KEY), column(VPAD), table, table],
            out_specs=pl.BlockSpec((seq, columns), lambda h, *_: (0, 0)),
            scratch_shapes=[
                pltpu.VMEM((rows, seq), F32),
                pltpu.VMEM((seq, VPAD), BF16),
                pltpu.VMEM((seq, KEY), F32),
                pltpu.VMEM((seq, VPAD), F32),
            ],
        ),
        compiler_params=pltpu.CompilerParams(vmem_limit_bytes=VMEM_LIMIT),
        cost_estimate=cost(heads * seq * seq * (3 * KEY + 2 * VPAD), heads * seq * 10000),
    )(place, log_decay, *grads, *projected, normed, scale, query, key, value, cosines, sines)


def rows_kernel(slots, pieces, *refs):
    lefts, weights, outs = refs[:slots], refs[slots : slots + pieces], refs[slots + pieces :]
    left = jnp.concatenate([ref[...] for ref in lefts], 0)
    result = times_plain(left, jnp.concatenate([ref[...] for ref in weights], 0)).astype(BF16)
    rows = lefts[0].shape[0]
    for slot in range(slots):
        outs[slot][...] = result[slot * rows : (slot + 1) * rows]


def rows_times(lefts, pieces, first, columns, tile=512):
    rows, width = lefts[0].shape
    return pl.pallas_call(
        partial(rows_kernel, len(lefts), len(pieces)),
        out_shape=[jax.ShapeDtypeStruct((rows, columns), BF16)] * len(lefts),
        grid=(columns // tile,),
        in_specs=[pl.BlockSpec((rows, width), lambda n: (0, 0))] * len(lefts)
        + [pl.BlockSpec((p.shape[0], tile), lambda n: (0, n + first // tile)) for p in pieces],
        out_specs=[pl.BlockSpec((rows, tile), lambda n: (0, n))] * len(lefts),
        compiler_params=params(),
        cost_estimate=cost(2 * len(lefts) * rows * width * columns, 2 * width * columns),
    )(*lefts, *pieces)


def rows_back_kernel(slots, pieces, weigh, *refs):
    lefts, weights, rest = refs[:slots], refs[slots : slots + pieces], refs[slots + pieces :]
    total = rest[-1]
    step = pl.program_id(0)
    left = jnp.concatenate([ref[...] for ref in lefts], 0)
    part = times_right(left, jnp.concatenate([ref[...] for ref in weights], 0))

    @pl.when(step == 0)
    def _():
        total[...] = part

    @pl.when(step > 0)
    def _():
        total[...] += part

    @pl.when(step == pl.num_programs(0) - 1)
    def _():
        rows = lefts[0].shape[0]
        for slot in range(slots):
            rest[weigh * slots + slot][...] = total[slot * rows : (slot + 1) * rows, :].astype(BF16)
        if weigh:
            other = jnp.concatenate([ref[...] for ref in rest[:slots]], 0).astype(F32)
            along = jnp.sum(total[...] * other, 0, keepdims=True)
            rest[2 * slots][...] = jnp.broadcast_to(along, (8, along.shape[1]))


def rows_back(left, slots, pieces, first=0, weigh=(), tile=512):
    rows = left.shape[0] // 4
    columns = left.shape[1]
    width = sum(p.shape[0] for p in pieces)
    whole = pl.BlockSpec((rows, width), lambda k: (0, 0))
    return pl.pallas_call(
        partial(rows_back_kernel, len(slots), len(pieces), 1 if weigh else 0),
        out_shape=[jax.ShapeDtypeStruct((rows, width), BF16)] * len(slots)
        + ([jax.ShapeDtypeStruct((8, width), F32)] if weigh else []),
        grid=(columns // tile,),
        in_specs=[pl.BlockSpec((rows, tile), partial(lambda s, k: (s, k), s)) for s in slots]
        + [pl.BlockSpec((p.shape[0], tile), lambda k: (0, k + first // tile)) for p in pieces]
        + [whole] * len(weigh),
        out_specs=[whole] * len(slots) + ([pl.BlockSpec((8, width), lambda k: (0, 0))] if weigh else []),
        scratch_shapes=[pltpu.VMEM((len(slots) * rows, width), F32)],
        compiler_params=params(),
        cost_estimate=cost(2 * len(slots) * rows * width * columns, 2 * width * columns),
    )(*([left] * len(slots)), *pieces, *weigh)


def turn(array):
    middle = array.shape[1] // 2
    return jnp.concatenate([array[:, middle:], array[:, :middle]], 1)


def mlp_kernel(pieces, units, own_ref, other_ref, own_grad_ref, other_grad_ref, *refs):
    sources, outs = refs[:pieces], refs[pieces : pieces + 8]
    gate_ref, up_ref, down_ref, semaphores = refs[pieces + 8 :]
    rows = own_ref.shape[0]
    copies = []
    for part, target in enumerate((gate_ref, up_ref, down_ref)):
        place = 0
        for index, source in enumerate(sources):
            height = source.shape[0]
            copy = pltpu.make_async_copy(
                source.at[:, pl.ds(part * units, units)],
                target.at[pl.ds(place, height), :],
                semaphores.at[part, index],
            )
            copy.start()
            copies.append(copy)
            place += height
    third = pieces
    left = jnp.concatenate([own_ref[...], turn(other_ref[...])], 0)
    grad = jnp.concatenate([own_grad_ref[...], turn(other_grad_ref[...])], 0)
    for copy in copies[:third]:
        copy.wait()
    gate = times_plain(left, gate_ref[...])
    for copy in copies[third : 2 * third]:
        copy.wait()
    up = times_plain(left, up_ref[...])
    for copy in copies[2 * third :]:
        copy.wait()
    grad_hidden = times_plain(grad, down_ref[...])
    below = 0.5 + 0.5 * lax.erf(gate * (0.5**0.5))
    density = jnp.exp(-0.5 * gate * gate) * 0.3989422804014327
    smooth = gate * below
    hidden = (smooth * up).astype(BF16)
    grad_gate = (grad_hidden * up * (below + gate * density)).astype(BF16)
    grad_up = (grad_hidden * smooth).astype(BF16)
    for slot in range(2):
        span = slice(slot * rows, (slot + 1) * rows)
        outs[slot][...] = hidden[span]
        outs[2 + slot][...] = grad_gate[span]
        outs[4 + slot][...] = grad_up[span]
    back = times_right(grad_gate, gate_ref[...]) + times_right(grad_up, up_ref[...])
    outs[6][...] = back[:rows].astype(BF16)
    outs[7][...] = turn(back[rows:]).astype(BF16)


def mlp(own, other, own_grad, other_grad, pieces):
    rows, width = own.shape
    units = pieces[0].shape[1] // 3
    narrow = pl.BlockSpec((rows, units), lambda i: (0, 0))
    wide = pl.BlockSpec((rows, width), lambda i: (0, 0))
    small, large = jax.ShapeDtypeStruct((rows, units), BF16), jax.ShapeDtypeStruct((rows, width), BF16)
    return pl.pallas_call(
        partial(mlp_kernel, len(pieces), units),
        out_shape=[small] * 6 + [large] * 2,
        grid=(1,),
        in_specs=[wide] * 4 + [pl.BlockSpec(memory_space=pl.ANY)] * len(pieces),
        out_specs=[narrow] * 6 + [wide] * 2,
        scratch_shapes=[pltpu.VMEM((width, units), BF16)] * 3 + [pltpu.SemaphoreType.DMA((3, len(pieces)))],
        compiler_params=params(),
        cost_estimate=cost(2 * 2 * rows * width * units * 5, 6 * width * units),
    )(own, other, own_grad, other_grad, *pieces)


def down_kernel(pieces, *refs):
    lefts, weights, outs = refs[:4], refs[4 : 4 + pieces], refs[4 + pieces :]
    rows = lefts[0].shape[0]
    weight = jnp.concatenate([ref[...] for ref in weights], 0)
    for core in range(2):
        left = jnp.concatenate([lefts[2 * core][...], lefts[2 * core + 1][...]], 0)
        result = times_right(left, weight)
        outs[core][...] = (turn(result) if core else result).astype(BF16)


def mlp_down(hidden, pieces):
    rows, units = hidden[0].shape
    width = sum(p.shape[0] for p in pieces)
    whole = pl.BlockSpec((rows, units), lambda n: (0, 0))
    out = pl.BlockSpec((2 * rows, width), lambda n: (0, 0))
    return pl.pallas_call(
        partial(down_kernel, len(pieces)),
        out_shape=[jax.ShapeDtypeStruct((2 * rows, width), BF16)] * 2,
        grid=(1,),
        in_specs=[whole] * 4 + [pl.BlockSpec((p.shape[0], units), lambda n: (0, 2)) for p in pieces],
        out_specs=[out] * 2,
        compiler_params=params(),
        cost_estimate=cost(8 * rows * width * units, 2 * width * units),
    )(*hidden, *pieces)


def mlp_grad_kernel(*refs):
    lefts, grads, rights, outs = refs[:4], refs[4:8], refs[8:20], refs[20:]
    left = jnp.concatenate([ref[...] for ref in lefts], 0)
    grad = jnp.concatenate([ref[...] for ref in grads], 0)
    parts = []
    for index, rows in enumerate((left, left, grad)):
        right = jnp.concatenate([ref[...] for ref in rights[4 * index : 4 * index + 4]], 0)
        parts.append(times_left(rows, right).astype(BF16))
    result = jnp.concatenate(parts, 1)
    for part in range(2):

        @pl.when(pl.program_id(0) == part)
        def _():
            outs[part][...] = result


def mlp_grads(end, core, lefts, grads, grad_gate, grad_up, hidden):
    rows, width = lefts[0].shape
    units = hidden[0].shape[1]
    tile = width // 8

    def column(other, step):
        return (0, (core ^ other) * 4 + step * 2 + end)

    narrow = [pl.BlockSpec((rows, tile), partial(column, other)) for other in (0, 0, 1, 1)]
    whole = pl.BlockSpec((rows, units), lambda i: (0, 0))
    return pl.pallas_call(
        mlp_grad_kernel,
        out_shape=[jax.ShapeDtypeStruct((tile, 3 * units), BF16)] * 2,
        grid=(2,),
        in_specs=narrow * 2 + [whole] * 12,
        out_specs=[pl.BlockSpec((tile, 3 * units), lambda i: (0, 0))] * 2,
        compiler_params=params(),
        cost_estimate=cost(2 * rows * width * units * 3, 2 * width * units),
    )(*lefts, *grads, *grad_gate, *grad_up, *hidden)


def attn_grad_kernel(*refs):
    left = jnp.concatenate([ref[...] for ref in refs[:4]], 0)
    refs[5][...] = times_left(left, refs[4][...]).astype(BF16)


def attn_grad_add_kernel(*refs):
    left = jnp.concatenate([ref[...] for ref in refs[:4]], 0)
    result = (times_left(left, refs[4][...]) + refs[5][...].astype(F32)).astype(BF16)
    for part in range(2):

        @pl.when(pl.program_id(0) == part)
        def _():
            refs[6 + part][...] = result


def attn_grads(end, lefts, right, other=None):
    rows, width = lefts[0].shape
    columns = right.shape[1]
    tile = width // 8
    core = 1 if other is None else 0
    narrow = pl.BlockSpec((rows, tile), lambda i: (0, core * 4 + 2 * i + end))
    block = pl.BlockSpec((tile, columns), lambda i: (i, 0))
    whole = pl.BlockSpec((tile, columns), lambda i: (0, 0))
    return pl.pallas_call(
        attn_grad_kernel if core else attn_grad_add_kernel,
        out_shape=jax.ShapeDtypeStruct((2 * tile, columns), BF16)
        if core
        else [jax.ShapeDtypeStruct((tile, columns), BF16)] * 2,
        grid=(2,),
        in_specs=[narrow] * 4 + [pl.BlockSpec(right.shape, lambda i: (0, 0))] + ([] if core else [block]),
        out_specs=block if core else [whole] * 2,
        compiler_params=params(),
        cost_estimate=cost(2 * rows * width * columns, width * columns),
    )(*lefts, right, *([] if core else [other]))


def own_order_kernel(blocks, sizes, mine_ref, *refs):
    (shard_rows, half_rows), count = sizes, len(refs) // 2
    for index, (mask, part) in enumerate(blocks):
        start = pl.multiple_of((mine_ref[0] ^ mask) * shard_rows + part * half_rows, half_rows)
        for source, target in zip(refs[:count], refs[count:]):
            target[:, index * half_rows : (index + 1) * half_rows] = source[:, pl.ds(start, half_rows)]


def global_order_kernel(blocks, sizes, mine_ref, source, target):
    shard_rows, half_rows = sizes
    for index, (mask, part) in enumerate(blocks):
        start = pl.multiple_of((mine_ref[0] ^ mask) * shard_rows + part * half_rows, half_rows)
        target[:, pl.ds(start, half_rows)] = source[:, index * half_rows : (index + 1) * half_rows]


def reorder(kernel, blocks, sizes, mine, arrays):
    specs = [pl.BlockSpec(a.shape, lambda i, *_: (0, 0)) for a in arrays]
    return pl.pallas_call(
        partial(kernel, blocks, sizes),
        out_shape=[jax.ShapeDtypeStruct(a.shape, a.dtype) for a in arrays],
        grid_spec=pltpu.PrefetchScalarGridSpec(num_scalar_prefetch=1, grid=(1,), in_specs=specs, out_specs=specs),
        compiler_params=params(),
    )(mine, *arrays)


def middle_back_kernel(near, come, middle, grad_final, gain, low, full, gain_sum):
    grad = near[...] + come[...].astype(F32)
    normed, inverse = norm_parts(middle[...])
    total = grad_final[...].astype(F32) + norm_back(normed, inverse, grad, gain[...])
    low[...] = total.astype(BF16)
    full[...] = total

    @pl.when(pl.program_id(0) == 0)
    def _():
        gain_sum[...] = jnp.zeros_like(gain_sum)

    gain_sum[...] += jnp.sum(grad * normed, 0, keepdims=True)


def middle_back(near, come, middle, grad_final, gain):
    rows, width = near.shape
    tile = 64
    block = pl.BlockSpec((tile, width), lambda i: (i, 0))
    vector = pl.BlockSpec((1, width), lambda i: (0, 0))
    return pl.pallas_call(
        middle_back_kernel,
        out_shape=[
            jax.ShapeDtypeStruct((rows, width), BF16),
            jax.ShapeDtypeStruct((rows, width), F32),
            jax.ShapeDtypeStruct((1, width), F32),
        ],
        grid=(rows // tile,),
        in_specs=[block] * 4 + [vector],
        out_specs=[block, block, vector],
        compiler_params=params(),
        cost_estimate=cost(0, rows * width * 18),
    )(near, come, middle, grad_final, gain)


def widen(array, height):
    return jnp.concatenate([array, jnp.zeros((height - array.shape[0], array.shape[1]), array.dtype)], 0)


def send_attn_kernel(heads, *refs):
    sources, targets = refs[:5], refs[5:]
    half = targets[0].shape[0]
    spans = [slice(part * half, (part + 1) * half) for part in range(2)]
    for index, source in enumerate(sources):
        if index < 2:
            for span, target in zip(spans, targets):
                target[:, index * heads * KEY : (index + 1) * heads * KEY] = source[span, :].astype(BF16)
        else:
            for head in range(heads):
                column = 2 * heads * KEY + ((index - 2) * heads + head) * VPAD
                block = widen(source[head * VAL : (head + 1) * VAL, :], VPAD).T.astype(BF16)
                for span, target in zip(spans, targets):
                    target[:, column : column + VPAD] = block[span, :]


def send_attn(weights, heads):
    half = weights[0].shape[0] // 2
    columns = heads * (2 * KEY + 3 * VPAD)
    arrays = [*weights[:2], *(w.T for w in weights[2:])]
    return pl.pallas_call(
        partial(send_attn_kernel, heads),
        out_shape=[jax.ShapeDtypeStruct((half, columns), BF16)] * 2,
        grid=(1,),
        in_specs=[pl.BlockSpec(w.shape, lambda i: (0, 0)) for w in arrays],
        out_specs=[pl.BlockSpec((half, columns), lambda i: (0, 0))] * 2,
        compiler_params=params(),
        cost_estimate=cost(0, half * columns * 12),
    )(*arrays)


def send_mlp_kernel(padded, *refs):
    target = refs[-1]
    for index, source in enumerate(refs[:-1]):
        target[:, index * padded : (index + 1) * padded] = widen(source[...], padded).T.astype(BF16)


def send_mlp(weights, padded):
    rows, units = weights[0].shape
    return pl.pallas_call(
        partial(send_mlp_kernel, padded),
        out_shape=jax.ShapeDtypeStruct((rows, len(weights) * padded), BF16),
        grid=(1,),
        in_specs=[pl.BlockSpec((units, rows), lambda i: (0, 0))] * len(weights),
        out_specs=pl.BlockSpec((rows, len(weights) * padded), lambda i: (0, 0)),
        compiler_params=params(),
        cost_estimate=cost(0, rows * padded * 18),
    )(*(w.T for w in weights))


def receive_kernel(narrow, heads, *refs):
    targets = refs[4:]
    total = jnp.concatenate(
        [refs[2 * part][...].astype(F32) + refs[2 * part + 1][...].astype(F32) for part in range(2)], 0
    )
    column = 0
    for index, target in enumerate(targets):
        if index < narrow:
            target[...] = total[:, column : column + heads * KEY]
            column += heads * KEY
        else:
            for head in range(heads):
                target[head * VAL : (head + 1) * VAL, :] = total[:, column : column + VPAD].T[:VAL]
                column += VPAD


def receive_attn(parts, narrow, wide, heads):
    rows = 2 * parts[0].shape[0]
    shapes = [(rows, heads * KEY)] * narrow + [(heads * VAL, rows)] * wide
    found = pl.pallas_call(
        partial(receive_kernel, narrow, heads),
        out_shape=[jax.ShapeDtypeStruct(s, F32) for s in shapes],
        grid=(1,),
        in_specs=[pl.BlockSpec(p.shape, lambda i: (0, 0)) for p in parts],
        out_specs=[pl.BlockSpec(s, lambda i: (0, 0)) for s in shapes],
        compiler_params=params(),
        cost_estimate=cost(0, rows * sum(s[0] for s in shapes) * 4),
    )(*parts)
    return [*found[:narrow], *(f.T for f in found[narrow:])]


def receive_mlp_kernel(padded, odd_ref, kept, turned, core, *targets):
    first = jnp.where(odd_ref[0] == 1, turned[...], kept[...]).astype(F32)
    total = first + core[...].astype(F32)
    for index, target in enumerate(targets):
        target[...] = total[:, index * padded : (index + 1) * padded].T[: target.shape[0]]


def receive_mlp(odd, kept, turned, core, units):
    rows, columns = kept.shape
    whole = pl.BlockSpec((rows, columns), lambda i, *_: (0, 0))
    found = pl.pallas_call(
        partial(receive_mlp_kernel, columns // 3),
        out_shape=[jax.ShapeDtypeStruct((units, rows), F32)] * 3,
        grid_spec=pltpu.PrefetchScalarGridSpec(
            num_scalar_prefetch=1,
            grid=(1,),
            in_specs=[whole] * 3,
            out_specs=[pl.BlockSpec((units, rows), lambda i, *_: (0, 0))] * 3,
        ),
        compiler_params=params(),
        cost_estimate=cost(0, rows * columns * 10),
    )(odd, kept, turned, core)
    return [f.T for f in found]


def per_device(
    dp_size,
    tensor_size,
    tokens,
    lengths,
    cotangent,
    gain_one,
    gain_two,
    w_query,
    w_key,
    w_value,
    w_gate,
    w_out,
    w_mgate,
    w_mup,
    w_down,
):
    rows, width = tokens.shape
    seq = rows * tensor_size
    heads = w_query.shape[1] // KEY
    units = w_mgate.shape[1]
    shard_rows = w_query.shape[0]
    half_rows = shard_rows // 2
    bits = dp_size.bit_length() - 1
    mine, place = lax.axis_index("dp"), lax.axis_index("tensor")
    inner = (place == 1) | (place == 2)
    odd = (mine & 1) == 1
    up_bits = list(range(1, bits))
    down_bits = up_bits[::-1]

    def add(*arrays):
        return sum(array.astype(F32) for array in arrays)

    def swap_dp(array, mask):
        return lax.ppermute(array, "dp", [(i, i ^ mask) for i in range(dp_size)])

    def move_tensor(array, pairs):
        return lax.ppermute(array, "tensor", pairs)

    def swap_tensor(array, mask):
        return move_tensor(array, [(i, i ^ mask) for i in range(tensor_size)])

    across = [(1, 2), (2, 1)]
    outward = [(1, 0), (2, 3)]
    inward = [(0, 1), (3, 2)]

    def pair(dp_index, tensor_index):
        return dp_index * tensor_size + tensor_index

    top = tensor_size - 1
    to_even = [(pair(m | 1, t), pair(m, t)) for m in range(0, dp_size, 2) for t in range(tensor_size)]
    to_odd = [(pair(m, t), pair(m | 1, t ^ top)) for m in range(0, dp_size, 2) for t in range(tensor_size)]
    odd_turn = [(pair(m | 1, t), pair(m | 1, t ^ top)) for m in range(0, dp_size, 2) for t in range(tensor_size)]
    both = ("dp", "tensor")

    def hold(array):
        return after(array, token[0])

    def close(*results):
        token[0] = after(token[0], *results)

    def line_out(slots, beside, middle):
        return move_tensor(hold(beside), across), move_tensor(hold(middle), outward)

    def line_all(own, beside, middle, far_inner, far_ends, last):
        return own, beside, jnp.where(inner, far_inner, far_ends), jnp.where(inner, middle, last)

    def first_level(piece, order):
        return swap_dp(piece, 1 << order[0])

    def second_level(piece, order):
        return swap_dp(hold(piece), 1 << order[1])

    def further(pieces, order):
        for bit in order[2:]:
            pieces = pieces + [swap_dp(p, 1 << bit) for p in pieces]
        return pieces

    def to_core(piece):
        return swap_dp(hold(piece), 1)

    def sum_start(high, order):
        return swap_dp(hold(high), 1 << order[-1])

    def sum_split(low, come):
        middle = low.shape[0] // 2
        return [add(low[span], come[span]).astype(BF16) for span in (slice(0, middle), slice(middle, 2 * middle))]

    def sum_end(low, high, order):
        for bit in order[-2:0:-1]:
            low, high = sum_split(low, swap_dp(hold(high), 1 << bit))
        return low, swap_dp(hold(high), 1 << order[0])

    blocks = [
        (chip << 1 | core, part)
        for core in range(2)
        for part, order in ((0, up_bits), (1, down_bits))
        for chip in [sum((i >> j & 1) << (b - 1) for j, b in enumerate(order)) for i in range(dp_size // 2)]
    ]

    sizes = (shard_rows, half_rows)
    aligned = half_rows % LANES == 0
    mine_arg = mine.astype(jnp.int32).reshape(1)

    def to_relative(*arrays):
        if aligned:
            return reorder(own_order_kernel, blocks, sizes, mine_arg, arrays)
        return [
            jnp.concatenate(
                [
                    lax.dynamic_slice_in_dim(a, (mine ^ mask) * shard_rows + part * half_rows, half_rows, -1)
                    for mask, part in blocks
                ],
                -1,
            )
            for a in arrays
        ]

    def to_global(array):
        if aligned:
            return reorder(global_order_kernel, blocks, sizes, mine_arg, [array])[0]
        found = []
        for shard in range(dp_size):
            mask = mine ^ shard
            for part, order in ((0, up_bits), (1, down_bits)):
                chip = sum((mask >> b & 1) << j for j, b in enumerate(order))
                index = (mask & 1) * dp_size + part * (dp_size // 2) + chip
                found.append(lax.dynamic_slice_in_dim(array, index * half_rows, half_rows, -1))
        return jnp.concatenate(found, -1)

    first_row = place * rows
    valid = (first_row + jnp.arange(rows, dtype=jnp.int32) < lengths[0])[:, None]
    head_ids = (place * heads + jnp.arange(heads, dtype=jnp.int32)).astype(F32)
    log_decay = jnp.log(1.0 - jnp.exp2(-5.0 - head_ids))
    place_arg = place.astype(jnp.int32).reshape(1)
    freqs = np.float32(10000.0) ** (-np.arange(KEY // 2, dtype=np.float32) / np.float32(KEY // 2))
    angles = np.arange(seq, dtype=np.float32)[:, None] * freqs[None, :]
    cosines, sines = jnp.asarray(np.cos(angles)), jnp.asarray(np.sin(angles))

    token = [mine_arg]
    proj_columns, out_columns = 2 * heads * (KEY + VPAD), heads * VPAD
    padded = -(-units // LANES) * LANES

    sent_up, sent_down = send_attn((w_query, w_key, w_value, w_gate, w_out), heads)
    features_low, gain_first = to_relative(tokens, gain_one[None])
    features = features_low.astype(F32)
    normed_one, inverse_one = norm_parts(features)
    first_own = (normed_one * gain_first).astype(BF16)
    close(sent_up, sent_down, first_own)

    up_one = first_level(hold(sent_up), up_bits)
    down_one = first_level(hold(sent_down), down_bits)
    first_beside = swap_tensor(hold(first_own), 1)
    first_middle = move_tensor(hold(first_own), across)
    local_two = send_mlp((w_mgate, w_mup, hold(w_down)), padded)
    cotangent_low, gain_second = to_relative(hold(cotangent), gain_two[None])
    grad_own = jnp.where(valid, cotangent_low, 0.0)
    grad_final = grad_own.astype(F32)
    core_one = [to_core(sent_up)]
    close(up_one, down_one, first_beside, first_middle, local_two, grad_own, core_one[0])

    up_two, down_two = second_level(sent_up, up_bits), second_level(sent_down, down_bits)
    first_far = line_out(None, first_beside, first_middle)
    core_one.append(to_core(sent_down))
    close(up_two, down_two, *first_far, *core_one)

    up_three, down_three = second_level(up_one, up_bits), second_level(down_one, down_bits)
    first_last = move_tensor(hold(first_far[0]), outward)
    core_two = [to_core(p) for p in (up_one, down_one)]
    close(up_three, down_three, first_last, *core_two)

    up_all = further([sent_up, up_one, up_two, up_three], up_bits)
    down_all = further([sent_down, down_one, down_two, down_three], down_bits)
    up_core = [core_one[0], core_two[0]] + [to_core(p) for p in up_all[2:]]
    down_core = [core_one[1], core_two[1]] + [to_core(p) for p in down_all[2:]]
    turned = lax.ppermute(hold(local_two), both, odd_turn)
    grad_beside = swap_tensor(hold(grad_own), 1)
    close(*up_core, *down_core)
    attn_low = up_all + down_all + up_core + down_core
    first_slots = line_all(first_own, first_beside, first_middle, *first_far, first_last)

    spans = slice(0, half_rows), slice(half_rows, shard_rows)
    orders = up_bits, down_bits

    def level_one(halves):
        return [first_level(half, order) for half, order in zip(halves, orders)]

    def level_two(halves, come):
        found = []
        for half, other, order in zip(halves, come, orders):
            both_pieces = jnp.concatenate([half, hold(other)], 0)
            found += further_two([both_pieces, swap_dp(both_pieces, 1 << order[1])], order)
        return found

    def further_two(pieces, order):
        for bit in order[2:]:
            pieces = pieces + [swap_dp(p, 1 << bit) for p in pieces]
        return pieces

    grad_core = to_core(grad_own)
    projected = rows_times([hold(first_slots[0]), *first_slots[1:]], attn_low, 0, proj_columns)
    close(turned, projected[0], grad_core)

    mlp_zero = [jnp.where(odd, hold(turned)[span], local_two[span]) for span in spans]
    zero_come = level_one(mlp_zero)
    mlp_one = [lax.ppermute(hold(local_two)[spans[0]], both, to_even + to_odd)]
    query, key, value, normed_head, scale_head, mixed = retain(
        [hold(projected[0]), *projected[1:]], place_arg, log_decay, cosines, sines, heads
    )
    (mixed_third,) = rows_back(mixed, (3,), attn_low, proj_columns)
    close(*zero_come, mlp_one[0], grad_beside, mixed_third)

    from_ends = move_tensor(hold(mixed_third), inward)
    mlp_one.append(lax.ppermute(hold(local_two)[spans[1]], both, to_even + to_odd))
    zero_pieces = level_two(mlp_zero, zero_come)
    mixed_second, mixed_first, mixed_own = rows_back(hold(mixed), (2, 1, 0), attn_low, proj_columns)
    mixed_partial = add(mixed_second, from_ends).astype(BF16)
    grad_rows = [grad_own, grad_beside, grad_core, to_core(grad_beside)]
    close(mlp_one[1], *zero_pieces, mixed_partial, grad_rows[3])

    from_inner = move_tensor(hold(mixed_partial), across)
    from_ends = move_tensor(hold(mixed_second), inward)
    one_come = level_one([hold(half) for half in mlp_one])
    close(*one_come, from_inner, from_ends)

    from_beside = swap_tensor(add(mixed_first, hold(from_inner)).astype(BF16), 1)
    from_middle = move_tensor(add(mixed_third, hold(from_ends)).astype(BF16), across)
    mlp_pieces = zero_pieces + level_two(mlp_one, one_come)
    middle = features + add(mixed_own, from_beside, from_middle)
    normed_two, inverse_two = norm_parts(middle)
    second_own = (normed_two * gain_second).astype(BF16)
    close(*mlp_pieces, second_own)

    second_beside = swap_tensor(hold(second_own), 1)
    second_core = to_core(second_own)
    first_part = mlp(hold(second_own), second_core, grad_rows[0], grad_rows[2], mlp_pieces)
    near_core = swap_dp(first_part[7], 1)
    close(second_beside, near_core)

    second_far = to_core(second_beside)
    second_rows = [second_own, second_beside, second_core, second_far]
    second_part = mlp(hold(second_beside), second_far, grad_rows[1], grad_rows[3], mlp_pieces)
    far_core = swap_dp(second_part[7], 1)
    hidden, grad_gate, grad_up = (
        [first_part[2 * i], second_part[2 * i], first_part[2 * i + 1], second_part[2 * i + 1]] for i in range(3)
    )

    far = add(second_part[6], far_core).astype(BF16)
    near = add(first_part[6], near_core)
    close(far, near)

    def mlp_grad(end, core):
        return mlp_grads(end, core, [hold(second_rows[0]), *second_rows[1:]], grad_rows, grad_gate, grad_up, hidden)

    second_back = swap_tensor(hold(far), 1)
    high = [mlp_grad(1, 0), mlp_grad(1, 1)]
    down_own, down_other = mlp_down([hold(hidden[0]), *hidden[1:]], mlp_pieces)
    close(second_back, *high[0], *high[1], down_own)

    attn_own, grad_middle, grad_gain_two = middle_back(near, hold(second_back), middle, grad_own, gain_second)
    attn_beside = swap_tensor(attn_own, 1)
    attn_middle = move_tensor(attn_own, across)
    come = [[sum_start(high[0][0], up_bits), sum_start(high[0][1], down_bits)]]
    low = [mlp_grad(0, 0), mlp_grad(0, 1)]
    close(attn_beside, attn_middle, *come[0], *low[0], *low[1])

    attn_far = line_out(None, attn_beside, attn_middle)
    come.append([sum_start(high[1][0], up_bits), sum_start(high[1][1], down_bits)])
    down_core = to_core(down_other)
    splits = [[sum_split(low[0][part], hold(come[0][part])) for part in range(2)]]
    close(*attn_far, *come[1], down_core, *splits[0][0], *splits[0][1])

    attn_last = move_tensor(hold(attn_far[0]), outward)
    splits.append([sum_split(low[1][part], hold(come[1][part])) for part in range(2)])

    def mlp_end(core):
        return [add(*sum_end(*splits[core][part], orders[part])).astype(BF16) for part in range(2)]

    mlp_total = [mlp_end(0)]
    attn_third = attn_far[0], attn_far[1]
    attn_second = jnp.where(inner, *attn_third)
    grad_mixed = rows_times([hold(attn_own), attn_beside, attn_second], attn_low, proj_columns, out_columns)
    down_sum = add(down_own, hold(down_core))
    down_sent = down_sum[rows:].astype(BF16)
    close(attn_last, *mlp_total[0], grad_mixed[0])
    attn_slots = attn_own, attn_beside, attn_second, jnp.where(inner, attn_middle, hold(attn_last))

    grad_turn = lax.ppermute(jnp.concatenate([hold(t) for t in mlp_total[0]], 0), both, [(b, a) for a, b in odd_turn])
    grad_mixed = grad_mixed + rows_times([attn_slots[3]], attn_low, proj_columns, out_columns)
    grad_proj = retain_back(
        grad_mixed, projected, normed_head, scale_head, query, key, value, place_arg, log_decay, cosines, sines, heads
    )
    back_third, gain_third = rows_back(grad_proj, (3,), attn_low, 0, first_slots[3:])
    mlp_total.append(mlp_end(1))
    close(grad_turn, back_third, *mlp_total[1])

    from_ends = move_tensor(hold(back_third), inward)
    to_owner = [(b, a) for a, b in to_even + to_odd]
    grad_core = [lax.ppermute(hold(mlp_total[1][0]), both, to_owner)]
    other_high = attn_grads(1, first_slots, hold(grad_proj))
    back_second, gain_second_part = rows_back(after(grad_proj, other_high), (2,), attn_low, 0, first_slots[2:3])
    other_low = attn_grads(0, first_slots, after(grad_proj, back_second))
    back_partial = add(back_second, from_ends).astype(BF16)
    close(back_partial, other_low, grad_core[0])

    from_inner = move_tensor(hold(back_partial), across)
    from_ends = move_tensor(hold(back_second), inward)
    core_high, core_low = to_core(other_high), to_core(other_low)
    out_other_high = attn_grads(1, attn_slots, hold(mixed))
    out_other_low = attn_grads(0, attn_slots, after(mixed, out_other_high))
    up_high, down_high = attn_grads(1, first_slots, after(grad_proj, out_other_low), core_high)
    proj_come = swap_dp(up_high, 1 << up_bits[-1]), swap_dp(down_high, 1 << down_bits[-1])
    back_own, back_first, gain_near = rows_back(after(grad_proj, up_high), (0, 1), attn_low, 0, first_slots[:2])
    close(from_inner, from_ends, back_own, core_low, out_other_low)

    from_beside = swap_tensor(add(back_first, hold(from_inner)).astype(BF16), 1)
    from_middle = move_tensor(add(back_third, hold(from_ends)).astype(BF16), across)
    out_core_high, out_core_low = to_core(out_other_high), to_core(out_other_low)
    up_low, down_low = attn_grads(0, first_slots, hold(grad_proj), core_low)
    out_up_high, out_down_high = attn_grads(1, attn_slots, after(mixed, up_low), out_core_high)
    out_up_low, out_down_low = attn_grads(0, attn_slots, after(mixed, out_up_high), out_core_low)
    gain_parts = gain_third[0] + gain_second_part[0] + hold(gain_near)[0]
    gains = to_global(jnp.stack([gain_parts / gain_first[0], grad_gain_two[0]]))
    gains = gains + swap_dp(gains, 1)
    close(from_beside, from_middle, *proj_come, gains, up_low, out_up_low)

    down_beside = swap_tensor(hold(down_sent), 1)
    proj_up = sum_end(*sum_split(up_low, hold(proj_come[0])), up_bits)
    proj_down = sum_end(*sum_split(down_low, hold(proj_come[1])), down_bits)
    out_come = sum_start(out_up_high, up_bits), sum_start(out_down_high, down_bits)
    grad_core.append(lax.ppermute(after(mlp_total[1][1], out_come[0]), both, to_owner))
    grad_first = add(back_own, hold(from_beside), from_middle)
    grad_tokens = grad_middle + norm_back(normed_one, inverse_one, grad_first, gain_first)
    grad_tokens = to_global(grad_tokens.astype(BF16))
    close(*proj_up, *proj_down, *out_come, grad_core[1], down_beside, grad_tokens)

    final = middle + down_sum[:rows] + hold(down_beside).astype(F32)
    output = to_global(jnp.where(valid, final, 0.0).astype(BF16))
    sum_mgate, sum_mup, sum_down = receive_mlp(
        (mine & 1).astype(jnp.int32).reshape(1),
        jnp.concatenate([hold(t) for t in mlp_total[0]], 0),
        grad_turn,
        jnp.concatenate(grad_core, 0),
        units,
    )
    out_up = sum_end(*sum_split(out_up_low, hold(out_come[0])), up_bits)
    out_down = sum_end(*sum_split(out_down_low, hold(out_come[1])), down_bits)
    gains = hold(gains)
    gains = gains + sum(swap_dp(gains, 2 * chip) for chip in range(1, dp_size // 2))
    gains = gains + sum(swap_tensor(gains, other) for other in range(1, tensor_size))
    sum_query, sum_key, sum_value, sum_gate = receive_attn(
        (hold(proj_up[0]), proj_up[1], *proj_down), 2, 2, heads
    )
    (sum_out,) = receive_attn((*out_up, *out_down), 0, 1, heads)
    return (
        output,
        grad_tokens,
        gains[0],
        gains[1],
        sum_query,
        sum_key,
        sum_value,
        sum_gate,
        sum_out,
        sum_mgate,
        sum_mup,
        sum_down,
    )


def solution(mesh):
    rows = P(("dp", "tensor"), None)
    block = P("dp", "tensor")
    return jax.shard_map(
        partial(per_device, mesh.shape["dp"], mesh.shape["tensor"]),
        mesh=mesh,
        in_specs=(rows, P("dp"), rows, P(), P()) + (block,) * 8,
        out_specs=(rows, rows, P(), P()) + (block,) * 8,
        check_vma=False,
    )
```

```python
from functools import partial

import jax
import jax.numpy as jnp
import numpy as np
from jax import lax
from jax.experimental import pallas as pl
from jax.experimental.pallas import tpu as pltpu
from jax.sharding import PartitionSpec as P

KEY = 256
VAL = 432
VPAD = 512
LANES = 128
EPS = 1e-05
HEAD_EPS = 1.0
F32 = jnp.float32
BF16 = jnp.bfloat16
VMEM_LIMIT = 48 * 1024 * 1024


def times_plain(left, right):
    return jnp.dot(left, right, preferred_element_type=F32)


def times_left(left, right):
    return lax.dot_general(left, right, (((0,), (0,)), ((), ())), preferred_element_type=F32)


def times_right(left, right):
    return lax.dot_general(left, right, (((1,), (1,)), ((), ())), preferred_element_type=F32)


def after(array, *earlier):
    return lax.optimization_barrier((array, *earlier))[0]


def params(**more):
    return pltpu.CompilerParams(vmem_limit_bytes=VMEM_LIMIT, **more)


def cost(flops, moved):
    return pl.CostEstimate(flops=flops // 64, bytes_accessed=moved // 64, transcendentals=0)


def norm_parts(features):
    centred = features - jnp.mean(features, -1, keepdims=True)
    inverse = lax.rsqrt(jnp.mean(centred * centred, -1, keepdims=True) + EPS)
    return centred * inverse, inverse


def norm_back(normed, inverse, grad, gain):
    scaled = grad * gain
    return inverse * (
        scaled
        - jnp.mean(scaled, -1, keepdims=True)
        - normed * jnp.mean(scaled * normed, -1, keepdims=True)
    )


def decay_rows(log_decay, rows, width):
    query = lax.broadcasted_iota(jnp.int32, (rows, width), 0) + (width - rows)
    key = lax.broadcasted_iota(jnp.int32, (rows, width), 1)
    spacing = query - key
    factor = jnp.exp(log_decay * jnp.maximum(spacing, 0).astype(F32))
    return jnp.where(spacing >= 0, factor, 0.0)


def retain_kernel(slots, rows, place_ref, decay_ref, *refs):
    ins, (cos_ref, sin_ref), outs = refs[: 4 * slots], refs[4 * slots : 4 * slots + 2], refs[4 * slots + 2 :]
    query_ref, key_ref, value_ref, normed_ref, scale_ref, mixed_ref, factor_ref, kept_ref = outs
    head = pl.program_id(0)
    place = place_ref[0]
    seq = slots * rows
    half = KEY // 2
    for slot in range(slots):
        start = pl.multiple_of((slot ^ place) * rows, rows)
        cosines, sines = cos_ref[pl.ds(start, rows), :], sin_ref[pl.ds(start, rows), :]
        for source, target, scale in ((ins[slot], query_ref, 1.0), (ins[slots + slot], key_ref, KEY**-0.5)):
            low = source[:, :half].astype(F32)
            high = source[:, half:].astype(F32)
            target[pl.ds(start, rows), :half] = ((low * cosines - high * sines) * scale).astype(BF16)
            target[pl.ds(start, rows), half:] = ((high * cosines + low * sines) * scale).astype(BF16)
        value_ref[pl.ds(start, rows), :] = ins[2 * slots + slot][...]
    factor_ref[...] = decay_rows(decay_ref[head], rows, seq)
    for block in range(slots):
        width = (block + 1) * rows
        scores = times_right(query_ref[block * rows : width, :], key_ref[:width, :])
        weights = (scores * factor_ref[:, seq - width :]).astype(BF16)
        kept_ref[block * rows : width, :] = times_plain(weights, value_ref[:width, :])
    inside = lax.broadcasted_iota(jnp.int32, (rows, VPAD), 1) < VAL
    for slot in range(slots):
        start = pl.multiple_of((slot ^ place) * rows, rows)
        kept = kept_ref[pl.ds(start, rows), :]
        mean = jnp.sum(kept, -1, keepdims=True) / VAL
        centred = jnp.where(inside, kept - mean, 0.0)
        inverse = lax.rsqrt(jnp.sum(centred * centred, -1, keepdims=True) / VAL + HEAD_EPS)
        normed = centred * inverse
        gate = ins[3 * slots + slot][...].astype(F32)
        mixed = gate * jax.nn.sigmoid(gate) * normed
        mixed_ref[slot * rows : (slot + 1) * rows, :] = mixed.astype(BF16)
        normed_ref[slot * rows : (slot + 1) * rows, :] = normed.astype(BF16)
        scale_ref[slot * rows : (slot + 1) * rows, :] = jnp.broadcast_to(inverse, (rows, 128))


def slot_specs(rows, heads):
    first_value = 2 * heads * KEY // VPAD
    return (
        pl.BlockSpec((rows, KEY), lambda h, *_: (0, h)),
        pl.BlockSpec((rows, KEY), lambda h, *_: (0, heads + h)),
        pl.BlockSpec((rows, VPAD), lambda h, *_: (0, first_value + h)),
        pl.BlockSpec((rows, VPAD), lambda h, *_: (0, first_value + heads + h)),
    )


def retain(projected, place, log_decay, cosines, sines, heads):
    slots, rows = len(projected), projected[0].shape[0]
    seq = slots * rows
    specs = slot_specs(rows, heads)
    table = pl.BlockSpec((seq, KEY // 2), lambda h, *_: (0, 0))

    def column(width):
        return pl.BlockSpec((seq, width), lambda h, *_: (0, h))

    return pl.pallas_call(
        partial(retain_kernel, slots, rows),
        out_shape=(
            jax.ShapeDtypeStruct((seq, heads * KEY), BF16),
            jax.ShapeDtypeStruct((seq, heads * KEY), BF16),
            jax.ShapeDtypeStruct((seq, heads * VPAD), BF16),
            jax.ShapeDtypeStruct((seq, heads * VPAD), BF16),
            jax.ShapeDtypeStruct((seq, heads * 128), F32),
            jax.ShapeDtypeStruct((seq, heads * VPAD), BF16),
        ),
        grid_spec=pltpu.PrefetchScalarGridSpec(
            num_scalar_prefetch=2,
            grid=(heads,),
            in_specs=[spec for spec in specs for _ in range(slots)] + [table, table],
            out_specs=[column(KEY), column(KEY), column(VPAD), column(VPAD), column(128), column(VPAD)],
            scratch_shapes=[pltpu.VMEM((rows, seq), F32), pltpu.VMEM((seq, VPAD), F32)],
        ),
        compiler_params=pltpu.CompilerParams(vmem_limit_bytes=VMEM_LIMIT),
        cost_estimate=cost(heads * seq * seq * (KEY + VPAD), heads * seq * 9000),
    )(place, log_decay, *(projected * 4), cosines, sines)


def retain_back_kernel(slots, rows, heads, place_ref, decay_ref, *refs):
    grads, gates, rest = refs[:slots], refs[slots : 2 * slots], refs[2 * slots :]
    (normed_ref, scale_ref, query_ref, key_ref, value_ref, cos_ref, sin_ref, out_ref, factor_ref, ret_ref, key_sum, value_sum) = rest
    head = pl.program_id(0)
    place = place_ref[0]
    seq = slots * rows
    half = KEY // 2
    query_col = pl.multiple_of(head * KEY, KEY)
    key_col = pl.multiple_of((heads + head) * KEY, KEY)
    value_col = pl.multiple_of(2 * heads * KEY + head * VPAD, VPAD)
    gate_col = pl.multiple_of(2 * heads * KEY + (heads + head) * VPAD, VPAD)
    inside = lax.broadcasted_iota(jnp.int32, (rows, VPAD), 1) < VAL
    for slot in range(slots):
        start = pl.multiple_of((slot ^ place) * rows, rows)
        span = slice(slot * rows, (slot + 1) * rows)
        grad, gate = grads[slot][...].astype(F32), gates[slot][...].astype(F32)
        normed, inverse = normed_ref[span, :].astype(F32), scale_ref[span, :1]
        sig = jax.nn.sigmoid(gate)
        out_ref[span, pl.ds(gate_col, VPAD)] = (grad * normed * sig * (1.0 + gate * (1.0 - sig))).astype(BF16)
        grad_normed = grad * gate * sig
        mean = jnp.sum(grad_normed, -1, keepdims=True) / VAL
        along = jnp.sum(grad_normed * normed, -1, keepdims=True) / VAL
        grad_ret = inverse * (grad_normed - mean - normed * along)
        ret_ref[pl.ds(start, rows), :] = jnp.where(inside, grad_ret, 0.0).astype(BF16)
    factor_ref[...] = decay_rows(decay_ref[head], rows, seq)
    key_sum[...] = jnp.zeros_like(key_sum)
    value_sum[...] = jnp.zeros_like(value_sum)
    for block in range(slots):
        width = (block + 1) * rows
        span = slice(block * rows, width)
        query, ret, keys = query_ref[span, :], ret_ref[span, :], key_ref[:width, :]
        factor = factor_ref[:, seq - width :]
        weights = (times_right(query, keys) * factor).astype(BF16)
        grad_scores = (times_right(ret, value_ref[:width, :]) * factor).astype(BF16)
        value_sum[:width, :] += times_left(weights, ret)
        key_sum[:width, :] += times_left(grad_scores, query)
        grad_query = times_plain(grad_scores, keys)
        row = pl.multiple_of((block ^ place) * rows, rows)
        cosines, sines = cos_ref[span, :], sin_ref[span, :]
        low, high = grad_query[:, :half], grad_query[:, half:]
        out_ref[pl.ds(row, rows), pl.ds(query_col, half)] = (low * cosines + high * sines).astype(BF16)
        out_ref[pl.ds(row, rows), pl.ds(pl.multiple_of(query_col + half, half), half)] = (
            high * cosines - low * sines
        ).astype(BF16)
    for block in range(slots):
        span = slice(block * rows, (block + 1) * rows)
        row = pl.multiple_of((block ^ place) * rows, rows)
        cosines, sines = cos_ref[span, :], sin_ref[span, :]
        low, high = key_sum[span, :half] * KEY**-0.5, key_sum[span, half:] * KEY**-0.5
        out_ref[pl.ds(row, rows), pl.ds(key_col, half)] = (low * cosines + high * sines).astype(BF16)
        out_ref[pl.ds(row, rows), pl.ds(pl.multiple_of(key_col + half, half), half)] = (
            high * cosines - low * sines
        ).astype(BF16)
        out_ref[pl.ds(row, rows), pl.ds(value_col, VPAD)] = value_sum[span, :].astype(BF16)


def retain_back(grads, projected, normed, scale, query, key, value, place, log_decay, cosines, sines, heads):
    slots, rows = len(projected), projected[0].shape[0]
    seq = slots * rows
    columns = 2 * heads * (KEY + VPAD)
    table = pl.BlockSpec((seq, KEY // 2), lambda h, *_: (0, 0))

    def column(width):
        return pl.BlockSpec((seq, width), lambda h, *_: (0, h))

    return pl.pallas_call(
        partial(retain_back_kernel, slots, rows, heads),
        out_shape=jax.ShapeDtypeStruct((seq, columns), BF16),
        grid_spec=pltpu.PrefetchScalarGridSpec(
            num_scalar_prefetch=2,
            grid=(heads,),
            in_specs=[pl.BlockSpec((rows, VPAD), lambda h, *_: (0, h))] * slots
            + [slot_specs(rows, heads)[3]] * slots
            + [column(VPAD), column(128), column(KEY), column(KEY), column(VPAD), table, table],
            out_specs=pl.BlockSpec((seq, columns), lambda h, *_: (0, 0)),
            scratch_shapes=[
                pltpu.VMEM((rows, seq), F32),
                pltpu.VMEM((seq, VPAD), BF16),
                pltpu.VMEM((seq, KEY), F32),
                pltpu.VMEM((seq, VPAD), F32),
            ],
        ),
        compiler_params=pltpu.CompilerParams(vmem_limit_bytes=VMEM_LIMIT),
        cost_estimate=cost(heads * seq * seq * (3 * KEY + 2 * VPAD), heads * seq * 10000),
    )(place, log_decay, *grads, *projected, normed, scale, query, key, value, cosines, sines)


def rows_kernel(slots, pieces, *refs):
    lefts, weights, outs = refs[:slots], refs[slots : slots + pieces], refs[slots + pieces :]
    left = jnp.concatenate([ref[...] for ref in lefts], 0)
    result = times_plain(left, jnp.concatenate([ref[...] for ref in weights], 0)).astype(BF16)
    rows = lefts[0].shape[0]
    for slot in range(slots):
        outs[slot][...] = result[slot * rows : (slot + 1) * rows]


def rows_times(lefts, pieces, first, columns, tile=512):
    rows, width = lefts[0].shape
    return pl.pallas_call(
        partial(rows_kernel, len(lefts), len(pieces)),
        out_shape=[jax.ShapeDtypeStruct((rows, columns), BF16)] * len(lefts),
        grid=(columns // tile,),
        in_specs=[pl.BlockSpec((rows, width), lambda n: (0, 0))] * len(lefts)
        + [pl.BlockSpec((p.shape[0], tile), lambda n: (0, n + first // tile)) for p in pieces],
        out_specs=[pl.BlockSpec((rows, tile), lambda n: (0, n))] * len(lefts),
        compiler_params=params(),
        cost_estimate=cost(2 * len(lefts) * rows * width * columns, 2 * width * columns),
    )(*lefts, *pieces)


def rows_back_kernel(slots, pieces, weigh, *refs):
    lefts, weights, rest = refs[:slots], refs[slots : slots + pieces], refs[slots + pieces :]
    total = rest[-1]
    step = pl.program_id(0)
    left = jnp.concatenate([ref[...] for ref in lefts], 0)
    part = times_right(left, jnp.concatenate([ref[...] for ref in weights], 0))

    @pl.when(step == 0)
    def _():
        total[...] = part

    @pl.when(step > 0)
    def _():
        total[...] += part

    @pl.when(step == pl.num_programs(0) - 1)
    def _():
        rows = lefts[0].shape[0]
        for slot in range(slots):
            rest[weigh * slots + slot][...] = total[slot * rows : (slot + 1) * rows, :].astype(BF16)
        if weigh:
            other = jnp.concatenate([ref[...] for ref in rest[:slots]], 0).astype(F32)
            along = jnp.sum(total[...] * other, 0, keepdims=True)
            rest[2 * slots][...] = jnp.broadcast_to(along, (8, along.shape[1]))


def rows_back(left, slots, pieces, first=0, weigh=(), tile=512):
    rows = left.shape[0] // 4
    columns = left.shape[1]
    width = sum(p.shape[0] for p in pieces)
    whole = pl.BlockSpec((rows, width), lambda k: (0, 0))
    return pl.pallas_call(
        partial(rows_back_kernel, len(slots), len(pieces), 1 if weigh else 0),
        out_shape=[jax.ShapeDtypeStruct((rows, width), BF16)] * len(slots)
        + ([jax.ShapeDtypeStruct((8, width), F32)] if weigh else []),
        grid=(columns // tile,),
        in_specs=[pl.BlockSpec((rows, tile), partial(lambda s, k: (s, k), s)) for s in slots]
        + [pl.BlockSpec((p.shape[0], tile), lambda k: (0, k + first // tile)) for p in pieces]
        + [whole] * len(weigh),
        out_specs=[whole] * len(slots) + ([pl.BlockSpec((8, width), lambda k: (0, 0))] if weigh else []),
        scratch_shapes=[pltpu.VMEM((len(slots) * rows, width), F32)],
        compiler_params=params(),
        cost_estimate=cost(2 * len(slots) * rows * width * columns, 2 * width * columns),
    )(*([left] * len(slots)), *pieces, *weigh)


def turn(array):
    middle = array.shape[1] // 2
    return jnp.concatenate([array[:, middle:], array[:, :middle]], 1)


def mlp_kernel(pieces, units, own_ref, other_ref, own_grad_ref, other_grad_ref, *refs):
    sources, outs, weights = refs[:pieces], refs[pieces : pieces + 8], refs[pieces + 8 : pieces + 11]
    semaphores = refs[pieces + 11]
    copies = []
    for part, target in enumerate(weights):
        place = 0
        for index, source in enumerate(sources):
            height = source.shape[0]
            copy = pltpu.make_async_copy(
                source.at[:, pl.ds(part * units, units)],
                target.at[pl.ds(place, height), :],
                semaphores.at[part, index],
            )
            copy.start()
            copies.append(copy)
            place += height

    def ready(part):
        for copy in copies[part * pieces : (part + 1) * pieces]:
            copy.wait()

    mlp_body(ready, own_ref, other_ref, own_grad_ref, other_grad_ref, weights, outs)


def mlp_again_kernel(own_ref, other_ref, own_grad_ref, other_grad_ref, *refs):
    mlp_body(lambda part: None, own_ref, other_ref, own_grad_ref, other_grad_ref, refs[:3], refs[3:])


def mlp_body(ready, own_ref, other_ref, own_grad_ref, other_grad_ref, weights, outs):
    gate_ref, up_ref, down_ref = weights
    rows = own_ref.shape[0]
    left = jnp.concatenate([own_ref[...], turn(other_ref[...])], 0)
    grad = jnp.concatenate([own_grad_ref[...], turn(other_grad_ref[...])], 0)
    ready(0)
    gate = times_plain(left, gate_ref[...])
    ready(1)
    up = times_plain(left, up_ref[...])
    ready(2)
    grad_hidden = times_plain(grad, down_ref[...])
    below = 0.5 + 0.5 * lax.erf(gate * (0.5**0.5))
    density = jnp.exp(-0.5 * gate * gate) * 0.3989422804014327
    smooth = gate * below
    hidden = (smooth * up).astype(BF16)
    grad_gate = (grad_hidden * up * (below + gate * density)).astype(BF16)
    grad_up = (grad_hidden * smooth).astype(BF16)
    for slot in range(2):
        span = slice(slot * rows, (slot + 1) * rows)
        outs[slot][...] = hidden[span]
        outs[2 + slot][...] = grad_gate[span]
        outs[4 + slot][...] = grad_up[span]
    back = times_right(grad_gate, gate_ref[...]) + times_right(grad_up, up_ref[...])
    outs[6][...] = back[:rows].astype(BF16)
    outs[7][...] = turn(back[rows:]).astype(BF16)


def mlp(own, other, own_grad, other_grad, pieces, weights=None):
    rows, width = own.shape
    units = weights[0].shape[1] if weights else pieces[0].shape[1] // 3
    narrow = pl.BlockSpec((rows, units), lambda i: (0, 0))
    wide = pl.BlockSpec((rows, width), lambda i: (0, 0))
    whole = pl.BlockSpec((width, units), lambda i: (0, 0))
    small, large = jax.ShapeDtypeStruct((rows, units), BF16), jax.ShapeDtypeStruct((rows, width), BF16)
    handed = [] if weights else [jax.ShapeDtypeStruct((width, units), BF16)] * 3
    return pl.pallas_call(
        mlp_again_kernel if weights else partial(mlp_kernel, len(pieces), units),
        out_shape=[small] * 6 + [large] * 2 + handed,
        grid=(1,),
        in_specs=[wide] * 4
        + ([whole] * 3 if weights else [pl.BlockSpec(memory_space=pl.ANY)] * len(pieces)),
        out_specs=[narrow] * 6 + [wide] * 2 + [whole] * len(handed),
        scratch_shapes=[] if weights else [pltpu.SemaphoreType.DMA((3, len(pieces)))],
        compiler_params=params(),
        cost_estimate=cost(2 * 2 * rows * width * units * 5, 6 * width * units),
    )(own, other, own_grad, other_grad, *(weights or pieces))


def down_kernel(*refs):
    lefts, weight, outs = refs[:4], refs[4], refs[5:]
    for core in range(2):
        left = jnp.concatenate([lefts[2 * core][...], lefts[2 * core + 1][...]], 0)
        result = times_right(left, weight[...])
        outs[core][...] = (turn(result) if core else result).astype(BF16)


def mlp_down(hidden, weight):
    rows, units = hidden[0].shape
    width = weight.shape[0]
    whole = pl.BlockSpec((rows, units), lambda n: (0, 0))
    out = pl.BlockSpec((2 * rows, width), lambda n: (0, 0))
    return pl.pallas_call(
        down_kernel,
        out_shape=[jax.ShapeDtypeStruct((2 * rows, width), BF16)] * 2,
        grid=(1,),
        in_specs=[whole] * 4 + [pl.BlockSpec((width, units), lambda n: (0, 0))],
        out_specs=[out] * 2,
        compiler_params=params(),
        cost_estimate=cost(8 * rows * width * units, 2 * width * units),
    )(*hidden, weight)


def mlp_grad_kernel(*refs):
    lefts, grads, rights, outs = refs[:4], refs[4:8], refs[8:20], refs[20:]
    left = jnp.concatenate([ref[...] for ref in lefts], 0)
    grad = jnp.concatenate([ref[...] for ref in grads], 0)
    parts = []
    for index, rows in enumerate((left, left, grad)):
        right = jnp.concatenate([ref[...] for ref in rights[4 * index : 4 * index + 4]], 0)
        parts.append(times_left(rows, right).astype(BF16))
    result = jnp.concatenate(parts, 1)
    for part in range(2):

        @pl.when(pl.program_id(0) == part)
        def _():
            outs[part][...] = result


def mlp_grads(end, core, lefts, grads, grad_gate, grad_up, hidden):
    rows, width = lefts[0].shape
    units = hidden[0].shape[1]
    tile = width // 8

    def column(other, step):
        return (0, (core ^ other) * 4 + step * 2 + end)

    narrow = [pl.BlockSpec((rows, tile), partial(column, other)) for other in (0, 0, 1, 1)]
    whole = pl.BlockSpec((rows, units), lambda i: (0, 0))
    return pl.pallas_call(
        mlp_grad_kernel,
        out_shape=[jax.ShapeDtypeStruct((tile, 3 * units), BF16)] * 2,
        grid=(2,),
        in_specs=narrow * 2 + [whole] * 12,
        out_specs=[pl.BlockSpec((tile, 3 * units), lambda i: (0, 0))] * 2,
        compiler_params=params(),
        cost_estimate=cost(2 * rows * width * units * 3, 2 * width * units),
    )(*lefts, *grads, *grad_gate, *grad_up, *hidden)


def attn_grad_kernel(*refs):
    left = jnp.concatenate([ref[...] for ref in refs[:4]], 0)
    refs[5][...] = times_left(left, refs[4][...]).astype(BF16)


def attn_grad_add_kernel(*refs):
    left = jnp.concatenate([ref[...] for ref in refs[:4]], 0)
    result = (times_left(left, refs[4][...]) + refs[5][...].astype(F32)).astype(BF16)
    for part in range(2):

        @pl.when(pl.program_id(0) == part)
        def _():
            refs[6 + part][...] = result


def attn_grads(end, lefts, right, other=None):
    rows, width = lefts[0].shape
    columns = right.shape[1]
    tile = width // 8
    core = 1 if other is None else 0
    narrow = pl.BlockSpec((rows, tile), lambda i: (0, core * 4 + 2 * i + end))
    block = pl.BlockSpec((tile, columns), lambda i: (i, 0))
    whole = pl.BlockSpec((tile, columns), lambda i: (0, 0))
    return pl.pallas_call(
        attn_grad_kernel if core else attn_grad_add_kernel,
        out_shape=jax.ShapeDtypeStruct((2 * tile, columns), BF16)
        if core
        else [jax.ShapeDtypeStruct((tile, columns), BF16)] * 2,
        grid=(2,),
        in_specs=[narrow] * 4 + [pl.BlockSpec(right.shape, lambda i: (0, 0))] + ([] if core else [block]),
        out_specs=block if core else [whole] * 2,
        compiler_params=params(),
        cost_estimate=cost(2 * rows * width * columns, width * columns),
    )(*lefts, right, *([] if core else [other]))


def own_order_kernel(blocks, sizes, mine_ref, *refs):
    (shard_rows, half_rows), count = sizes, len(refs) // 2
    for index, (mask, part) in enumerate(blocks):
        start = pl.multiple_of((mine_ref[0] ^ mask) * shard_rows + part * half_rows, half_rows)
        for source, target in zip(refs[:count], refs[count:]):
            target[:, index * half_rows : (index + 1) * half_rows] = source[:, pl.ds(start, half_rows)]


def global_order_kernel(blocks, sizes, mine_ref, source, target):
    shard_rows, half_rows = sizes
    for index, (mask, part) in enumerate(blocks):
        start = pl.multiple_of((mine_ref[0] ^ mask) * shard_rows + part * half_rows, half_rows)
        target[:, pl.ds(start, half_rows)] = source[:, index * half_rows : (index + 1) * half_rows]


def reorder(kernel, blocks, sizes, mine, arrays):
    specs = [pl.BlockSpec(a.shape, lambda i, *_: (0, 0)) for a in arrays]
    return pl.pallas_call(
        partial(kernel, blocks, sizes),
        out_shape=[jax.ShapeDtypeStruct(a.shape, a.dtype) for a in arrays],
        grid_spec=pltpu.PrefetchScalarGridSpec(num_scalar_prefetch=1, grid=(1,), in_specs=specs, out_specs=specs),
        compiler_params=params(),
    )(mine, *arrays)


def middle_back_kernel(near, come, middle, grad_final, gain, low, full, gain_sum):
    grad = near[...] + come[...].astype(F32)
    normed, inverse = norm_parts(middle[...])
    total = grad_final[...].astype(F32) + norm_back(normed, inverse, grad, gain[...])
    low[...] = total.astype(BF16)
    full[...] = total

    @pl.when(pl.program_id(0) == 0)
    def _():
        gain_sum[...] = jnp.zeros_like(gain_sum)

    gain_sum[...] += jnp.sum(grad * normed, 0, keepdims=True)


def middle_back(near, come, middle, grad_final, gain):
    rows, width = near.shape
    tile = 64
    block = pl.BlockSpec((tile, width), lambda i: (i, 0))
    vector = pl.BlockSpec((1, width), lambda i: (0, 0))
    return pl.pallas_call(
        middle_back_kernel,
        out_shape=[
            jax.ShapeDtypeStruct((rows, width), BF16),
            jax.ShapeDtypeStruct((rows, width), F32),
            jax.ShapeDtypeStruct((1, width), F32),
        ],
        grid=(rows // tile,),
        in_specs=[block] * 4 + [vector],
        out_specs=[block, block, vector],
        compiler_params=params(),
        cost_estimate=cost(0, rows * width * 18),
    )(near, come, middle, grad_final, gain)


def widen(array, height):
    return jnp.concatenate([array, jnp.zeros((height - array.shape[0], array.shape[1]), array.dtype)], 0)


def send_attn_kernel(heads, *refs):
    sources, targets = refs[:5], refs[5:]
    half = targets[0].shape[0]
    spans = [slice(part * half, (part + 1) * half) for part in range(2)]
    for index, source in enumerate(sources):
        if index < 2:
            for span, target in zip(spans, targets):
                target[:, index * heads * KEY : (index + 1) * heads * KEY] = source[span, :].astype(BF16)
        else:
            for head in range(heads):
                column = 2 * heads * KEY + ((index - 2) * heads + head) * VPAD
                block = widen(source[head * VAL : (head + 1) * VAL, :], VPAD).T.astype(BF16)
                for span, target in zip(spans, targets):
                    target[:, column : column + VPAD] = block[span, :]


def send_attn(weights, heads):
    half = weights[0].shape[0] // 2
    columns = heads * (2 * KEY + 3 * VPAD)
    arrays = [*weights[:2], *(w.T for w in weights[2:])]
    return pl.pallas_call(
        partial(send_attn_kernel, heads),
        out_shape=[jax.ShapeDtypeStruct((half, columns), BF16)] * 2,
        grid=(1,),
        in_specs=[pl.BlockSpec(w.shape, lambda i: (0, 0)) for w in arrays],
        out_specs=[pl.BlockSpec((half, columns), lambda i: (0, 0))] * 2,
        compiler_params=params(),
        cost_estimate=cost(0, half * columns * 12),
    )(*arrays)


def send_mlp_kernel(padded, *refs):
    target = refs[-1]
    for index, source in enumerate(refs[:-1]):
        target[:, index * padded : (index + 1) * padded] = widen(source[...], padded).T.astype(BF16)


def send_mlp(weights, padded):
    rows, units = weights[0].shape
    return pl.pallas_call(
        partial(send_mlp_kernel, padded),
        out_shape=jax.ShapeDtypeStruct((rows, len(weights) * padded), BF16),
        grid=(1,),
        in_specs=[pl.BlockSpec((units, rows), lambda i: (0, 0))] * len(weights),
        out_specs=pl.BlockSpec((rows, len(weights) * padded), lambda i: (0, 0)),
        compiler_params=params(),
        cost_estimate=cost(0, rows * padded * 18),
    )(*(w.T for w in weights))


def receive_kernel(narrow, heads, *refs):
    targets = refs[4:]
    total = jnp.concatenate(
        [refs[2 * part][...].astype(F32) + refs[2 * part + 1][...].astype(F32) for part in range(2)], 0
    )
    column = 0
    for index, target in enumerate(targets):
        if index < narrow:
            target[...] = total[:, column : column + heads * KEY]
            column += heads * KEY
        else:
            for head in range(heads):
                target[head * VAL : (head + 1) * VAL, :] = total[:, column : column + VPAD].T[:VAL]
                column += VPAD


def receive_attn(parts, narrow, wide, heads):
    rows = 2 * parts[0].shape[0]
    shapes = [(rows, heads * KEY)] * narrow + [(heads * VAL, rows)] * wide
    found = pl.pallas_call(
        partial(receive_kernel, narrow, heads),
        out_shape=[jax.ShapeDtypeStruct(s, F32) for s in shapes],
        grid=(1,),
        in_specs=[pl.BlockSpec(p.shape, lambda i: (0, 0)) for p in parts],
        out_specs=[pl.BlockSpec(s, lambda i: (0, 0)) for s in shapes],
        compiler_params=params(),
        cost_estimate=cost(0, rows * sum(s[0] for s in shapes) * 4),
    )(*parts)
    return [*found[:narrow], *(f.T for f in found[narrow:])]


def receive_mlp_kernel(padded, odd_ref, kept, turned, core, *targets):
    first = jnp.where(odd_ref[0] == 1, turned[...], kept[...]).astype(F32)
    total = first + core[...].astype(F32)
    for index, target in enumerate(targets):
        target[...] = total[:, index * padded : (index + 1) * padded].T[: target.shape[0]]


def receive_mlp(odd, kept, turned, core, units):
    rows, columns = kept.shape
    whole = pl.BlockSpec((rows, columns), lambda i, *_: (0, 0))
    found = pl.pallas_call(
        partial(receive_mlp_kernel, columns // 3),
        out_shape=[jax.ShapeDtypeStruct((units, rows), F32)] * 3,
        grid_spec=pltpu.PrefetchScalarGridSpec(
            num_scalar_prefetch=1,
            grid=(1,),
            in_specs=[whole] * 3,
            out_specs=[pl.BlockSpec((units, rows), lambda i, *_: (0, 0))] * 3,
        ),
        compiler_params=params(),
        cost_estimate=cost(0, rows * columns * 10),
    )(odd, kept, turned, core)
    return [f.T for f in found]


def per_device(
    dp_size,
    tensor_size,
    tokens,
    lengths,
    cotangent,
    gain_one,
    gain_two,
    w_query,
    w_key,
    w_value,
    w_gate,
    w_out,
    w_mgate,
    w_mup,
    w_down,
):
    rows, width = tokens.shape
    seq = rows * tensor_size
    heads = w_query.shape[1] // KEY
    units = w_mgate.shape[1]
    shard_rows = w_query.shape[0]
    half_rows = shard_rows // 2
    bits = dp_size.bit_length() - 1
    mine, place = lax.axis_index("dp"), lax.axis_index("tensor")
    inner = (place == 1) | (place == 2)
    odd = (mine & 1) == 1
    up_bits = list(range(1, bits))
    down_bits = up_bits[::-1]

    def add(*arrays):
        return sum(array.astype(F32) for array in arrays)

    def swap_dp(array, mask):
        return lax.ppermute(array, "dp", [(i, i ^ mask) for i in range(dp_size)])

    def move_tensor(array, pairs):
        return lax.ppermute(array, "tensor", pairs)

    def swap_tensor(array, mask):
        return move_tensor(array, [(i, i ^ mask) for i in range(tensor_size)])

    across = [(1, 2), (2, 1)]
    outward = [(1, 0), (2, 3)]
    inward = [(0, 1), (3, 2)]

    def pair(dp_index, tensor_index):
        return dp_index * tensor_size + tensor_index

    top = tensor_size - 1
    to_even = [(pair(m | 1, t), pair(m, t)) for m in range(0, dp_size, 2) for t in range(tensor_size)]
    stay = [(pair(m, t), pair(m, t)) for m in range(0, dp_size, 2) for t in range(tensor_size)]
    to_odd = [(pair(m, t), pair(m | 1, t ^ top)) for m in range(0, dp_size, 2) for t in range(tensor_size)]
    odd_turn = [(pair(m | 1, t), pair(m | 1, t ^ top)) for m in range(0, dp_size, 2) for t in range(tensor_size)]
    both = ("dp", "tensor")

    def hold(array):
        return after(array, token[0])

    def close(*results):
        token[0] = after(token[0], *results)

    def line_out(slots, beside, middle):
        return move_tensor(hold(beside), across), move_tensor(hold(middle), outward)

    def line_all(own, beside, middle, far_inner, far_ends, last):
        return own, beside, jnp.where(inner, far_inner, far_ends), jnp.where(inner, middle, last)

    def first_level(piece, order):
        return swap_dp(piece, 1 << order[0])

    def second_level(piece, order):
        return swap_dp(hold(piece), 1 << order[1])

    def further(pieces, order):
        for bit in order[2:]:
            pieces = pieces + [swap_dp(p, 1 << bit) for p in pieces]
        return pieces

    def to_core(piece):
        return swap_dp(hold(piece), 1)

    def sum_start(high, order):
        return swap_dp(hold(high), 1 << order[-1])

    def sum_split(low, come):
        middle = low.shape[0] // 2
        return [add(low[span], come[span]).astype(BF16) for span in (slice(0, middle), slice(middle, 2 * middle))]

    def sum_end(low, high, order):
        for bit in order[-2:0:-1]:
            low, high = sum_split(low, swap_dp(hold(high), 1 << bit))
        return low, swap_dp(hold(high), 1 << order[0])

    blocks = [
        (chip << 1 | core, part)
        for core in range(2)
        for part, order in ((0, up_bits), (1, down_bits))
        for chip in [sum((i >> j & 1) << (b - 1) for j, b in enumerate(order)) for i in range(dp_size // 2)]
    ]

    sizes = (shard_rows, half_rows)
    aligned = half_rows % LANES == 0
    mine_arg = mine.astype(jnp.int32).reshape(1)

    def to_relative(*arrays):
        if aligned:
            return reorder(own_order_kernel, blocks, sizes, mine_arg, arrays)
        return [
            jnp.concatenate(
                [
                    lax.dynamic_slice_in_dim(a, (mine ^ mask) * shard_rows + part * half_rows, half_rows, -1)
                    for mask, part in blocks
                ],
                -1,
            )
            for a in arrays
        ]

    def to_global(array):
        if aligned:
            return reorder(global_order_kernel, blocks, sizes, mine_arg, [array])[0]
        found = []
        for shard in range(dp_size):
            mask = mine ^ shard
            for part, order in ((0, up_bits), (1, down_bits)):
                chip = sum((mask >> b & 1) << j for j, b in enumerate(order))
                index = (mask & 1) * dp_size + part * (dp_size // 2) + chip
                found.append(lax.dynamic_slice_in_dim(array, index * half_rows, half_rows, -1))
        return jnp.concatenate(found, -1)

    first_row = place * rows
    valid = (first_row + jnp.arange(rows, dtype=jnp.int32) < lengths[0])[:, None]
    head_ids = (place * heads + jnp.arange(heads, dtype=jnp.int32)).astype(F32)
    log_decay = jnp.log(1.0 - jnp.exp2(-5.0 - head_ids))
    place_arg = place.astype(jnp.int32).reshape(1)
    freqs = np.float32(10000.0) ** (-np.arange(KEY // 2, dtype=np.float32) / np.float32(KEY // 2))
    angles = np.arange(seq, dtype=np.float32)[:, None] * freqs[None, :]
    cosines, sines = jnp.asarray(np.cos(angles)), jnp.asarray(np.sin(angles))

    token = [mine_arg]
    spans = slice(0, half_rows), slice(half_rows, shard_rows)
    proj_columns, out_columns = 2 * heads * (KEY + VPAD), heads * VPAD
    padded = -(-units // LANES) * LANES

    sent_up, sent_down = send_attn((w_query, w_key, w_value, w_gate, w_out), heads)
    features_low, gain_first = to_relative(tokens, gain_one[None])
    features = features_low.astype(F32)
    normed_one, inverse_one = norm_parts(features)
    first_own = (normed_one * gain_first).astype(BF16)
    close(sent_up, sent_down, first_own)

    up_one = first_level(hold(sent_up), up_bits)
    down_one = first_level(hold(sent_down), down_bits)
    first_beside = swap_tensor(hold(first_own), 1)
    first_middle = move_tensor(hold(first_own), across)
    local_two = send_mlp((w_mgate, w_mup, hold(w_down)), padded)
    cotangent_low, gain_second = to_relative(hold(cotangent), gain_two[None])
    grad_own = jnp.where(valid, cotangent_low, 0.0)
    grad_final = grad_own.astype(F32)
    core_one = [to_core(sent_up)]
    close(up_one, down_one, first_beside, first_middle, local_two, grad_own, core_one[0])

    up_two, down_two = second_level(sent_up, up_bits), second_level(sent_down, down_bits)
    first_far = line_out(None, first_beside, first_middle)
    core_one.append(to_core(sent_down))
    close(up_two, down_two, *first_far, *core_one)

    up_three, down_three = second_level(up_one, up_bits), second_level(down_one, down_bits)
    first_last = move_tensor(hold(first_far[0]), outward)
    core_two = [to_core(p) for p in (up_one, down_one)]
    close(up_three, down_three, first_last, *core_two)

    up_all = further([sent_up, up_one, up_two, up_three], up_bits)
    down_all = further([sent_down, down_one, down_two, down_three], down_bits)
    up_core = [core_one[0], core_two[0]] + [to_core(p) for p in up_all[2:]]
    down_core = [core_one[1], core_two[1]] + [to_core(p) for p in down_all[2:]]
    mlp_zero = [lax.ppermute(hold(local_two[span]), both, odd_turn + stay) for span in spans]
    grad_beside = swap_tensor(hold(grad_own), 1)
    close(*up_core, *down_core)
    attn_low = up_all + down_all + up_core + down_core
    first_slots = line_all(first_own, first_beside, first_middle, *first_far, first_last)

    orders = up_bits, down_bits

    def level_one(halves):
        return [first_level(half, order) for half, order in zip(halves, orders)]

    def level_two(halves, come):
        found = []
        for half, other, order in zip(halves, come, orders):
            both_pieces = jnp.concatenate([half, hold(other)], 0)
            found += further_two([both_pieces, swap_dp(both_pieces, 1 << order[1])], order)
        return found

    def further_two(pieces, order):
        for bit in order[2:]:
            pieces = pieces + [swap_dp(p, 1 << bit) for p in pieces]
        return pieces

    grad_core = to_core(grad_own)
    projected = rows_times([hold(first_slots[0]), *first_slots[1:]], attn_low, 0, proj_columns)
    close(*mlp_zero, projected[0], grad_core)

    zero_come = level_one([hold(half) for half in mlp_zero])
    mlp_one = [lax.ppermute(hold(local_two)[spans[0]], both, to_even + to_odd)]
    query, key, value, normed_head, scale_head, mixed = retain(
        [hold(projected[0]), *projected[1:]], place_arg, log_decay, cosines, sines, heads
    )
    (mixed_third,) = rows_back(mixed, (3,), attn_low, proj_columns)
    close(*zero_come, mlp_one[0], grad_beside, mixed_third)

    from_ends = move_tensor(hold(mixed_third), inward)
    mlp_one.append(lax.ppermute(hold(local_two)[spans[1]], both, to_even + to_odd))
    zero_pieces = level_two(mlp_zero, zero_come)
    mixed_second, mixed_first, mixed_own = rows_back(hold(mixed), (2, 1, 0), attn_low, proj_columns)
    mixed_partial = add(mixed_second, from_ends).astype(BF16)
    grad_rows = [grad_own, grad_beside, grad_core, to_core(grad_beside)]
    close(mlp_one[1], *zero_pieces, mixed_partial, grad_rows[3])

    from_inner = move_tensor(hold(mixed_partial), across)
    from_ends = move_tensor(hold(mixed_second), inward)
    one_come = level_one([hold(half) for half in mlp_one])
    close(*one_come, from_inner, from_ends)

    from_beside = swap_tensor(add(mixed_first, hold(from_inner)).astype(BF16), 1)
    from_middle = move_tensor(add(mixed_third, hold(from_ends)).astype(BF16), across)
    mlp_pieces = zero_pieces + level_two(mlp_one, one_come)
    middle = features + add(mixed_own, from_beside, from_middle)
    normed_two, inverse_two = norm_parts(middle)
    second_own = (normed_two * gain_second).astype(BF16)
    close(*mlp_pieces, second_own)

    second_beside = swap_tensor(hold(second_own), 1)
    second_core = to_core(second_own)
    first_part = mlp(hold(second_own), second_core, grad_rows[0], grad_rows[2], mlp_pieces)
    near_core = swap_dp(first_part[7], 1)
    close(second_beside, near_core)

    second_far = to_core(second_beside)
    second_rows = [second_own, second_beside, second_core, second_far]
    second_part = mlp(hold(second_beside), second_far, grad_rows[1], grad_rows[3], None, first_part[8:])
    far_core = swap_dp(second_part[7], 1)
    hidden, grad_gate, grad_up = (
        [first_part[2 * i], second_part[2 * i], first_part[2 * i + 1], second_part[2 * i + 1]] for i in range(3)
    )

    far = add(second_part[6], far_core).astype(BF16)
    near = add(first_part[6], near_core)
    close(far, near)

    def mlp_grad(end, core):
        return mlp_grads(end, core, [hold(second_rows[0]), *second_rows[1:]], grad_rows, grad_gate, grad_up, hidden)

    second_back = swap_tensor(hold(far), 1)
    high = [mlp_grad(1, 0), mlp_grad(1, 1)]
    down_own, down_other = mlp_down([hold(hidden[0]), *hidden[1:]], first_part[10])
    close(second_back, *high[0], *high[1], down_own)

    attn_own, grad_middle, grad_gain_two = middle_back(near, hold(second_back), middle, grad_own, gain_second)
    attn_beside = swap_tensor(attn_own, 1)
    attn_second = swap_tensor(attn_own, 2)
    come = [[sum_start(high[0][0], up_bits), sum_start(high[0][1], down_bits)]]
    come.append(
        [sum_start(after(high[1][0], come[0][0]), up_bits), sum_start(after(high[1][1], come[0][1]), down_bits)]
    )
    low = [mlp_grad(0, 0), mlp_grad(0, 1)]
    down_core = to_core(down_other)
    splits = [[sum_split(low[0][part], come[0][part]) for part in range(2)]]
    close(attn_beside, attn_second, *come[1], *low[1], down_core, *splits[0][0], *splits[0][1])

    attn_middle = move_tensor(hold(attn_own), across)
    attn_last = move_tensor(hold(attn_second), outward)
    splits.append([sum_split(low[1][part], hold(come[1][part])) for part in range(2)])

    def mlp_end(core):
        return [sum_end(*splits[core][part], orders[part]) for part in range(2)]

    def mlp_sum(ends):
        return [add(*end).astype(BF16) for end in ends]

    mlp_total = [mlp_sum(mlp_end(0))]
    grad_mixed = rows_times([hold(attn_own), attn_beside, attn_second], attn_low, proj_columns, out_columns)
    down_sum = add(down_own, hold(down_core))
    down_sent = down_sum[rows:].astype(BF16)
    close(attn_middle, attn_last, *mlp_total[0], grad_mixed[0])
    attn_slots = attn_own, attn_beside, attn_second, jnp.where(inner, attn_middle, hold(attn_last))

    grad_mixed = grad_mixed + rows_times([attn_slots[3]], attn_low, proj_columns, out_columns)
    grad_turn = lax.ppermute(
        jnp.concatenate([after(t, grad_mixed[3]) for t in mlp_total[0]], 0), both, [(b, a) for a, b in odd_turn]
    )
    grad_proj = retain_back(
        grad_mixed, projected, normed_head, scale_head, query, key, value, place_arg, log_decay, cosines, sines, heads
    )
    back_third, gain_third = rows_back(grad_proj, (3,), attn_low, 0, first_slots[3:])
    mlp_ends = mlp_end(1)
    close(grad_turn, back_third, mlp_ends[0][1], mlp_ends[1][1])

    from_ends = move_tensor(hold(back_third), inward)
    to_owner = [(b, a) for a, b in to_even + to_odd]
    mlp_total.append(mlp_sum([(low_part, hold(come_part)) for low_part, come_part in mlp_ends]))
    grad_core = [lax.ppermute(mlp_total[1][0], both, to_owner)]
    other_high = attn_grads(1, first_slots, hold(grad_proj))
    back_second, gain_second_part = rows_back(after(grad_proj, other_high), (2,), attn_low, 0, first_slots[2:3])
    other_low = attn_grads(0, first_slots, after(grad_proj, back_second))
    back_partial = add(back_second, from_ends).astype(BF16)
    close(back_partial, other_low, grad_core[0])

    from_inner = move_tensor(hold(back_partial), across)
    from_ends = move_tensor(hold(back_second), inward)
    core_high, core_low = to_core(other_high), to_core(other_low)
    out_other_high = attn_grads(1, attn_slots, hold(mixed))
    out_other_low = attn_grads(0, attn_slots, after(mixed, out_other_high))
    back_own, back_first, gain_near = rows_back(after(grad_proj, out_other_low), (0, 1), attn_low, 0, first_slots[:2])
    up_high, down_high = attn_grads(1, first_slots, after(grad_proj, back_own), core_high)
    proj_come = swap_dp(up_high, 1 << up_bits[-1]), swap_dp(down_high, 1 << down_bits[-1])
    close(from_inner, from_ends, back_own, core_low, out_other_low, up_high)

    from_beside = swap_tensor(add(back_first, hold(from_inner)).astype(BF16), 1)
    from_middle = move_tensor(add(back_third, hold(from_ends)).astype(BF16), across)
    out_core_high, out_core_low = to_core(out_other_high), to_core(out_other_low)
    up_low, down_low = attn_grads(0, first_slots, hold(grad_proj), core_low)
    out_up_high, out_down_high = attn_grads(1, attn_slots, after(mixed, up_low), out_core_high)
    out_up_low, out_down_low = attn_grads(0, attn_slots, after(mixed, out_up_high), out_core_low)
    gain_parts = gain_third[0] + gain_second_part[0] + hold(gain_near)[0]
    gains = to_global(jnp.stack([gain_parts / gain_first[0], grad_gain_two[0]]))
    gains = gains + swap_dp(gains, 1)
    close(from_beside, from_middle, *proj_come, gains, up_low, out_up_low)

    down_beside = swap_tensor(hold(down_sent), 1)
    proj_up = sum_end(*sum_split(up_low, hold(proj_come[0])), up_bits)
    proj_down = sum_end(*sum_split(down_low, hold(proj_come[1])), down_bits)
    out_come = sum_start(out_up_high, up_bits), sum_start(out_down_high, down_bits)
    grad_core.append(lax.ppermute(after(mlp_total[1][1], out_come[0]), both, to_owner))
    grad_first = add(back_own, hold(from_beside), from_middle)
    grad_tokens = grad_middle + norm_back(normed_one, inverse_one, grad_first, gain_first)
    grad_tokens = to_global(grad_tokens.astype(BF16))
    close(*proj_up, *proj_down, *out_come, grad_core[1], down_beside, grad_tokens)

    final = middle + down_sum[:rows] + hold(down_beside).astype(F32)
    output = to_global(jnp.where(valid, final, 0.0).astype(BF16))
    sum_mgate, sum_mup, sum_down = receive_mlp(
        (mine & 1).astype(jnp.int32).reshape(1),
        jnp.concatenate([hold(t) for t in mlp_total[0]], 0),
        grad_turn,
        jnp.concatenate(grad_core, 0),
        units,
    )
    out_up = sum_end(*sum_split(out_up_low, hold(out_come[0])), up_bits)
    out_down = sum_end(*sum_split(out_down_low, hold(out_come[1])), down_bits)
    gains = hold(gains)
    gains = gains + sum(swap_dp(gains, 2 * chip) for chip in range(1, dp_size // 2))
    gains = gains + sum(swap_tensor(gains, other) for other in range(1, tensor_size))
    sum_query, sum_key, sum_value, sum_gate = receive_attn(
        (hold(proj_up[0]), proj_up[1], *proj_down), 2, 2, heads
    )
    (sum_out,) = receive_attn((*out_up, *out_down), 0, 1, heads)
    return (
        output,
        grad_tokens,
        gains[0],
        gains[1],
        sum_query,
        sum_key,
        sum_value,
        sum_gate,
        sum_out,
        sum_mgate,
        sum_mup,
        sum_down,
    )


def solution(mesh):
    rows = P(("dp", "tensor"), None)
    block = P("dp", "tensor")
    return jax.shard_map(
        partial(per_device, mesh.shape["dp"], mesh.shape["tensor"]),
        mesh=mesh,
        in_specs=(rows, P("dp"), rows, P(), P()) + (block,) * 8,
        out_specs=(rows, rows, P(), P()) + (block,) * 8,
        check_vma=False,
    )
```

```python
from functools import partial

import jax
import jax.numpy as jnp
import numpy as np
from jax import lax
from jax.experimental import pallas as pl
from jax.experimental.pallas import tpu as pltpu
from jax.sharding import PartitionSpec as P

KEY = 256
VAL = 432
VPAD = 512
LANES = 128
EPS = 1e-05
HEAD_EPS = 1.0
F32 = jnp.float32
BF16 = jnp.bfloat16
VMEM_LIMIT = 48 * 1024 * 1024


def times_plain(left, right):
    return jnp.dot(left, right, preferred_element_type=F32)


def times_left(left, right):
    return lax.dot_general(left, right, (((0,), (0,)), ((), ())), preferred_element_type=F32)


def times_right(left, right):
    return lax.dot_general(left, right, (((1,), (1,)), ((), ())), preferred_element_type=F32)


def after(array, *earlier):
    return lax.optimization_barrier((array, *earlier))[0]


def params(**more):
    return pltpu.CompilerParams(vmem_limit_bytes=VMEM_LIMIT, **more)


def cost(flops, moved):
    return pl.CostEstimate(flops=flops // 64, bytes_accessed=moved // 64, transcendentals=0)


def norm_parts(features):
    centred = features - jnp.mean(features, -1, keepdims=True)
    inverse = lax.rsqrt(jnp.mean(centred * centred, -1, keepdims=True) + EPS)
    return centred * inverse, inverse


def norm_back(normed, inverse, grad, gain):
    scaled = grad * gain
    return inverse * (
        scaled
        - jnp.mean(scaled, -1, keepdims=True)
        - normed * jnp.mean(scaled * normed, -1, keepdims=True)
    )


def decay_rows(log_decay, rows, width):
    query = lax.broadcasted_iota(jnp.int32, (rows, width), 0) + (width - rows)
    key = lax.broadcasted_iota(jnp.int32, (rows, width), 1)
    spacing = query - key
    factor = jnp.exp(log_decay * jnp.maximum(spacing, 0).astype(F32))
    return jnp.where(spacing >= 0, factor, 0.0)


def retain_kernel(slots, rows, place_ref, decay_ref, *refs):
    ins, (cos_ref, sin_ref), outs = refs[: 4 * slots], refs[4 * slots : 4 * slots + 2], refs[4 * slots + 2 :]
    query_ref, key_ref, value_ref, normed_ref, scale_ref, mixed_ref, factor_ref, kept_ref = outs
    head = pl.program_id(0)
    place = place_ref[0]
    seq = slots * rows
    half = KEY // 2
    for slot in range(slots):
        start = pl.multiple_of((slot ^ place) * rows, rows)
        cosines, sines = cos_ref[pl.ds(start, rows), :], sin_ref[pl.ds(start, rows), :]
        for source, target, scale in ((ins[slot], query_ref, 1.0), (ins[slots + slot], key_ref, KEY**-0.5)):
            low = source[:, :half].astype(F32)
            high = source[:, half:].astype(F32)
            target[pl.ds(start, rows), :half] = ((low * cosines - high * sines) * scale).astype(BF16)
            target[pl.ds(start, rows), half:] = ((high * cosines + low * sines) * scale).astype(BF16)
        value_ref[pl.ds(start, rows), :] = ins[2 * slots + slot][...]
    factor_ref[...] = decay_rows(decay_ref[head], rows, seq)
    for block in range(slots):
        width = (block + 1) * rows
        scores = times_right(query_ref[block * rows : width, :], key_ref[:width, :])
        weights = (scores * factor_ref[:, seq - width :]).astype(BF16)
        kept_ref[block * rows : width, :] = times_plain(weights, value_ref[:width, :])
    inside = lax.broadcasted_iota(jnp.int32, (rows, VPAD), 1) < VAL
    for slot in range(slots):
        start = pl.multiple_of((slot ^ place) * rows, rows)
        kept = kept_ref[pl.ds(start, rows), :]
        mean = jnp.sum(kept, -1, keepdims=True) / VAL
        centred = jnp.where(inside, kept - mean, 0.0)
        inverse = lax.rsqrt(jnp.sum(centred * centred, -1, keepdims=True) / VAL + HEAD_EPS)
        normed = centred * inverse
        gate = ins[3 * slots + slot][...].astype(F32)
        mixed = gate * jax.nn.sigmoid(gate) * normed
        mixed_ref[slot * rows : (slot + 1) * rows, :] = mixed.astype(BF16)
        normed_ref[slot * rows : (slot + 1) * rows, :] = normed.astype(BF16)
        scale_ref[slot * rows : (slot + 1) * rows, :] = jnp.broadcast_to(inverse, (rows, 128))


def slot_specs(rows, heads):
    first_value = 2 * heads * KEY // VPAD
    return (
        pl.BlockSpec((rows, KEY), lambda h, *_: (0, h)),
        pl.BlockSpec((rows, KEY), lambda h, *_: (0, heads + h)),
        pl.BlockSpec((rows, VPAD), lambda h, *_: (0, first_value + h)),
        pl.BlockSpec((rows, VPAD), lambda h, *_: (0, first_value + heads + h)),
    )


def retain(projected, place, log_decay, cosines, sines, heads):
    slots, rows = len(projected), projected[0].shape[0]
    seq = slots * rows
    specs = slot_specs(rows, heads)
    table = pl.BlockSpec((seq, KEY // 2), lambda h, *_: (0, 0))

    def column(width):
        return pl.BlockSpec((seq, width), lambda h, *_: (0, h))

    return pl.pallas_call(
        partial(retain_kernel, slots, rows),
        out_shape=(
            jax.ShapeDtypeStruct((seq, heads * KEY), BF16),
            jax.ShapeDtypeStruct((seq, heads * KEY), BF16),
            jax.ShapeDtypeStruct((seq, heads * VPAD), BF16),
            jax.ShapeDtypeStruct((seq, heads * VPAD), BF16),
            jax.ShapeDtypeStruct((seq, heads * 128), F32),
            jax.ShapeDtypeStruct((seq, heads * VPAD), BF16),
        ),
        grid_spec=pltpu.PrefetchScalarGridSpec(
            num_scalar_prefetch=2,
            grid=(heads,),
            in_specs=[spec for spec in specs for _ in range(slots)] + [table, table],
            out_specs=[column(KEY), column(KEY), column(VPAD), column(VPAD), column(128), column(VPAD)],
            scratch_shapes=[pltpu.VMEM((rows, seq), F32), pltpu.VMEM((seq, VPAD), F32)],
        ),
        compiler_params=pltpu.CompilerParams(vmem_limit_bytes=VMEM_LIMIT),
        cost_estimate=cost(heads * seq * seq * (KEY + VPAD), heads * seq * 9000),
    )(place, log_decay, *(projected * 4), cosines, sines)


def retain_back_kernel(slots, rows, heads, place_ref, decay_ref, *refs):
    grads, gates, rest = refs[:slots], refs[slots : 2 * slots], refs[2 * slots :]
    (normed_ref, scale_ref, query_ref, key_ref, value_ref, cos_ref, sin_ref, out_ref, factor_ref, ret_ref, key_sum, value_sum) = rest
    head = pl.program_id(0)
    place = place_ref[0]
    seq = slots * rows
    half = KEY // 2
    query_col = pl.multiple_of(head * KEY, KEY)
    key_col = pl.multiple_of((heads + head) * KEY, KEY)
    value_col = pl.multiple_of(2 * heads * KEY + head * VPAD, VPAD)
    gate_col = pl.multiple_of(2 * heads * KEY + (heads + head) * VPAD, VPAD)
    inside = lax.broadcasted_iota(jnp.int32, (rows, VPAD), 1) < VAL
    for slot in range(slots):
        start = pl.multiple_of((slot ^ place) * rows, rows)
        span = slice(slot * rows, (slot + 1) * rows)
        grad, gate = grads[slot][...].astype(F32), gates[slot][...].astype(F32)
        normed, inverse = normed_ref[span, :].astype(F32), scale_ref[span, :1]
        sig = jax.nn.sigmoid(gate)
        out_ref[span, pl.ds(gate_col, VPAD)] = (grad * normed * sig * (1.0 + gate * (1.0 - sig))).astype(BF16)
        grad_normed = grad * gate * sig
        mean = jnp.sum(grad_normed, -1, keepdims=True) / VAL
        along = jnp.sum(grad_normed * normed, -1, keepdims=True) / VAL
        grad_ret = inverse * (grad_normed - mean - normed * along)
        ret_ref[pl.ds(start, rows), :] = jnp.where(inside, grad_ret, 0.0).astype(BF16)
    factor_ref[...] = decay_rows(decay_ref[head], rows, seq)
    key_sum[...] = jnp.zeros_like(key_sum)
    value_sum[...] = jnp.zeros_like(value_sum)
    for block in range(slots):
        width = (block + 1) * rows
        span = slice(block * rows, width)
        query, ret, keys = query_ref[span, :], ret_ref[span, :], key_ref[:width, :]
        factor = factor_ref[:, seq - width :]
        weights = (times_right(query, keys) * factor).astype(BF16)
        grad_scores = (times_right(ret, value_ref[:width, :]) * factor).astype(BF16)
        value_sum[:width, :] += times_left(weights, ret)
        key_sum[:width, :] += times_left(grad_scores, query)
        grad_query = times_plain(grad_scores, keys)
        row = pl.multiple_of((block ^ place) * rows, rows)
        cosines, sines = cos_ref[span, :], sin_ref[span, :]
        low, high = grad_query[:, :half], grad_query[:, half:]
        out_ref[pl.ds(row, rows), pl.ds(query_col, half)] = (low * cosines + high * sines).astype(BF16)
        out_ref[pl.ds(row, rows), pl.ds(pl.multiple_of(query_col + half, half), half)] = (
            high * cosines - low * sines
        ).astype(BF16)
    for block in range(slots):
        span = slice(block * rows, (block + 1) * rows)
        row = pl.multiple_of((block ^ place) * rows, rows)
        cosines, sines = cos_ref[span, :], sin_ref[span, :]
        low, high = key_sum[span, :half] * KEY**-0.5, key_sum[span, half:] * KEY**-0.5
        out_ref[pl.ds(row, rows), pl.ds(key_col, half)] = (low * cosines + high * sines).astype(BF16)
        out_ref[pl.ds(row, rows), pl.ds(pl.multiple_of(key_col + half, half), half)] = (
            high * cosines - low * sines
        ).astype(BF16)
        out_ref[pl.ds(row, rows), pl.ds(value_col, VPAD)] = value_sum[span, :].astype(BF16)


def retain_back(grads, projected, normed, scale, query, key, value, place, log_decay, cosines, sines, heads):
    slots, rows = len(projected), projected[0].shape[0]
    seq = slots * rows
    columns = 2 * heads * (KEY + VPAD)
    table = pl.BlockSpec((seq, KEY // 2), lambda h, *_: (0, 0))

    def column(width):
        return pl.BlockSpec((seq, width), lambda h, *_: (0, h))

    return pl.pallas_call(
        partial(retain_back_kernel, slots, rows, heads),
        out_shape=jax.ShapeDtypeStruct((seq, columns), BF16),
        grid_spec=pltpu.PrefetchScalarGridSpec(
            num_scalar_prefetch=2,
            grid=(heads,),
            in_specs=[pl.BlockSpec((rows, VPAD), lambda h, *_: (0, h))] * slots
            + [slot_specs(rows, heads)[3]] * slots
            + [column(VPAD), column(128), column(KEY), column(KEY), column(VPAD), table, table],
            out_specs=pl.BlockSpec((seq, columns), lambda h, *_: (0, 0)),
            scratch_shapes=[
                pltpu.VMEM((rows, seq), F32),
                pltpu.VMEM((seq, VPAD), BF16),
                pltpu.VMEM((seq, KEY), F32),
                pltpu.VMEM((seq, VPAD), F32),
            ],
        ),
        compiler_params=pltpu.CompilerParams(vmem_limit_bytes=VMEM_LIMIT),
        cost_estimate=cost(heads * seq * seq * (3 * KEY + 2 * VPAD), heads * seq * 10000),
    )(place, log_decay, *grads, *projected, normed, scale, query, key, value, cosines, sines)


def rows_kernel(slots, pieces, *refs):
    lefts, weights, outs = refs[:slots], refs[slots : slots + pieces], refs[slots + pieces :]
    left = jnp.concatenate([ref[...] for ref in lefts], 0)
    result = times_plain(left, jnp.concatenate([ref[...] for ref in weights], 0)).astype(BF16)
    rows = lefts[0].shape[0]
    for slot in range(slots):
        outs[slot][...] = result[slot * rows : (slot + 1) * rows]


def rows_times(lefts, pieces, first, columns, tile=512):
    rows, width = lefts[0].shape
    return pl.pallas_call(
        partial(rows_kernel, len(lefts), len(pieces)),
        out_shape=[jax.ShapeDtypeStruct((rows, columns), BF16)] * len(lefts),
        grid=(columns // tile,),
        in_specs=[pl.BlockSpec((rows, width), lambda n: (0, 0))] * len(lefts)
        + [pl.BlockSpec((p.shape[0], tile), lambda n: (0, n + first // tile)) for p in pieces],
        out_specs=[pl.BlockSpec((rows, tile), lambda n: (0, n))] * len(lefts),
        compiler_params=params(),
        cost_estimate=cost(2 * len(lefts) * rows * width * columns, 2 * width * columns),
    )(*lefts, *pieces)


def rows_back_kernel(slots, pieces, weigh, *refs):
    lefts, weights, rest = refs[:slots], refs[slots : slots + pieces], refs[slots + pieces :]
    total = rest[-1]
    step = pl.program_id(0)
    left = jnp.concatenate([ref[...] for ref in lefts], 0)
    part = times_right(left, jnp.concatenate([ref[...] for ref in weights], 0))

    @pl.when(step == 0)
    def _():
        total[...] = part

    @pl.when(step > 0)
    def _():
        total[...] += part

    @pl.when(step == pl.num_programs(0) - 1)
    def _():
        rows = lefts[0].shape[0]
        for slot in range(slots):
            rest[weigh * slots + slot][...] = total[slot * rows : (slot + 1) * rows, :].astype(BF16)
        if weigh:
            other = jnp.concatenate([ref[...] for ref in rest[:slots]], 0).astype(F32)
            along = jnp.sum(total[...] * other, 0, keepdims=True)
            rest[2 * slots][...] = jnp.broadcast_to(along, (8, along.shape[1]))


def rows_back(left, slots, pieces, first=0, weigh=(), tile=512):
    rows = left.shape[0] // 4
    columns = left.shape[1]
    width = sum(p.shape[0] for p in pieces)
    whole = pl.BlockSpec((rows, width), lambda k: (0, 0))
    return pl.pallas_call(
        partial(rows_back_kernel, len(slots), len(pieces), 1 if weigh else 0),
        out_shape=[jax.ShapeDtypeStruct((rows, width), BF16)] * len(slots)
        + ([jax.ShapeDtypeStruct((8, width), F32)] if weigh else []),
        grid=(columns // tile,),
        in_specs=[pl.BlockSpec((rows, tile), partial(lambda s, k: (s, k), s)) for s in slots]
        + [pl.BlockSpec((p.shape[0], tile), lambda k: (0, k + first // tile)) for p in pieces]
        + [whole] * len(weigh),
        out_specs=[whole] * len(slots) + ([pl.BlockSpec((8, width), lambda k: (0, 0))] if weigh else []),
        scratch_shapes=[pltpu.VMEM((len(slots) * rows, width), F32)],
        compiler_params=params(),
        cost_estimate=cost(2 * len(slots) * rows * width * columns, 2 * width * columns),
    )(*([left] * len(slots)), *pieces, *weigh)


def turn(array):
    middle = array.shape[1] // 2
    return jnp.concatenate([array[:, middle:], array[:, :middle]], 1)


def mlp_kernel(pieces, units, own_ref, other_ref, own_grad_ref, other_grad_ref, *refs):
    sources, outs, weights = refs[:pieces], refs[pieces : pieces + 8], refs[pieces + 8 : pieces + 11]
    semaphores = refs[pieces + 11]
    copies = []
    for part, target in enumerate(weights):
        place = 0
        for index, source in enumerate(sources):
            height = source.shape[0]
            copy = pltpu.make_async_copy(
                source.at[:, pl.ds(part * units, units)],
                target.at[pl.ds(place, height), :],
                semaphores.at[part, index],
            )
            copy.start()
            copies.append(copy)
            place += height

    def ready(part):
        for copy in copies[part * pieces : (part + 1) * pieces]:
            copy.wait()

    mlp_body(ready, own_ref, other_ref, own_grad_ref, other_grad_ref, weights, outs)


def mlp_again_kernel(own_ref, other_ref, own_grad_ref, other_grad_ref, *refs):
    mlp_body(lambda part: None, own_ref, other_ref, own_grad_ref, other_grad_ref, refs[:3], refs[3:])


def mlp_body(ready, own_ref, other_ref, own_grad_ref, other_grad_ref, weights, outs):
    gate_ref, up_ref, down_ref = weights
    rows = own_ref.shape[0]
    left = jnp.concatenate([own_ref[...], turn(other_ref[...])], 0)
    grad = jnp.concatenate([own_grad_ref[...], turn(other_grad_ref[...])], 0)
    ready(0)
    gate = times_plain(left, gate_ref[...])
    ready(1)
    up = times_plain(left, up_ref[...])
    ready(2)
    grad_hidden = times_plain(grad, down_ref[...])
    below = 0.5 + 0.5 * lax.erf(gate * (0.5**0.5))
    density = jnp.exp(-0.5 * gate * gate) * 0.3989422804014327
    smooth = gate * below
    hidden = (smooth * up).astype(BF16)
    grad_gate = (grad_hidden * up * (below + gate * density)).astype(BF16)
    grad_up = (grad_hidden * smooth).astype(BF16)
    for slot in range(2):
        span = slice(slot * rows, (slot + 1) * rows)
        outs[slot][...] = hidden[span]
        outs[2 + slot][...] = grad_gate[span]
        outs[4 + slot][...] = grad_up[span]
    back = times_right(grad_gate, gate_ref[...]) + times_right(grad_up, up_ref[...])
    outs[6][...] = back[:rows].astype(BF16)
    outs[7][...] = turn(back[rows:]).astype(BF16)


def mlp(own, other, own_grad, other_grad, pieces, weights=None):
    rows, width = own.shape
    units = weights[0].shape[1] if weights else pieces[0].shape[1] // 3
    narrow = pl.BlockSpec((rows, units), lambda i: (0, 0))
    wide = pl.BlockSpec((rows, width), lambda i: (0, 0))
    whole = pl.BlockSpec((width, units), lambda i: (0, 0))
    small, large = jax.ShapeDtypeStruct((rows, units), BF16), jax.ShapeDtypeStruct((rows, width), BF16)
    handed = [] if weights else [jax.ShapeDtypeStruct((width, units), BF16)] * 3
    return pl.pallas_call(
        mlp_again_kernel if weights else partial(mlp_kernel, len(pieces), units),
        out_shape=[small] * 6 + [large] * 2 + handed,
        grid=(1,),
        in_specs=[wide] * 4
        + ([whole] * 3 if weights else [pl.BlockSpec(memory_space=pl.ANY)] * len(pieces)),
        out_specs=[narrow] * 6 + [wide] * 2 + [whole] * len(handed),
        scratch_shapes=[] if weights else [pltpu.SemaphoreType.DMA((3, len(pieces)))],
        compiler_params=params(),
        cost_estimate=cost(2 * 2 * rows * width * units * 5, 6 * width * units),
    )(own, other, own_grad, other_grad, *(weights or pieces))


def down_kernel(*refs):
    lefts, weight, outs = refs[:4], refs[4], refs[5:]
    for core in range(2):
        left = jnp.concatenate([lefts[2 * core][...], lefts[2 * core + 1][...]], 0)
        result = times_right(left, weight[...])
        outs[core][...] = (turn(result) if core else result).astype(BF16)


def mlp_down(hidden, weight):
    rows, units = hidden[0].shape
    width = weight.shape[0]
    whole = pl.BlockSpec((rows, units), lambda n: (0, 0))
    out = pl.BlockSpec((2 * rows, width), lambda n: (0, 0))
    return pl.pallas_call(
        down_kernel,
        out_shape=[jax.ShapeDtypeStruct((2 * rows, width), BF16)] * 2,
        grid=(1,),
        in_specs=[whole] * 4 + [pl.BlockSpec((width, units), lambda n: (0, 0))],
        out_specs=[out] * 2,
        compiler_params=params(),
        cost_estimate=cost(8 * rows * width * units, 2 * width * units),
    )(*hidden, weight)


def mlp_grad_kernel(*refs):
    lefts, grads, rights, outs = refs[:4], refs[4:8], refs[8:20], refs[20:]
    left = jnp.concatenate([ref[...] for ref in lefts], 0)
    grad = jnp.concatenate([ref[...] for ref in grads], 0)
    parts = []
    for index, rows in enumerate((left, left, grad)):
        right = jnp.concatenate([ref[...] for ref in rights[4 * index : 4 * index + 4]], 0)
        parts.append(times_left(rows, right).astype(BF16))
    result = jnp.concatenate(parts, 1)
    for part in range(2):

        @pl.when(pl.program_id(0) == part)
        def _():
            outs[part][...] = result


def mlp_grads(end, core, lefts, grads, grad_gate, grad_up, hidden):
    rows, width = lefts[0].shape
    units = hidden[0].shape[1]
    tile = width // 8

    def column(other, step):
        return (0, (core ^ other) * 4 + step * 2 + end)

    narrow = [pl.BlockSpec((rows, tile), partial(column, other)) for other in (0, 0, 1, 1)]
    whole = pl.BlockSpec((rows, units), lambda i: (0, 0))
    return pl.pallas_call(
        mlp_grad_kernel,
        out_shape=[jax.ShapeDtypeStruct((tile, 3 * units), BF16)] * 2,
        grid=(2,),
        in_specs=narrow * 2 + [whole] * 12,
        out_specs=[pl.BlockSpec((tile, 3 * units), lambda i: (0, 0))] * 2,
        compiler_params=params(),
        cost_estimate=cost(2 * rows * width * units * 3, 2 * width * units),
    )(*lefts, *grads, *grad_gate, *grad_up, *hidden)


def attn_grad_kernel(*refs):
    left = jnp.concatenate([ref[...] for ref in refs[:4]], 0)
    refs[5][...] = times_left(left, refs[4][...]).astype(BF16)


def attn_grad_add_kernel(*refs):
    left = jnp.concatenate([ref[...] for ref in refs[:4]], 0)
    result = (times_left(left, refs[4][...]) + refs[5][...].astype(F32)).astype(BF16)
    for part in range(2):

        @pl.when(pl.program_id(0) == part)
        def _():
            refs[6 + part][...] = result


def attn_grads(end, lefts, right, other=None):
    rows, width = lefts[0].shape
    columns = right.shape[1]
    tile = width // 8
    core = 1 if other is None else 0
    narrow = pl.BlockSpec((rows, tile), lambda i: (0, core * 4 + 2 * i + end))
    block = pl.BlockSpec((tile, columns), lambda i: (i, 0))
    whole = pl.BlockSpec((tile, columns), lambda i: (0, 0))
    return pl.pallas_call(
        attn_grad_kernel if core else attn_grad_add_kernel,
        out_shape=jax.ShapeDtypeStruct((2 * tile, columns), BF16)
        if core
        else [jax.ShapeDtypeStruct((tile, columns), BF16)] * 2,
        grid=(2,),
        in_specs=[narrow] * 4 + [pl.BlockSpec(right.shape, lambda i: (0, 0))] + ([] if core else [block]),
        out_specs=block if core else [whole] * 2,
        compiler_params=params(),
        cost_estimate=cost(2 * rows * width * columns, width * columns),
    )(*lefts, right, *([] if core else [other]))


def own_order_kernel(blocks, sizes, mine_ref, *refs):
    (shard_rows, half_rows), count = sizes, len(refs) // 2
    for index, (mask, part) in enumerate(blocks):
        start = pl.multiple_of((mine_ref[0] ^ mask) * shard_rows + part * half_rows, half_rows)
        for source, target in zip(refs[:count], refs[count:]):
            target[:, index * half_rows : (index + 1) * half_rows] = source[:, pl.ds(start, half_rows)]


def global_order_kernel(blocks, sizes, mine_ref, source, target):
    shard_rows, half_rows = sizes
    for index, (mask, part) in enumerate(blocks):
        start = pl.multiple_of((mine_ref[0] ^ mask) * shard_rows + part * half_rows, half_rows)
        target[:, pl.ds(start, half_rows)] = source[:, index * half_rows : (index + 1) * half_rows]


def reorder(kernel, blocks, sizes, mine, arrays):
    specs = [pl.BlockSpec(a.shape, lambda i, *_: (0, 0)) for a in arrays]
    return pl.pallas_call(
        partial(kernel, blocks, sizes),
        out_shape=[jax.ShapeDtypeStruct(a.shape, a.dtype) for a in arrays],
        grid_spec=pltpu.PrefetchScalarGridSpec(num_scalar_prefetch=1, grid=(1,), in_specs=specs, out_specs=specs),
        compiler_params=params(),
    )(mine, *arrays)


def middle_back_kernel(near, come, middle, grad_final, gain, low, full, gain_sum):
    grad = near[...] + come[...].astype(F32)
    normed, inverse = norm_parts(middle[...])
    total = grad_final[...].astype(F32) + norm_back(normed, inverse, grad, gain[...])
    low[...] = total.astype(BF16)
    full[...] = total

    @pl.when(pl.program_id(0) == 0)
    def _():
        gain_sum[...] = jnp.zeros_like(gain_sum)

    gain_sum[...] += jnp.sum(grad * normed, 0, keepdims=True)


def middle_back(near, come, middle, grad_final, gain):
    rows, width = near.shape
    tile = 64
    block = pl.BlockSpec((tile, width), lambda i: (i, 0))
    vector = pl.BlockSpec((1, width), lambda i: (0, 0))
    return pl.pallas_call(
        middle_back_kernel,
        out_shape=[
            jax.ShapeDtypeStruct((rows, width), BF16),
            jax.ShapeDtypeStruct((rows, width), F32),
            jax.ShapeDtypeStruct((1, width), F32),
        ],
        grid=(rows // tile,),
        in_specs=[block] * 4 + [vector],
        out_specs=[block, block, vector],
        compiler_params=params(),
        cost_estimate=cost(0, rows * width * 18),
    )(near, come, middle, grad_final, gain)


def widen(array, height):
    return jnp.concatenate([array, jnp.zeros((height - array.shape[0], array.shape[1]), array.dtype)], 0)


def send_attn_kernel(heads, *refs):
    sources, targets = refs[:5], refs[5:]
    half = targets[0].shape[0]
    spans = [slice(part * half, (part + 1) * half) for part in range(2)]
    for index, source in enumerate(sources):
        if index < 2:
            for span, target in zip(spans, targets):
                target[:, index * heads * KEY : (index + 1) * heads * KEY] = source[span, :].astype(BF16)
        else:
            for head in range(heads):
                column = 2 * heads * KEY + ((index - 2) * heads + head) * VPAD
                block = widen(source[head * VAL : (head + 1) * VAL, :], VPAD).T.astype(BF16)
                for span, target in zip(spans, targets):
                    target[:, column : column + VPAD] = block[span, :]


def send_attn(weights, heads):
    half = weights[0].shape[0] // 2
    columns = heads * (2 * KEY + 3 * VPAD)
    arrays = [*weights[:2], *(w.T for w in weights[2:])]
    return pl.pallas_call(
        partial(send_attn_kernel, heads),
        out_shape=[jax.ShapeDtypeStruct((half, columns), BF16)] * 2,
        grid=(1,),
        in_specs=[pl.BlockSpec(w.shape, lambda i: (0, 0)) for w in arrays],
        out_specs=[pl.BlockSpec((half, columns), lambda i: (0, 0))] * 2,
        compiler_params=params(),
        cost_estimate=cost(0, half * columns * 12),
    )(*arrays)


def send_mlp_kernel(padded, *refs):
    target = refs[-1]
    for index, source in enumerate(refs[:-1]):
        target[:, index * padded : (index + 1) * padded] = widen(source[...], padded).T.astype(BF16)


def send_mlp(weights, padded):
    rows, units = weights[0].shape
    return pl.pallas_call(
        partial(send_mlp_kernel, padded),
        out_shape=jax.ShapeDtypeStruct((rows, len(weights) * padded), BF16),
        grid=(1,),
        in_specs=[pl.BlockSpec((units, rows), lambda i: (0, 0))] * len(weights),
        out_specs=pl.BlockSpec((rows, len(weights) * padded), lambda i: (0, 0)),
        compiler_params=params(),
        cost_estimate=cost(0, rows * padded * 18),
    )(*(w.T for w in weights))


def receive_kernel(narrow, heads, *refs):
    targets = refs[4:]
    total = jnp.concatenate(
        [refs[2 * part][...].astype(F32) + refs[2 * part + 1][...].astype(F32) for part in range(2)], 0
    )
    column = 0
    for index, target in enumerate(targets):
        if index < narrow:
            target[...] = total[:, column : column + heads * KEY]
            column += heads * KEY
        else:
            for head in range(heads):
                target[head * VAL : (head + 1) * VAL, :] = total[:, column : column + VPAD].T[:VAL]
                column += VPAD


def receive_attn(parts, narrow, wide, heads):
    rows = 2 * parts[0].shape[0]
    shapes = [(rows, heads * KEY)] * narrow + [(heads * VAL, rows)] * wide
    found = pl.pallas_call(
        partial(receive_kernel, narrow, heads),
        out_shape=[jax.ShapeDtypeStruct(s, F32) for s in shapes],
        grid=(1,),
        in_specs=[pl.BlockSpec(p.shape, lambda i: (0, 0)) for p in parts],
        out_specs=[pl.BlockSpec(s, lambda i: (0, 0)) for s in shapes],
        compiler_params=params(),
        cost_estimate=cost(0, rows * sum(s[0] for s in shapes) * 4),
    )(*parts)
    return [*found[:narrow], *(f.T for f in found[narrow:])]


def receive_mlp_kernel(padded, odd_ref, kept, turned, core, *targets):
    first = jnp.where(odd_ref[0] == 1, turned[...], kept[...]).astype(F32)
    total = first + core[...].astype(F32)
    for index, target in enumerate(targets):
        target[...] = total[:, index * padded : (index + 1) * padded].T[: target.shape[0]]


def receive_mlp(odd, kept, turned, core, units):
    rows, columns = kept.shape
    whole = pl.BlockSpec((rows, columns), lambda i, *_: (0, 0))
    found = pl.pallas_call(
        partial(receive_mlp_kernel, columns // 3),
        out_shape=[jax.ShapeDtypeStruct((units, rows), F32)] * 3,
        grid_spec=pltpu.PrefetchScalarGridSpec(
            num_scalar_prefetch=1,
            grid=(1,),
            in_specs=[whole] * 3,
            out_specs=[pl.BlockSpec((units, rows), lambda i, *_: (0, 0))] * 3,
        ),
        compiler_params=params(),
        cost_estimate=cost(0, rows * columns * 10),
    )(odd, kept, turned, core)
    return [f.T for f in found]


def per_device(
    dp_size,
    tensor_size,
    tokens,
    lengths,
    cotangent,
    gain_one,
    gain_two,
    w_query,
    w_key,
    w_value,
    w_gate,
    w_out,
    w_mgate,
    w_mup,
    w_down,
):
    rows, width = tokens.shape
    seq = rows * tensor_size
    heads = w_query.shape[1] // KEY
    units = w_mgate.shape[1]
    shard_rows = w_query.shape[0]
    half_rows = shard_rows // 2
    bits = dp_size.bit_length() - 1
    mine, place = lax.axis_index("dp"), lax.axis_index("tensor")
    inner = (place == 1) | (place == 2)
    odd = (mine & 1) == 1
    up_bits = list(range(1, bits))
    down_bits = up_bits[::-1]

    def add(*arrays):
        return sum(array.astype(F32) for array in arrays)

    def swap_dp(array, mask):
        return lax.ppermute(array, "dp", [(i, i ^ mask) for i in range(dp_size)])

    def move_tensor(array, pairs):
        return lax.ppermute(array, "tensor", pairs)

    def swap_tensor(array, mask):
        return move_tensor(array, [(i, i ^ mask) for i in range(tensor_size)])

    across = [(1, 2), (2, 1)]
    outward = [(1, 0), (2, 3)]
    inward = [(0, 1), (3, 2)]

    def pair(dp_index, tensor_index):
        return dp_index * tensor_size + tensor_index

    top = tensor_size - 1
    to_even = [(pair(m | 1, t), pair(m, t)) for m in range(0, dp_size, 2) for t in range(tensor_size)]
    stay = [(pair(m, t), pair(m, t)) for m in range(0, dp_size, 2) for t in range(tensor_size)]
    to_odd = [(pair(m, t), pair(m | 1, t ^ top)) for m in range(0, dp_size, 2) for t in range(tensor_size)]
    odd_turn = [(pair(m | 1, t), pair(m | 1, t ^ top)) for m in range(0, dp_size, 2) for t in range(tensor_size)]
    both = ("dp", "tensor")

    def hold(array):
        return after(array, token[0])

    def close(*results):
        token[0] = after(token[0], *results)

    def line_out(slots, beside, middle):
        return move_tensor(hold(beside), across), move_tensor(hold(middle), outward)

    def line_all(own, beside, middle, far_inner, far_ends, last):
        return own, beside, jnp.where(inner, far_inner, far_ends), jnp.where(inner, middle, last)

    def first_level(piece, order):
        return swap_dp(piece, 1 << order[0])

    def second_level(piece, order):
        return swap_dp(hold(piece), 1 << order[1])

    def further(pieces, order):
        for bit in order[2:]:
            pieces = pieces + [swap_dp(p, 1 << bit) for p in pieces]
        return pieces

    def to_core(piece):
        return swap_dp(hold(piece), 1)

    def sum_start(high, order):
        return swap_dp(hold(high), 1 << order[-1])

    def sum_split(low, come):
        middle = low.shape[0] // 2
        return [add(low[span], come[span]).astype(BF16) for span in (slice(0, middle), slice(middle, 2 * middle))]

    def sum_end(low, high, order):
        for bit in order[-2:0:-1]:
            low, high = sum_split(low, swap_dp(hold(high), 1 << bit))
        return low, swap_dp(hold(high), 1 << order[0])

    blocks = [
        (chip << 1 | core, part)
        for core in range(2)
        for part, order in ((0, up_bits), (1, down_bits))
        for chip in [sum((i >> j & 1) << (b - 1) for j, b in enumerate(order)) for i in range(dp_size // 2)]
    ]

    sizes = (shard_rows, half_rows)
    aligned = half_rows % LANES == 0
    mine_arg = mine.astype(jnp.int32).reshape(1)

    def to_relative(*arrays):
        if aligned:
            return reorder(own_order_kernel, blocks, sizes, mine_arg, arrays)
        return [
            jnp.concatenate(
                [
                    lax.dynamic_slice_in_dim(a, (mine ^ mask) * shard_rows + part * half_rows, half_rows, -1)
                    for mask, part in blocks
                ],
                -1,
            )
            for a in arrays
        ]

    def to_global(array):
        if aligned:
            return reorder(global_order_kernel, blocks, sizes, mine_arg, [array])[0]
        found = []
        for shard in range(dp_size):
            mask = mine ^ shard
            for part, order in ((0, up_bits), (1, down_bits)):
                chip = sum((mask >> b & 1) << j for j, b in enumerate(order))
                index = (mask & 1) * dp_size + part * (dp_size // 2) + chip
                found.append(lax.dynamic_slice_in_dim(array, index * half_rows, half_rows, -1))
        return jnp.concatenate(found, -1)

    first_row = place * rows
    valid = (first_row + jnp.arange(rows, dtype=jnp.int32) < lengths[0])[:, None]
    head_ids = (place * heads + jnp.arange(heads, dtype=jnp.int32)).astype(F32)
    log_decay = jnp.log(1.0 - jnp.exp2(-5.0 - head_ids))
    place_arg = place.astype(jnp.int32).reshape(1)
    freqs = np.float32(10000.0) ** (-np.arange(KEY // 2, dtype=np.float32) / np.float32(KEY // 2))
    angles = np.arange(seq, dtype=np.float32)[:, None] * freqs[None, :]
    cosines, sines = jnp.asarray(np.cos(angles)), jnp.asarray(np.sin(angles))

    token = [mine_arg]
    spans = slice(0, half_rows), slice(half_rows, shard_rows)
    proj_columns, out_columns = 2 * heads * (KEY + VPAD), heads * VPAD
    padded = -(-units // LANES) * LANES

    sent_up, sent_down = send_attn((w_query, w_key, w_value, w_gate, w_out), heads)
    features_low, gain_first = to_relative(tokens, gain_one[None])
    features = features_low.astype(F32)
    normed_one, inverse_one = norm_parts(features)
    first_own = (normed_one * gain_first).astype(BF16)
    close(sent_up, sent_down, first_own)

    up_one = first_level(hold(sent_up), up_bits)
    down_one = first_level(hold(sent_down), down_bits)
    first_beside = swap_tensor(hold(first_own), 1)
    first_middle = move_tensor(hold(first_own), across)
    local_two = send_mlp((w_mgate, w_mup, hold(w_down)), padded)
    cotangent_low, gain_second = to_relative(hold(cotangent), gain_two[None])
    grad_own = jnp.where(valid, cotangent_low, 0.0)
    grad_final = grad_own.astype(F32)
    core_one = [to_core(sent_up)]
    close(up_one, down_one, first_beside, first_middle, local_two, grad_own, core_one[0])

    up_two, down_two = second_level(sent_up, up_bits), second_level(sent_down, down_bits)
    first_far = line_out(None, first_beside, first_middle)
    core_one.append(to_core(sent_down))
    close(up_two, down_two, *first_far, *core_one)

    up_three, down_three = second_level(up_one, up_bits), second_level(down_one, down_bits)
    first_last = move_tensor(hold(first_far[0]), outward)
    core_two = [to_core(p) for p in (up_one, down_one)]
    close(up_three, down_three, first_last, *core_two)

    up_all = further([sent_up, up_one, up_two, up_three], up_bits)
    down_all = further([sent_down, down_one, down_two, down_three], down_bits)
    up_core = [core_one[0], core_two[0]] + [to_core(p) for p in up_all[2:]]
    down_core = [core_one[1], core_two[1]] + [to_core(p) for p in down_all[2:]]
    mlp_zero = [lax.ppermute(hold(local_two[span]), both, odd_turn + stay) for span in spans]
    grad_beside = swap_tensor(hold(grad_own), 1)
    close(*up_core, *down_core)
    attn_low = up_all + down_all + up_core + down_core
    first_slots = line_all(first_own, first_beside, first_middle, *first_far, first_last)

    orders = up_bits, down_bits

    def level_one(halves):
        return [first_level(half, order) for half, order in zip(halves, orders)]

    def level_two(halves, come):
        firsts = [second_level(half, order) for half, order in zip(halves, orders)]
        found = []
        for half, other, first, order in zip(halves, come, firsts, orders):
            last = swap_dp(after(hold(other), first), 1 << order[1])
            found += further_two([half, other, first, last], order)
        return found

    def further_two(pieces, order):
        for bit in order[2:]:
            pieces = pieces + [swap_dp(p, 1 << bit) for p in pieces]
        return pieces

    grad_core = to_core(grad_own)
    projected = rows_times([hold(first_slots[0]), *first_slots[1:]], attn_low, 0, proj_columns)
    close(*mlp_zero, projected[0], grad_core)

    zero_come = level_one([hold(half) for half in mlp_zero])
    mlp_one = [lax.ppermute(hold(local_two)[spans[0]], both, to_even + to_odd)]
    query, key, value, normed_head, scale_head, mixed = retain(
        [hold(projected[0]), *projected[1:]], place_arg, log_decay, cosines, sines, heads
    )
    (mixed_third,) = rows_back(mixed, (3,), attn_low, proj_columns)
    close(*zero_come, mlp_one[0], grad_beside, mixed_third)

    from_ends = move_tensor(hold(mixed_third), inward)
    mlp_one.append(lax.ppermute(hold(local_two)[spans[1]], both, to_even + to_odd))
    zero_pieces = level_two(mlp_zero, zero_come)
    mixed_second, mixed_first, mixed_own = rows_back(hold(mixed), (2, 1, 0), attn_low, proj_columns)
    mixed_partial = add(mixed_second, from_ends).astype(BF16)
    grad_rows = [grad_own, grad_beside, grad_core, to_core(grad_beside)]
    close(mlp_one[1], *zero_pieces, mixed_partial, grad_rows[3])

    from_inner = move_tensor(hold(mixed_partial), across)
    from_ends = move_tensor(hold(mixed_second), inward)
    one_come = level_one([hold(half) for half in mlp_one])
    close(*one_come, from_inner, from_ends)

    from_beside = swap_tensor(add(mixed_first, hold(from_inner)).astype(BF16), 1)
    from_middle = move_tensor(add(mixed_third, hold(from_ends)).astype(BF16), across)
    mlp_pieces = zero_pieces + level_two(mlp_one, one_come)
    middle = features + add(mixed_own, from_beside, from_middle)
    normed_two, inverse_two = norm_parts(middle)
    second_own = (normed_two * gain_second).astype(BF16)
    close(*mlp_pieces, second_own)

    second_beside = swap_tensor(hold(second_own), 1)
    second_core = to_core(second_own)
    first_part = mlp(hold(second_own), second_core, grad_rows[0], grad_rows[2], mlp_pieces)
    near_core = swap_dp(first_part[7], 1)
    close(second_beside, near_core)

    second_far = to_core(second_beside)
    second_rows = [second_own, second_beside, second_core, second_far]
    second_part = mlp(hold(second_beside), second_far, grad_rows[1], grad_rows[3], None, first_part[8:])
    far_core = swap_dp(second_part[7], 1)
    hidden, grad_gate, grad_up = (
        [first_part[2 * i], second_part[2 * i], first_part[2 * i + 1], second_part[2 * i + 1]] for i in range(3)
    )

    far = add(second_part[6], far_core).astype(BF16)
    near = add(first_part[6], near_core)
    close(far, near)

    def mlp_grad(end, core):
        return mlp_grads(end, core, [hold(second_rows[0]), *second_rows[1:]], grad_rows, grad_gate, grad_up, hidden)

    second_back = swap_tensor(hold(far), 1)
    high = [mlp_grad(1, 0), mlp_grad(1, 1)]
    down_own, down_other = mlp_down([hold(hidden[0]), *hidden[1:]], first_part[10])
    close(second_back, *high[0], *high[1], down_own)

    attn_own, grad_middle, grad_gain_two = middle_back(near, hold(second_back), middle, grad_own, gain_second)
    attn_beside = swap_tensor(attn_own, 1)
    attn_second = swap_tensor(attn_own, 2)
    come = [[sum_start(high[0][0], up_bits), sum_start(high[0][1], down_bits)]]
    come.append(
        [sum_start(after(high[1][0], come[0][0]), up_bits), sum_start(after(high[1][1], come[0][1]), down_bits)]
    )
    low = [mlp_grad(0, 0), mlp_grad(0, 1)]
    down_core = to_core(down_other)
    splits = [[sum_split(low[0][part], come[0][part]) for part in range(2)]]
    close(attn_beside, attn_second, *come[1], *low[1], down_core, *splits[0][0], *splits[0][1])

    attn_middle = move_tensor(hold(attn_own), across)
    attn_last = move_tensor(hold(attn_second), outward)
    splits.append([sum_split(low[1][part], hold(come[1][part])) for part in range(2)])

    def mlp_end(core):
        return [sum_end(*splits[core][part], orders[part]) for part in range(2)]

    def mlp_sum(ends):
        return [add(*end).astype(BF16) for end in ends]

    mlp_total = [mlp_sum(mlp_end(0))]
    grad_mixed = rows_times([hold(attn_own), attn_beside, attn_second], attn_low, proj_columns, out_columns)
    down_sum = add(down_own, hold(down_core))
    down_sent = down_sum[rows:].astype(BF16)
    close(attn_middle, attn_last, *mlp_total[0], grad_mixed[0])
    attn_slots = attn_own, attn_beside, attn_second, jnp.where(inner, attn_middle, hold(attn_last))

    grad_mixed = grad_mixed + rows_times([attn_slots[3]], attn_low, proj_columns, out_columns)
    grad_turn = [
        lax.ppermute(after(t, grad_mixed[3]), both, [(b, a) for a, b in odd_turn]) for t in mlp_total[0]
    ]
    grad_proj = retain_back(
        grad_mixed, projected, normed_head, scale_head, query, key, value, place_arg, log_decay, cosines, sines, heads
    )
    back_third, gain_third = rows_back(grad_proj, (3,), attn_low, 0, first_slots[3:])
    mlp_ends = mlp_end(1)
    close(*grad_turn, back_third, mlp_ends[0][1], mlp_ends[1][1])

    from_ends = move_tensor(hold(back_third), inward)
    to_owner = [(b, a) for a, b in to_even + to_odd]
    mlp_total.append(mlp_sum([(low_part, hold(come_part)) for low_part, come_part in mlp_ends]))
    grad_core = [lax.ppermute(mlp_total[1][0], both, to_owner)]
    other_high = attn_grads(1, first_slots, hold(grad_proj))
    back_second, gain_second_part = rows_back(after(grad_proj, other_high), (2,), attn_low, 0, first_slots[2:3])
    other_low = attn_grads(0, first_slots, after(grad_proj, back_second))
    back_partial = add(back_second, from_ends).astype(BF16)
    close(back_partial, other_low, grad_core[0])

    from_inner = move_tensor(hold(back_partial), across)
    from_ends = move_tensor(hold(back_second), inward)
    core_high, core_low = to_core(other_high), to_core(other_low)
    out_other_high = attn_grads(1, attn_slots, hold(mixed))
    out_other_low = attn_grads(0, attn_slots, after(mixed, out_other_high))
    back_own, back_first, gain_near = rows_back(after(grad_proj, out_other_low), (0, 1), attn_low, 0, first_slots[:2])
    up_high, down_high = attn_grads(1, first_slots, after(grad_proj, back_own), core_high)
    proj_come = swap_dp(up_high, 1 << up_bits[-1]), swap_dp(down_high, 1 << down_bits[-1])
    close(from_inner, from_ends, back_own, core_low, out_other_low, up_high)

    from_beside = swap_tensor(add(back_first, hold(from_inner)).astype(BF16), 1)
    from_middle = move_tensor(add(back_third, hold(from_ends)).astype(BF16), across)
    out_core_high, out_core_low = to_core(out_other_high), to_core(out_other_low)
    up_low, down_low = attn_grads(0, first_slots, hold(grad_proj), core_low)
    out_up_high, out_down_high = attn_grads(1, attn_slots, after(mixed, up_low), out_core_high)
    out_up_low, out_down_low = attn_grads(0, attn_slots, after(mixed, out_up_high), out_core_low)
    gain_parts = gain_third[0] + gain_second_part[0] + hold(gain_near)[0]
    gains = to_global(jnp.stack([gain_parts / gain_first[0], grad_gain_two[0]]))
    gains = gains + swap_dp(gains, 1)
    close(from_beside, from_middle, *proj_come, gains, up_low, out_up_low)

    down_beside = swap_tensor(hold(down_sent), 1)
    proj_up = sum_end(*sum_split(up_low, hold(proj_come[0])), up_bits)
    proj_down = sum_end(*sum_split(down_low, hold(proj_come[1])), down_bits)
    out_come = sum_start(out_up_high, up_bits), sum_start(out_down_high, down_bits)
    grad_core.append(lax.ppermute(after(mlp_total[1][1], out_come[0]), both, to_owner))
    grad_first = add(back_own, hold(from_beside), from_middle)
    grad_tokens = grad_middle + norm_back(normed_one, inverse_one, grad_first, gain_first)
    grad_tokens = to_global(grad_tokens.astype(BF16))
    close(*proj_up, *proj_down, *out_come, grad_core[1], down_beside, grad_tokens)

    final = middle + down_sum[:rows] + hold(down_beside).astype(F32)
    output = to_global(jnp.where(valid, final, 0.0).astype(BF16))
    sum_mgate, sum_mup, sum_down = receive_mlp(
        (mine & 1).astype(jnp.int32).reshape(1),
        jnp.concatenate([hold(t) for t in mlp_total[0]], 0),
        jnp.concatenate(grad_turn, 0),
        jnp.concatenate(grad_core, 0),
        units,
    )
    out_up = sum_end(*sum_split(out_up_low, hold(out_come[0])), up_bits)
    out_down = sum_end(*sum_split(out_down_low, hold(out_come[1])), down_bits)
    gains = hold(gains)
    for other in (1, 2):
        gains = gains + swap_tensor(gains, other)
    for bit in range(1, bits):
        gains = gains + swap_dp(gains, 1 << bit)
    sum_query, sum_key, sum_value, sum_gate = receive_attn(
        (hold(proj_up[0]), proj_up[1], *proj_down), 2, 2, heads
    )
    (sum_out,) = receive_attn((*out_up, *out_down), 0, 1, heads)
    return (
        output,
        grad_tokens,
        gains[0],
        gains[1],
        sum_query,
        sum_key,
        sum_value,
        sum_gate,
        sum_out,
        sum_mgate,
        sum_mup,
        sum_down,
    )


def solution(mesh):
    rows = P(("dp", "tensor"), None)
    block = P("dp", "tensor")
    return jax.shard_map(
        partial(per_device, mesh.shape["dp"], mesh.shape["tensor"]),
        mesh=mesh,
        in_specs=(rows, P("dp"), rows, P(), P()) + (block,) * 8,
        out_specs=(rows, rows, P(), P()) + (block,) * 8,
        check_vma=False,
    )
```

```python
from functools import partial

import jax
import jax.numpy as jnp
import numpy as np
from jax import lax
from jax.experimental import pallas as pl
from jax.experimental.pallas import tpu as pltpu
from jax.sharding import PartitionSpec as P

KEY = 256
VAL = 432
VPAD = 512
LANES = 128
EPS = 1e-05
HEAD_EPS = 1.0
F32 = jnp.float32
BF16 = jnp.bfloat16
VMEM_LIMIT = 48 * 1024 * 1024


def times_plain(left, right):
    return jnp.dot(left, right, preferred_element_type=F32)


def times_left(left, right):
    return lax.dot_general(left, right, (((0,), (0,)), ((), ())), preferred_element_type=F32)


def times_right(left, right):
    return lax.dot_general(left, right, (((1,), (1,)), ((), ())), preferred_element_type=F32)


def after(array, *earlier):
    return lax.optimization_barrier((array, *earlier))[0]


def params(**more):
    return pltpu.CompilerParams(vmem_limit_bytes=VMEM_LIMIT, **more)


def cost(flops, moved):
    return pl.CostEstimate(flops=flops // 64, bytes_accessed=moved // 64, transcendentals=0)


def norm_parts(features):
    centred = features - jnp.mean(features, -1, keepdims=True)
    inverse = lax.rsqrt(jnp.mean(centred * centred, -1, keepdims=True) + EPS)
    return centred * inverse, inverse


def norm_back(normed, inverse, grad, gain):
    scaled = grad * gain
    return inverse * (
        scaled
        - jnp.mean(scaled, -1, keepdims=True)
        - normed * jnp.mean(scaled * normed, -1, keepdims=True)
    )


def decay_rows(log_decay, rows, width):
    query = lax.broadcasted_iota(jnp.int32, (rows, width), 0) + (width - rows)
    key = lax.broadcasted_iota(jnp.int32, (rows, width), 1)
    spacing = query - key
    factor = jnp.exp(log_decay * jnp.maximum(spacing, 0).astype(F32))
    return jnp.where(spacing >= 0, factor, 0.0)


def retain_kernel(slots, rows, place_ref, decay_ref, *refs):
    ins, (cos_ref, sin_ref), outs = refs[: 4 * slots], refs[4 * slots : 4 * slots + 2], refs[4 * slots + 2 :]
    query_ref, key_ref, value_ref, normed_ref, scale_ref, mixed_ref, factor_ref, kept_ref = outs
    head = pl.program_id(0)
    place = place_ref[0]
    seq = slots * rows
    half = KEY // 2
    for slot in range(slots):
        start = pl.multiple_of((slot ^ place) * rows, rows)
        cosines, sines = cos_ref[pl.ds(start, rows), :], sin_ref[pl.ds(start, rows), :]
        for source, target, scale in ((ins[slot], query_ref, 1.0), (ins[slots + slot], key_ref, KEY**-0.5)):
            low = source[:, :half].astype(F32)
            high = source[:, half:].astype(F32)
            target[pl.ds(start, rows), :half] = ((low * cosines - high * sines) * scale).astype(BF16)
            target[pl.ds(start, rows), half:] = ((high * cosines + low * sines) * scale).astype(BF16)
        value_ref[pl.ds(start, rows), :] = ins[2 * slots + slot][...]
    factor_ref[...] = decay_rows(decay_ref[head], rows, seq)
    for block in range(slots):
        width = (block + 1) * rows
        scores = times_right(query_ref[block * rows : width, :], key_ref[:width, :])
        weights = (scores * factor_ref[:, seq - width :]).astype(BF16)
        kept_ref[block * rows : width, :] = times_plain(weights, value_ref[:width, :])
    inside = lax.broadcasted_iota(jnp.int32, (rows, VPAD), 1) < VAL
    for slot in range(slots):
        start = pl.multiple_of((slot ^ place) * rows, rows)
        kept = kept_ref[pl.ds(start, rows), :]
        mean = jnp.sum(kept, -1, keepdims=True) / VAL
        centred = jnp.where(inside, kept - mean, 0.0)
        inverse = lax.rsqrt(jnp.sum(centred * centred, -1, keepdims=True) / VAL + HEAD_EPS)
        normed = centred * inverse
        gate = ins[3 * slots + slot][...].astype(F32)
        mixed = gate * jax.nn.sigmoid(gate) * normed
        mixed_ref[slot * rows : (slot + 1) * rows, :] = mixed.astype(BF16)
        normed_ref[slot * rows : (slot + 1) * rows, :] = normed.astype(BF16)
        scale_ref[slot * rows : (slot + 1) * rows, :] = jnp.broadcast_to(inverse, (rows, 128))


def slot_specs(rows, heads):
    first_value = 2 * heads * KEY // VPAD
    return (
        pl.BlockSpec((rows, KEY), lambda h, *_: (0, h)),
        pl.BlockSpec((rows, KEY), lambda h, *_: (0, heads + h)),
        pl.BlockSpec((rows, VPAD), lambda h, *_: (0, first_value + h)),
        pl.BlockSpec((rows, VPAD), lambda h, *_: (0, first_value + heads + h)),
    )


def retain(projected, place, log_decay, cosines, sines, heads):
    slots, rows = len(projected), projected[0].shape[0]
    seq = slots * rows
    specs = slot_specs(rows, heads)
    table = pl.BlockSpec((seq, KEY // 2), lambda h, *_: (0, 0))

    def column(width):
        return pl.BlockSpec((seq, width), lambda h, *_: (0, h))

    return pl.pallas_call(
        partial(retain_kernel, slots, rows),
        out_shape=(
            jax.ShapeDtypeStruct((seq, heads * KEY), BF16),
            jax.ShapeDtypeStruct((seq, heads * KEY), BF16),
            jax.ShapeDtypeStruct((seq, heads * VPAD), BF16),
            jax.ShapeDtypeStruct((seq, heads * VPAD), BF16),
            jax.ShapeDtypeStruct((seq, heads * 128), F32),
            jax.ShapeDtypeStruct((seq, heads * VPAD), BF16),
        ),
        grid_spec=pltpu.PrefetchScalarGridSpec(
            num_scalar_prefetch=2,
            grid=(heads,),
            in_specs=[spec for spec in specs for _ in range(slots)] + [table, table],
            out_specs=[column(KEY), column(KEY), column(VPAD), column(VPAD), column(128), column(VPAD)],
            scratch_shapes=[pltpu.VMEM((rows, seq), F32), pltpu.VMEM((seq, VPAD), F32)],
        ),
        compiler_params=pltpu.CompilerParams(vmem_limit_bytes=VMEM_LIMIT),
        cost_estimate=cost(heads * seq * seq * (KEY + VPAD), heads * seq * 9000),
    )(place, log_decay, *(projected * 4), cosines, sines)


def retain_back_kernel(slots, rows, heads, place_ref, decay_ref, *refs):
    grads, gates, rest = refs[:slots], refs[slots : 2 * slots], refs[2 * slots :]
    (normed_ref, scale_ref, query_ref, key_ref, value_ref, cos_ref, sin_ref, out_ref, factor_ref, ret_ref, key_sum, value_sum) = rest
    head = pl.program_id(0)
    place = place_ref[0]
    seq = slots * rows
    half = KEY // 2
    query_col = pl.multiple_of(head * KEY, KEY)
    key_col = pl.multiple_of((heads + head) * KEY, KEY)
    value_col = pl.multiple_of(2 * heads * KEY + head * VPAD, VPAD)
    gate_col = pl.multiple_of(2 * heads * KEY + (heads + head) * VPAD, VPAD)
    inside = lax.broadcasted_iota(jnp.int32, (rows, VPAD), 1) < VAL
    for slot in range(slots):
        start = pl.multiple_of((slot ^ place) * rows, rows)
        span = slice(slot * rows, (slot + 1) * rows)
        grad, gate = grads[slot][...].astype(F32), gates[slot][...].astype(F32)
        normed, inverse = normed_ref[span, :].astype(F32), scale_ref[span, :1]
        sig = jax.nn.sigmoid(gate)
        out_ref[span, pl.ds(gate_col, VPAD)] = (grad * normed * sig * (1.0 + gate * (1.0 - sig))).astype(BF16)
        grad_normed = grad * gate * sig
        mean = jnp.sum(grad_normed, -1, keepdims=True) / VAL
        along = jnp.sum(grad_normed * normed, -1, keepdims=True) / VAL
        grad_ret = inverse * (grad_normed - mean - normed * along)
        ret_ref[pl.ds(start, rows), :] = jnp.where(inside, grad_ret, 0.0).astype(BF16)
    factor_ref[...] = decay_rows(decay_ref[head], rows, seq)
    key_sum[...] = jnp.zeros_like(key_sum)
    value_sum[...] = jnp.zeros_like(value_sum)
    for block in range(slots):
        width = (block + 1) * rows
        span = slice(block * rows, width)
        query, ret, keys = query_ref[span, :], ret_ref[span, :], key_ref[:width, :]
        factor = factor_ref[:, seq - width :]
        weights = (times_right(query, keys) * factor).astype(BF16)
        grad_scores = (times_right(ret, value_ref[:width, :]) * factor).astype(BF16)
        value_sum[:width, :] += times_left(weights, ret)
        key_sum[:width, :] += times_left(grad_scores, query)
        grad_query = times_plain(grad_scores, keys)
        row = pl.multiple_of((block ^ place) * rows, rows)
        cosines, sines = cos_ref[span, :], sin_ref[span, :]
        low, high = grad_query[:, :half], grad_query[:, half:]
        out_ref[pl.ds(row, rows), pl.ds(query_col, half)] = (low * cosines + high * sines).astype(BF16)
        out_ref[pl.ds(row, rows), pl.ds(pl.multiple_of(query_col + half, half), half)] = (
            high * cosines - low * sines
        ).astype(BF16)
    for block in range(slots):
        span = slice(block * rows, (block + 1) * rows)
        row = pl.multiple_of((block ^ place) * rows, rows)
        cosines, sines = cos_ref[span, :], sin_ref[span, :]
        low, high = key_sum[span, :half] * KEY**-0.5, key_sum[span, half:] * KEY**-0.5
        out_ref[pl.ds(row, rows), pl.ds(key_col, half)] = (low * cosines + high * sines).astype(BF16)
        out_ref[pl.ds(row, rows), pl.ds(pl.multiple_of(key_col + half, half), half)] = (
            high * cosines - low * sines
        ).astype(BF16)
        out_ref[pl.ds(row, rows), pl.ds(value_col, VPAD)] = value_sum[span, :].astype(BF16)


def retain_back(grads, projected, normed, scale, query, key, value, place, log_decay, cosines, sines, heads):
    slots, rows = len(projected), projected[0].shape[0]
    seq = slots * rows
    columns = 2 * heads * (KEY + VPAD)
    table = pl.BlockSpec((seq, KEY // 2), lambda h, *_: (0, 0))

    def column(width):
        return pl.BlockSpec((seq, width), lambda h, *_: (0, h))

    return pl.pallas_call(
        partial(retain_back_kernel, slots, rows, heads),
        out_shape=jax.ShapeDtypeStruct((seq, columns), BF16),
        grid_spec=pltpu.PrefetchScalarGridSpec(
            num_scalar_prefetch=2,
            grid=(heads,),
            in_specs=[pl.BlockSpec((rows, VPAD), lambda h, *_: (0, h))] * slots
            + [slot_specs(rows, heads)[3]] * slots
            + [column(VPAD), column(128), column(KEY), column(KEY), column(VPAD), table, table],
            out_specs=pl.BlockSpec((seq, columns), lambda h, *_: (0, 0)),
            scratch_shapes=[
                pltpu.VMEM((rows, seq), F32),
                pltpu.VMEM((seq, VPAD), BF16),
                pltpu.VMEM((seq, KEY), F32),
                pltpu.VMEM((seq, VPAD), F32),
            ],
        ),
        compiler_params=pltpu.CompilerParams(vmem_limit_bytes=VMEM_LIMIT),
        cost_estimate=cost(heads * seq * seq * (3 * KEY + 2 * VPAD), heads * seq * 10000),
    )(place, log_decay, *grads, *projected, normed, scale, query, key, value, cosines, sines)


def rows_kernel(slots, pieces, *refs):
    lefts, weights, outs = refs[:slots], refs[slots : slots + pieces], refs[slots + pieces :]
    left = jnp.concatenate([ref[...] for ref in lefts], 0)
    result = times_plain(left, jnp.concatenate([ref[...] for ref in weights], 0)).astype(BF16)
    rows = lefts[0].shape[0]
    for slot in range(slots):
        outs[slot][...] = result[slot * rows : (slot + 1) * rows]


def rows_times(lefts, pieces, first, columns, tile=512):
    rows, width = lefts[0].shape
    return pl.pallas_call(
        partial(rows_kernel, len(lefts), len(pieces)),
        out_shape=[jax.ShapeDtypeStruct((rows, columns), BF16)] * len(lefts),
        grid=(columns // tile,),
        in_specs=[pl.BlockSpec((rows, width), lambda n: (0, 0))] * len(lefts)
        + [pl.BlockSpec((p.shape[0], tile), lambda n: (0, n + first // tile)) for p in pieces],
        out_specs=[pl.BlockSpec((rows, tile), lambda n: (0, n))] * len(lefts),
        compiler_params=params(),
        cost_estimate=cost(2 * len(lefts) * rows * width * columns, 2 * width * columns),
    )(*lefts, *pieces)


def rows_back_kernel(slots, pieces, weigh, *refs):
    lefts, weights, rest = refs[:slots], refs[slots : slots + pieces], refs[slots + pieces :]
    total = rest[-1]
    step = pl.program_id(0)
    left = jnp.concatenate([ref[...] for ref in lefts], 0)
    part = times_right(left, jnp.concatenate([ref[...] for ref in weights], 0))

    @pl.when(step == 0)
    def _():
        total[...] = part

    @pl.when(step > 0)
    def _():
        total[...] += part

    @pl.when(step == pl.num_programs(0) - 1)
    def _():
        rows = lefts[0].shape[0]
        for slot in range(slots):
            rest[weigh * slots + slot][...] = total[slot * rows : (slot + 1) * rows, :].astype(BF16)
        if weigh:
            other = jnp.concatenate([ref[...] for ref in rest[:slots]], 0).astype(F32)
            along = jnp.sum(total[...] * other, 0, keepdims=True)
            rest[2 * slots][...] = jnp.broadcast_to(along, (8, along.shape[1]))


def rows_back(left, slots, pieces, first=0, weigh=(), tile=512):
    rows = left.shape[0] // 4
    columns = left.shape[1]
    width = sum(p.shape[0] for p in pieces)
    whole = pl.BlockSpec((rows, width), lambda k: (0, 0))
    return pl.pallas_call(
        partial(rows_back_kernel, len(slots), len(pieces), 1 if weigh else 0),
        out_shape=[jax.ShapeDtypeStruct((rows, width), BF16)] * len(slots)
        + ([jax.ShapeDtypeStruct((8, width), F32)] if weigh else []),
        grid=(columns // tile,),
        in_specs=[pl.BlockSpec((rows, tile), partial(lambda s, k: (s, k), s)) for s in slots]
        + [pl.BlockSpec((p.shape[0], tile), lambda k: (0, k + first // tile)) for p in pieces]
        + [whole] * len(weigh),
        out_specs=[whole] * len(slots) + ([pl.BlockSpec((8, width), lambda k: (0, 0))] if weigh else []),
        scratch_shapes=[pltpu.VMEM((len(slots) * rows, width), F32)],
        compiler_params=params(),
        cost_estimate=cost(2 * len(slots) * rows * width * columns, 2 * width * columns),
    )(*([left] * len(slots)), *pieces, *weigh)


def turn(array):
    middle = array.shape[1] // 2
    return jnp.concatenate([array[:, middle:], array[:, :middle]], 1)


def mlp_kernel(pieces, units, own_ref, other_ref, own_grad_ref, other_grad_ref, *refs):
    sources, outs, weights = refs[:pieces], refs[pieces : pieces + 8], refs[pieces + 8 : pieces + 11]
    semaphores = refs[pieces + 11]
    copies = []
    for part, target in enumerate(weights):
        place = 0
        for index, source in enumerate(sources):
            height = source.shape[0]
            copy = pltpu.make_async_copy(
                source.at[:, pl.ds(part * units, units)],
                target.at[pl.ds(place, height), :],
                semaphores.at[part, index],
            )
            copy.start()
            copies.append(copy)
            place += height

    def ready(part):
        for copy in copies[part * pieces : (part + 1) * pieces]:
            copy.wait()

    mlp_body(ready, own_ref, other_ref, own_grad_ref, other_grad_ref, weights, outs)


def mlp_again_kernel(own_ref, other_ref, own_grad_ref, other_grad_ref, *refs):
    mlp_body(lambda part: None, own_ref, other_ref, own_grad_ref, other_grad_ref, refs[:3], refs[3:])


def mlp_body(ready, own_ref, other_ref, own_grad_ref, other_grad_ref, weights, outs):
    gate_ref, up_ref, down_ref = weights
    rows = own_ref.shape[0]
    left = jnp.concatenate([own_ref[...], turn(other_ref[...])], 0)
    grad = jnp.concatenate([own_grad_ref[...], turn(other_grad_ref[...])], 0)
    ready(0)
    gate = times_plain(left, gate_ref[...])
    ready(1)
    up = times_plain(left, up_ref[...])
    ready(2)
    grad_hidden = times_plain(grad, down_ref[...])
    below = 0.5 + 0.5 * lax.erf(gate * (0.5**0.5))
    density = jnp.exp(-0.5 * gate * gate) * 0.3989422804014327
    smooth = gate * below
    hidden = (smooth * up).astype(BF16)
    grad_gate = (grad_hidden * up * (below + gate * density)).astype(BF16)
    grad_up = (grad_hidden * smooth).astype(BF16)
    for slot in range(2):
        span = slice(slot * rows, (slot + 1) * rows)
        outs[slot][...] = hidden[span]
        outs[2 + slot][...] = grad_gate[span]
        outs[4 + slot][...] = grad_up[span]
    back = times_right(grad_gate, gate_ref[...]) + times_right(grad_up, up_ref[...])
    outs[6][...] = back[:rows].astype(BF16)
    outs[7][...] = turn(back[rows:]).astype(BF16)


def mlp(own, other, own_grad, other_grad, pieces, weights=None):
    rows, width = own.shape
    units = weights[0].shape[1] if weights else pieces[0].shape[1] // 3
    narrow = pl.BlockSpec((rows, units), lambda i: (0, 0))
    wide = pl.BlockSpec((rows, width), lambda i: (0, 0))
    whole = pl.BlockSpec((width, units), lambda i: (0, 0))
    small, large = jax.ShapeDtypeStruct((rows, units), BF16), jax.ShapeDtypeStruct((rows, width), BF16)
    handed = [] if weights else [jax.ShapeDtypeStruct((width, units), BF16)] * 3
    return pl.pallas_call(
        mlp_again_kernel if weights else partial(mlp_kernel, len(pieces), units),
        out_shape=[small] * 6 + [large] * 2 + handed,
        grid=(1,),
        in_specs=[wide] * 4
        + ([whole] * 3 if weights else [pl.BlockSpec(memory_space=pl.ANY)] * len(pieces)),
        out_specs=[narrow] * 6 + [wide] * 2 + [whole] * len(handed),
        scratch_shapes=[] if weights else [pltpu.SemaphoreType.DMA((3, len(pieces)))],
        compiler_params=params(),
        cost_estimate=cost(2 * 2 * rows * width * units * 5, 6 * width * units),
    )(own, other, own_grad, other_grad, *(weights or pieces))


def down_kernel(*refs):
    lefts, weight, outs = refs[:4], refs[4], refs[5:]
    for core in range(2):
        left = jnp.concatenate([lefts[2 * core][...], lefts[2 * core + 1][...]], 0)
        result = times_right(left, weight[...])
        outs[core][...] = (turn(result) if core else result).astype(BF16)


def mlp_down(hidden, weight):
    rows, units = hidden[0].shape
    width = weight.shape[0]
    whole = pl.BlockSpec((rows, units), lambda n: (0, 0))
    out = pl.BlockSpec((2 * rows, width), lambda n: (0, 0))
    return pl.pallas_call(
        down_kernel,
        out_shape=[jax.ShapeDtypeStruct((2 * rows, width), BF16)] * 2,
        grid=(1,),
        in_specs=[whole] * 4 + [pl.BlockSpec((width, units), lambda n: (0, 0))],
        out_specs=[out] * 2,
        compiler_params=params(),
        cost_estimate=cost(8 * rows * width * units, 2 * width * units),
    )(*hidden, weight)


def mlp_grad_kernel(*refs):
    lefts, grads, rights, outs = refs[:4], refs[4:8], refs[8:20], refs[20:]
    left = jnp.concatenate([ref[...] for ref in lefts], 0)
    grad = jnp.concatenate([ref[...] for ref in grads], 0)
    parts = []
    for index, rows in enumerate((left, left, grad)):
        right = jnp.concatenate([ref[...] for ref in rights[4 * index : 4 * index + 4]], 0)
        parts.append(times_left(rows, right).astype(BF16))
    result = jnp.concatenate(parts, 1)
    for part in range(2):

        @pl.when(pl.program_id(0) == part)
        def _():
            outs[part][...] = result


def mlp_grads(end, core, lefts, grads, grad_gate, grad_up, hidden):
    rows, width = lefts[0].shape
    units = hidden[0].shape[1]
    tile = width // 8

    def column(other, step):
        return (0, (core ^ other) * 4 + step * 2 + end)

    narrow = [pl.BlockSpec((rows, tile), partial(column, other)) for other in (0, 0, 1, 1)]
    whole = pl.BlockSpec((rows, units), lambda i: (0, 0))
    return pl.pallas_call(
        mlp_grad_kernel,
        out_shape=[jax.ShapeDtypeStruct((tile, 3 * units), BF16)] * 2,
        grid=(2,),
        in_specs=narrow * 2 + [whole] * 12,
        out_specs=[pl.BlockSpec((tile, 3 * units), lambda i: (0, 0))] * 2,
        compiler_params=params(),
        cost_estimate=cost(2 * rows * width * units * 3, 2 * width * units),
    )(*lefts, *grads, *grad_gate, *grad_up, *hidden)


def attn_grad_kernel(*refs):
    left = jnp.concatenate([ref[...] for ref in refs[:4]], 0)
    refs[5][...] = times_left(left, refs[4][...]).astype(BF16)


def attn_grad_add_kernel(*refs):
    left = jnp.concatenate([ref[...] for ref in refs[:4]], 0)
    result = (times_left(left, refs[4][...]) + refs[5][...].astype(F32)).astype(BF16)
    for part in range(2):

        @pl.when(pl.program_id(0) == part)
        def _():
            refs[6 + part][...] = result


def attn_grads(end, lefts, right, other=None):
    rows, width = lefts[0].shape
    columns = right.shape[1]
    tile = width // 8
    core = 1 if other is None else 0
    narrow = pl.BlockSpec((rows, tile), lambda i: (0, core * 4 + 2 * i + end))
    block = pl.BlockSpec((tile, columns), lambda i: (i, 0))
    whole = pl.BlockSpec((tile, columns), lambda i: (0, 0))
    return pl.pallas_call(
        attn_grad_kernel if core else attn_grad_add_kernel,
        out_shape=jax.ShapeDtypeStruct((2 * tile, columns), BF16)
        if core
        else [jax.ShapeDtypeStruct((tile, columns), BF16)] * 2,
        grid=(2,),
        in_specs=[narrow] * 4 + [pl.BlockSpec(right.shape, lambda i: (0, 0))] + ([] if core else [block]),
        out_specs=block if core else [whole] * 2,
        compiler_params=params(),
        cost_estimate=cost(2 * rows * width * columns, width * columns),
    )(*lefts, right, *([] if core else [other]))


def own_order_kernel(blocks, sizes, mine_ref, *refs):
    (shard_rows, half_rows), count = sizes, len(refs) // 2
    for index, (mask, part) in enumerate(blocks):
        start = pl.multiple_of((mine_ref[0] ^ mask) * shard_rows + part * half_rows, half_rows)
        for source, target in zip(refs[:count], refs[count:]):
            target[:, index * half_rows : (index + 1) * half_rows] = source[:, pl.ds(start, half_rows)]


def global_order_kernel(blocks, sizes, mine_ref, source, target):
    shard_rows, half_rows = sizes
    for index, (mask, part) in enumerate(blocks):
        start = pl.multiple_of((mine_ref[0] ^ mask) * shard_rows + part * half_rows, half_rows)
        target[:, pl.ds(start, half_rows)] = source[:, index * half_rows : (index + 1) * half_rows]


def reorder(kernel, blocks, sizes, mine, arrays):
    specs = [pl.BlockSpec(a.shape, lambda i, *_: (0, 0)) for a in arrays]
    return pl.pallas_call(
        partial(kernel, blocks, sizes),
        out_shape=[jax.ShapeDtypeStruct(a.shape, a.dtype) for a in arrays],
        grid_spec=pltpu.PrefetchScalarGridSpec(num_scalar_prefetch=1, grid=(1,), in_specs=specs, out_specs=specs),
        compiler_params=params(),
    )(mine, *arrays)


def middle_back_kernel(near, come, middle, grad_final, gain, low, full, gain_sum):
    grad = near[...] + come[...].astype(F32)
    normed, inverse = norm_parts(middle[...])
    total = grad_final[...].astype(F32) + norm_back(normed, inverse, grad, gain[...])
    low[...] = total.astype(BF16)
    full[...] = total

    @pl.when(pl.program_id(0) == 0)
    def _():
        gain_sum[...] = jnp.zeros_like(gain_sum)

    gain_sum[...] += jnp.sum(grad * normed, 0, keepdims=True)


def middle_back(near, come, middle, grad_final, gain):
    rows, width = near.shape
    tile = 64
    block = pl.BlockSpec((tile, width), lambda i: (i, 0))
    vector = pl.BlockSpec((1, width), lambda i: (0, 0))
    return pl.pallas_call(
        middle_back_kernel,
        out_shape=[
            jax.ShapeDtypeStruct((rows, width), BF16),
            jax.ShapeDtypeStruct((rows, width), F32),
            jax.ShapeDtypeStruct((1, width), F32),
        ],
        grid=(rows // tile,),
        in_specs=[block] * 4 + [vector],
        out_specs=[block, block, vector],
        compiler_params=params(),
        cost_estimate=cost(0, rows * width * 18),
    )(near, come, middle, grad_final, gain)


def widen(array, height):
    return jnp.concatenate([array, jnp.zeros((height - array.shape[0], array.shape[1]), array.dtype)], 0)


def send_attn_kernel(heads, *refs):
    sources, targets = refs[:5], refs[5:]
    half = targets[0].shape[0]
    spans = [slice(part * half, (part + 1) * half) for part in range(2)]
    for index, source in enumerate(sources):
        if index < 2:
            for span, target in zip(spans, targets):
                target[:, index * heads * KEY : (index + 1) * heads * KEY] = source[span, :].astype(BF16)
        else:
            for head in range(heads):
                column = 2 * heads * KEY + ((index - 2) * heads + head) * VPAD
                block = widen(source[head * VAL : (head + 1) * VAL, :], VPAD).T.astype(BF16)
                for span, target in zip(spans, targets):
                    target[:, column : column + VPAD] = block[span, :]


def send_attn(weights, heads):
    half = weights[0].shape[0] // 2
    columns = heads * (2 * KEY + 3 * VPAD)
    arrays = [*weights[:2], *(w.T for w in weights[2:])]
    return pl.pallas_call(
        partial(send_attn_kernel, heads),
        out_shape=[jax.ShapeDtypeStruct((half, columns), BF16)] * 2,
        grid=(1,),
        in_specs=[pl.BlockSpec(w.shape, lambda i: (0, 0)) for w in arrays],
        out_specs=[pl.BlockSpec((half, columns), lambda i: (0, 0))] * 2,
        compiler_params=params(),
        cost_estimate=cost(0, half * columns * 12),
    )(*arrays)


def send_mlp_kernel(padded, *refs):
    target = refs[-1]
    for index, source in enumerate(refs[:-1]):
        target[:, index * padded : (index + 1) * padded] = widen(source[...], padded).T.astype(BF16)


def send_mlp(weights, padded):
    rows, units = weights[0].shape
    return pl.pallas_call(
        partial(send_mlp_kernel, padded),
        out_shape=jax.ShapeDtypeStruct((rows, len(weights) * padded), BF16),
        grid=(1,),
        in_specs=[pl.BlockSpec((units, rows), lambda i: (0, 0))] * len(weights),
        out_specs=pl.BlockSpec((rows, len(weights) * padded), lambda i: (0, 0)),
        compiler_params=params(),
        cost_estimate=cost(0, rows * padded * 18),
    )(*(w.T for w in weights))


def receive_kernel(narrow, heads, *refs):
    targets = refs[4:]
    total = jnp.concatenate(
        [refs[2 * part][...].astype(F32) + refs[2 * part + 1][...].astype(F32) for part in range(2)], 0
    )
    column = 0
    for index, target in enumerate(targets):
        if index < narrow:
            target[...] = total[:, column : column + heads * KEY]
            column += heads * KEY
        else:
            for head in range(heads):
                target[head * VAL : (head + 1) * VAL, :] = total[:, column : column + VPAD].T[:VAL]
                column += VPAD


def receive_attn(parts, narrow, wide, heads):
    rows = 2 * parts[0].shape[0]
    shapes = [(rows, heads * KEY)] * narrow + [(heads * VAL, rows)] * wide
    found = pl.pallas_call(
        partial(receive_kernel, narrow, heads),
        out_shape=[jax.ShapeDtypeStruct(s, F32) for s in shapes],
        grid=(1,),
        in_specs=[pl.BlockSpec(p.shape, lambda i: (0, 0)) for p in parts],
        out_specs=[pl.BlockSpec(s, lambda i: (0, 0)) for s in shapes],
        compiler_params=params(),
        cost_estimate=cost(0, rows * sum(s[0] for s in shapes) * 4),
    )(*parts)
    return [*found[:narrow], *(f.T for f in found[narrow:])]


def receive_mlp_kernel(padded, odd_ref, kept, turned, core, *targets):
    first = jnp.where(odd_ref[0] == 1, turned[...], kept[...]).astype(F32)
    total = first + core[...].astype(F32)
    for index, target in enumerate(targets):
        target[...] = total[:, index * padded : (index + 1) * padded].T[: target.shape[0]]


def receive_mlp(odd, kept, turned, core, units):
    rows, columns = kept.shape
    whole = pl.BlockSpec((rows, columns), lambda i, *_: (0, 0))
    found = pl.pallas_call(
        partial(receive_mlp_kernel, columns // 3),
        out_shape=[jax.ShapeDtypeStruct((units, rows), F32)] * 3,
        grid_spec=pltpu.PrefetchScalarGridSpec(
            num_scalar_prefetch=1,
            grid=(1,),
            in_specs=[whole] * 3,
            out_specs=[pl.BlockSpec((units, rows), lambda i, *_: (0, 0))] * 3,
        ),
        compiler_params=params(),
        cost_estimate=cost(0, rows * columns * 10),
    )(odd, kept, turned, core)
    return [f.T for f in found]


def per_device(
    dp_size,
    tensor_size,
    tokens,
    lengths,
    cotangent,
    gain_one,
    gain_two,
    w_query,
    w_key,
    w_value,
    w_gate,
    w_out,
    w_mgate,
    w_mup,
    w_down,
):
    rows, width = tokens.shape
    seq = rows * tensor_size
    heads = w_query.shape[1] // KEY
    units = w_mgate.shape[1]
    shard_rows = w_query.shape[0]
    half_rows = shard_rows // 2
    bits = dp_size.bit_length() - 1
    mine, place = lax.axis_index("dp"), lax.axis_index("tensor")
    inner = (place == 1) | (place == 2)
    odd = (mine & 1) == 1
    up_bits = list(range(1, bits))
    down_bits = up_bits[::-1]

    def add(*arrays):
        return sum(array.astype(F32) for array in arrays)

    def swap_dp(array, mask):
        return lax.ppermute(array, "dp", [(i, i ^ mask) for i in range(dp_size)])

    def move_tensor(array, pairs):
        return lax.ppermute(array, "tensor", pairs)

    def swap_tensor(array, mask):
        return move_tensor(array, [(i, i ^ mask) for i in range(tensor_size)])

    across = [(1, 2), (2, 1)]
    outward = [(1, 0), (2, 3)]
    inward = [(0, 1), (3, 2)]

    def pair(dp_index, tensor_index):
        return dp_index * tensor_size + tensor_index

    top = tensor_size - 1
    to_even = [(pair(m | 1, t), pair(m, t)) for m in range(0, dp_size, 2) for t in range(tensor_size)]
    stay = [(pair(m, t), pair(m, t)) for m in range(0, dp_size, 2) for t in range(tensor_size)]
    to_odd = [(pair(m, t), pair(m | 1, t ^ top)) for m in range(0, dp_size, 2) for t in range(tensor_size)]
    odd_turn = [(pair(m | 1, t), pair(m | 1, t ^ top)) for m in range(0, dp_size, 2) for t in range(tensor_size)]
    both = ("dp", "tensor")

    def hold(array):
        return after(array, token[0])

    def close(*results):
        token[0] = after(token[0], *results)

    def line_out(slots, beside, middle):
        return move_tensor(hold(beside), across), move_tensor(hold(middle), outward)

    def line_all(own, beside, middle, far_inner, far_ends, last):
        return own, beside, jnp.where(inner, far_inner, far_ends), jnp.where(inner, middle, last)

    def first_level(piece, order):
        return swap_dp(piece, 1 << order[0])

    def second_level(piece, order):
        return swap_dp(hold(piece), 1 << order[1])

    def further(pieces, order):
        for bit in order[2:]:
            pieces = pieces + [swap_dp(p, 1 << bit) for p in pieces]
        return pieces

    def to_core(piece):
        return swap_dp(hold(piece), 1)

    def sum_start(high, order):
        return swap_dp(hold(high), 1 << order[-1])

    def sum_split(low, come):
        middle = low.shape[0] // 2
        return [add(low[span], come[span]).astype(BF16) for span in (slice(0, middle), slice(middle, 2 * middle))]

    def sum_end(low, high, order):
        for bit in order[-2:0:-1]:
            low, high = sum_split(low, swap_dp(hold(high), 1 << bit))
        return low, swap_dp(hold(high), 1 << order[0])

    blocks = [
        (chip << 1 | core, part)
        for core in range(2)
        for part, order in ((0, up_bits), (1, down_bits))
        for chip in [sum((i >> j & 1) << (b - 1) for j, b in enumerate(order)) for i in range(dp_size // 2)]
    ]

    sizes = (shard_rows, half_rows)
    aligned = half_rows % LANES == 0
    mine_arg = mine.astype(jnp.int32).reshape(1)

    def to_relative(*arrays):
        if aligned:
            return reorder(own_order_kernel, blocks, sizes, mine_arg, arrays)
        return [
            jnp.concatenate(
                [
                    lax.dynamic_slice_in_dim(a, (mine ^ mask) * shard_rows + part * half_rows, half_rows, -1)
                    for mask, part in blocks
                ],
                -1,
            )
            for a in arrays
        ]

    def to_global(array):
        if aligned:
            return reorder(global_order_kernel, blocks, sizes, mine_arg, [array])[0]
        found = []
        for shard in range(dp_size):
            mask = mine ^ shard
            for part, order in ((0, up_bits), (1, down_bits)):
                chip = sum((mask >> b & 1) << j for j, b in enumerate(order))
                index = (mask & 1) * dp_size + part * (dp_size // 2) + chip
                found.append(lax.dynamic_slice_in_dim(array, index * half_rows, half_rows, -1))
        return jnp.concatenate(found, -1)

    first_row = place * rows
    valid = (first_row + jnp.arange(rows, dtype=jnp.int32) < lengths[0])[:, None]
    head_ids = (place * heads + jnp.arange(heads, dtype=jnp.int32)).astype(F32)
    log_decay = jnp.log(1.0 - jnp.exp2(-5.0 - head_ids))
    place_arg = place.astype(jnp.int32).reshape(1)
    freqs = np.float32(10000.0) ** (-np.arange(KEY // 2, dtype=np.float32) / np.float32(KEY // 2))
    angles = np.arange(seq, dtype=np.float32)[:, None] * freqs[None, :]
    cosines, sines = jnp.asarray(np.cos(angles)), jnp.asarray(np.sin(angles))

    token = [mine_arg]
    spans = slice(0, half_rows), slice(half_rows, shard_rows)
    proj_columns, out_columns = 2 * heads * (KEY + VPAD), heads * VPAD
    padded = -(-units // LANES) * LANES

    sent_up, sent_down = send_attn((w_query, w_key, w_value, w_gate, w_out), heads)
    features_low, gain_first = to_relative(tokens, gain_one[None])
    features = features_low.astype(F32)
    normed_one, inverse_one = norm_parts(features)
    first_own = (normed_one * gain_first).astype(BF16)
    close(sent_up, sent_down, first_own)

    up_one = first_level(hold(sent_up), up_bits)
    down_one = first_level(hold(sent_down), down_bits)
    first_beside = swap_tensor(hold(first_own), 1)
    first_middle = move_tensor(hold(first_own), across)
    local_two = send_mlp((w_mgate, w_mup, hold(w_down)), padded)
    cotangent_low, gain_second = to_relative(hold(cotangent), gain_two[None])
    grad_own = jnp.where(valid, cotangent_low, 0.0)
    grad_final = grad_own.astype(F32)
    core_one = [to_core(sent_up)]
    close(up_one, down_one, first_beside, first_middle, local_two, grad_own, core_one[0])

    up_two, down_two = second_level(sent_up, up_bits), second_level(sent_down, down_bits)
    first_far = line_out(None, first_beside, first_middle)
    core_one.append(to_core(sent_down))
    close(up_two, down_two, *first_far, *core_one)

    up_three, down_three = second_level(up_one, up_bits), second_level(down_one, down_bits)
    first_last = move_tensor(hold(first_far[0]), outward)
    core_two = [to_core(p) for p in (up_one, down_one)]
    close(up_three, down_three, first_last, *core_two)

    up_all = further([sent_up, up_one, up_two, up_three], up_bits)
    down_all = further([sent_down, down_one, down_two, down_three], down_bits)
    up_core = [core_one[0], core_two[0]] + [to_core(p) for p in up_all[2:]]
    down_core = [core_one[1], core_two[1]] + [to_core(p) for p in down_all[2:]]
    mlp_zero = [lax.ppermute(hold(local_two[span]), both, odd_turn + stay) for span in spans]
    grad_beside = swap_tensor(hold(grad_own), 1)
    close(*up_core, *down_core)
    attn_low = up_all + down_all + up_core + down_core
    first_slots = line_all(first_own, first_beside, first_middle, *first_far, first_last)

    orders = up_bits, down_bits

    def level_one(halves):
        return [first_level(half, order) for half, order in zip(halves, orders)]

    def level_two(halves, come):
        found = []
        for half, other, order in zip(halves, come, orders):
            both_pieces = jnp.concatenate([half, hold(other)], 0)
            found += further_two([both_pieces, swap_dp(both_pieces, 1 << order[1])], order)
        return found

    def further_two(pieces, order):
        for bit in order[2:]:
            pieces = pieces + [swap_dp(p, 1 << bit) for p in pieces]
        return pieces

    grad_core = to_core(grad_own)
    projected = rows_times([hold(first_slots[0]), *first_slots[1:]], attn_low, 0, proj_columns)
    close(*mlp_zero, projected[0], grad_core)

    zero_come = level_one([hold(half) for half in mlp_zero])
    mlp_one = [lax.ppermute(hold(local_two)[spans[0]], both, to_even + to_odd)]
    query, key, value, normed_head, scale_head, mixed = retain(
        [hold(projected[0]), *projected[1:]], place_arg, log_decay, cosines, sines, heads
    )
    (mixed_third,) = rows_back(mixed, (3,), attn_low, proj_columns)
    close(*zero_come, mlp_one[0], grad_beside, mixed_third)

    from_ends = move_tensor(hold(mixed_third), inward)
    mlp_one.append(lax.ppermute(hold(local_two)[spans[1]], both, to_even + to_odd))
    zero_pieces = level_two(mlp_zero, zero_come)
    mixed_second, mixed_first, mixed_own = rows_back(hold(mixed), (2, 1, 0), attn_low, proj_columns)
    mixed_partial = add(mixed_second, from_ends).astype(BF16)
    grad_rows = [grad_own, grad_beside, grad_core, to_core(grad_beside)]
    close(mlp_one[1], *zero_pieces, mixed_partial, grad_rows[3])

    from_inner = move_tensor(hold(mixed_partial), across)
    from_ends = move_tensor(hold(mixed_second), inward)
    one_come = level_one([hold(half) for half in mlp_one])
    close(*one_come, from_inner, from_ends)

    from_beside = swap_tensor(add(mixed_first, hold(from_inner)).astype(BF16), 1)
    from_middle = move_tensor(add(mixed_third, hold(from_ends)).astype(BF16), across)
    mlp_pieces = zero_pieces + level_two(mlp_one, one_come)
    middle = features + add(mixed_own, from_beside, from_middle)
    normed_two, inverse_two = norm_parts(middle)
    second_own = (normed_two * gain_second).astype(BF16)
    close(*mlp_pieces, second_own)

    second_beside = swap_tensor(hold(second_own), 1)
    second_core = to_core(second_own)
    first_part = mlp(hold(second_own), second_core, grad_rows[0], grad_rows[2], mlp_pieces)
    near_core = swap_dp(first_part[7], 1)
    close(second_beside, near_core)

    second_far = to_core(second_beside)
    second_rows = [second_own, second_beside, second_core, second_far]
    second_part = mlp(hold(second_beside), second_far, grad_rows[1], grad_rows[3], None, first_part[8:])
    far_core = swap_dp(second_part[7], 1)
    hidden, grad_gate, grad_up = (
        [first_part[2 * i], second_part[2 * i], first_part[2 * i + 1], second_part[2 * i + 1]] for i in range(3)
    )

    far = add(second_part[6], far_core).astype(BF16)
    near = add(first_part[6], near_core)
    close(far, near)

    def mlp_grad(end, core):
        return mlp_grads(end, core, [hold(second_rows[0]), *second_rows[1:]], grad_rows, grad_gate, grad_up, hidden)

    second_back = swap_tensor(hold(far), 1)
    high = [mlp_grad(1, 0), mlp_grad(1, 1)]
    down_own, down_other = mlp_down([hold(hidden[0]), *hidden[1:]], first_part[10])
    close(second_back, *high[0], *high[1], down_own)

    attn_own, grad_middle, grad_gain_two = middle_back(near, hold(second_back), middle, grad_own, gain_second)
    attn_beside = swap_tensor(attn_own, 1)
    attn_second = swap_tensor(attn_own, 2)
    come = [[sum_start(high[0][0], up_bits), sum_start(high[0][1], down_bits)]]
    come.append(
        [sum_start(after(high[1][0], come[0][0]), up_bits), sum_start(after(high[1][1], come[0][1]), down_bits)]
    )
    low = [mlp_grad(0, 0), mlp_grad(0, 1)]
    down_core = to_core(down_other)
    splits = [[sum_split(low[0][part], come[0][part]) for part in range(2)]]
    close(attn_beside, attn_second, *come[1], *low[1], down_core, *splits[0][0], *splits[0][1])

    attn_middle = move_tensor(hold(attn_own), across)
    attn_last = move_tensor(hold(attn_second), outward)
    splits.append([sum_split(low[1][part], hold(come[1][part])) for part in range(2)])

    def mlp_end(core):
        return [sum_end(*splits[core][part], orders[part]) for part in range(2)]

    def mlp_sum(ends):
        return [add(*end).astype(BF16) for end in ends]

    mlp_total = [mlp_sum(mlp_end(0))]
    grad_mixed = rows_times([hold(attn_own), attn_beside, attn_second], attn_low, proj_columns, out_columns)
    down_sum = add(down_own, hold(down_core))
    down_sent = down_sum[rows:].astype(BF16)
    close(attn_middle, attn_last, *mlp_total[0], grad_mixed[0])
    attn_slots = attn_own, attn_beside, attn_second, jnp.where(inner, attn_middle, hold(attn_last))

    grad_mixed = grad_mixed + rows_times([attn_slots[3]], attn_low, proj_columns, out_columns)
    grad_turn = [
        lax.ppermute(after(t, grad_mixed[3]), both, [(b, a) for a, b in odd_turn]) for t in mlp_total[0]
    ]
    grad_proj = retain_back(
        grad_mixed, projected, normed_head, scale_head, query, key, value, place_arg, log_decay, cosines, sines, heads
    )
    back_third, gain_third = rows_back(grad_proj, (3,), attn_low, 0, first_slots[3:])
    mlp_ends = mlp_end(1)
    close(*grad_turn, back_third, mlp_ends[0][1], mlp_ends[1][1])

    from_ends = move_tensor(hold(back_third), inward)
    to_owner = [(b, a) for a, b in to_even + to_odd]
    mlp_total.append(mlp_sum([(low_part, hold(come_part)) for low_part, come_part in mlp_ends]))
    grad_core = [lax.ppermute(mlp_total[1][0], both, to_owner)]
    other_high = attn_grads(1, first_slots, hold(grad_proj))
    back_second, gain_second_part = rows_back(after(grad_proj, other_high), (2,), attn_low, 0, first_slots[2:3])
    other_low = attn_grads(0, first_slots, after(grad_proj, back_second))
    back_partial = add(back_second, from_ends).astype(BF16)
    close(back_partial, other_low, grad_core[0])

    from_inner = move_tensor(hold(back_partial), across)
    from_ends = move_tensor(hold(back_second), inward)
    core_high, core_low = to_core(other_high), to_core(other_low)
    out_other_high = attn_grads(1, attn_slots, hold(mixed))
    out_other_low = attn_grads(0, attn_slots, after(mixed, out_other_high))
    back_own, back_first, gain_near = rows_back(after(grad_proj, out_other_low), (0, 1), attn_low, 0, first_slots[:2])
    up_high, down_high = attn_grads(1, first_slots, after(grad_proj, back_own), core_high)
    proj_come = swap_dp(up_high, 1 << up_bits[-1]), swap_dp(down_high, 1 << down_bits[-1])
    close(from_inner, from_ends, back_own, core_low, out_other_low, up_high)

    from_beside = swap_tensor(add(back_first, hold(from_inner)).astype(BF16), 1)
    from_middle = move_tensor(add(back_third, hold(from_ends)).astype(BF16), across)
    out_core_high, out_core_low = to_core(out_other_high), to_core(out_other_low)
    up_low, down_low = attn_grads(0, first_slots, hold(grad_proj), core_low)
    out_up_high, out_down_high = attn_grads(1, attn_slots, after(mixed, up_low), out_core_high)
    out_up_low, out_down_low = attn_grads(0, attn_slots, after(mixed, out_up_high), out_core_low)
    gain_parts = gain_third[0] + gain_second_part[0] + hold(gain_near)[0]
    gains = to_global(jnp.stack([gain_parts / gain_first[0], grad_gain_two[0]]))
    gains = gains + swap_dp(gains, 1)
    close(from_beside, from_middle, *proj_come, gains, up_low, out_up_low)

    down_beside = swap_tensor(hold(down_sent), 1)
    proj_up = sum_end(*sum_split(up_low, hold(proj_come[0])), up_bits)
    proj_down = sum_end(*sum_split(down_low, hold(proj_come[1])), down_bits)
    out_come = sum_start(out_up_high, up_bits), sum_start(out_down_high, down_bits)
    grad_core.append(lax.ppermute(after(mlp_total[1][1], out_come[0]), both, to_owner))
    grad_first = add(back_own, hold(from_beside), from_middle)
    grad_tokens = grad_middle + norm_back(normed_one, inverse_one, grad_first, gain_first)
    grad_tokens = to_global(grad_tokens.astype(BF16))
    close(*proj_up, *proj_down, *out_come, grad_core[1], down_beside, grad_tokens)

    final = middle + down_sum[:rows] + hold(down_beside).astype(F32)
    output = to_global(jnp.where(valid, final, 0.0).astype(BF16))
    sum_mgate, sum_mup, sum_down = receive_mlp(
        (mine & 1).astype(jnp.int32).reshape(1),
        jnp.concatenate([hold(t) for t in mlp_total[0]], 0),
        jnp.concatenate(grad_turn, 0),
        jnp.concatenate(grad_core, 0),
        units,
    )
    out_up = sum_end(*sum_split(out_up_low, hold(out_come[0])), up_bits)
    out_down = sum_end(*sum_split(out_down_low, hold(out_come[1])), down_bits)
    gains = hold(gains)
    for other in (1, 2):
        gains = gains + swap_tensor(gains, other)
    for bit in range(1, bits):
        gains = gains + swap_dp(gains, 1 << bit)
    sum_query, sum_key, sum_value, sum_gate = receive_attn(
        (hold(proj_up[0]), proj_up[1], *proj_down), 2, 2, heads
    )
    (sum_out,) = receive_attn((*out_up, *out_down), 0, 1, heads)
    return (
        output,
        grad_tokens,
        gains[0],
        gains[1],
        sum_query,
        sum_key,
        sum_value,
        sum_gate,
        sum_out,
        sum_mgate,
        sum_mup,
        sum_down,
    )


def solution(mesh):
    rows = P(("dp", "tensor"), None)
    block = P("dp", "tensor")
    return jax.shard_map(
        partial(per_device, mesh.shape["dp"], mesh.shape["tensor"]),
        mesh=mesh,
        in_specs=(rows, P("dp"), rows, P(), P()) + (block,) * 8,
        out_specs=(rows, rows, P(), P()) + (block,) * 8,
        check_vma=False,
    )
```
